32 devices in a mesh: ctx: 2 (over core), exp: 16 (over z, y, x).
Axes of the slice: x: 2, y: 2, z: 4, core: 2. Of those that a mesh axis runs over, the one named last changes fastest.
Arguments:
- inputs: bfloat16 [2, 16, 1024, 768], P(None, 'exp', 'ctx'), may hold values from -6 to 6
- cotangent: bfloat16 [2, 16, 1024, 768], P(None, 'exp', 'ctx'), may hold values from -6 to 6
- doc_ids: int32 [2, 16, 1024], P(None, 'exp'), may hold values from 0 to 3, never falling along the last dimension, each value on 1 to 512 neighbouring positions
- routes: int32 [2, 16, 1024, 2], P(None, 'exp', 'ctx'), may hold values from 0 to 15, all different within a row; in each aligned block of 512 rows (0 to 511, 512 to 1023, ..., all dimensions but the last counted through in order) at most 91 rows name the same one
- query_key_value_weight: bfloat16 [768, 2304], P(('ctx', 'exp')), may hold values from -0.21875 to 0.21875
- output_projection_weight: bfloat16 [768, 768], P(('ctx', 'exp')), may hold values from -0.875 to 0.875
- router: bfloat16 [768, 16], P(('ctx', 'exp')), may hold values from -0.15625 to 0.15625
- attn_gain: bfloat16 [768], P(('ctx', 'exp')), may hold values from 0.5 to 1.5
- expert_gain: bfloat16 [768], P(('ctx', 'exp')), may hold values from 0.5 to 1.5
- position_bias: bfloat16 [12, 32], replicated, may hold values from -3 to 3
- expert_up: bfloat16 [16, 768, 3072], P('exp', 'ctx'), may hold values from -0.21875 to 0.21875
- expert_down: bfloat16 [16, 3072, 768], P('exp', 'ctx'), may hold values from -0.109375 to 0.109375
Outputs:
- activations: bfloat16 [2, 16, 1024, 768], P(None, 'exp', 'ctx')
- input_grad: bfloat16 [2, 16, 1024, 768], P(None, 'exp', 'ctx')
- qkv_weight_grad: float32 [768, 2304], P(('ctx', 'exp'))
- proj_weight_grad: float32 [768, 768], P(('ctx', 'exp'))
- router_grad: float32 [768, 16], P(('ctx', 'exp'))
- attn_gain_grad: float32 [768], P(('ctx', 'exp'))
- expert_gain_grad: float32 [768], P(('ctx', 'exp'))
- pos_bias_grad: float32 [12, 32], replicated
- expert_up_grad: float32 [16, 768, 3072], P('exp', 'ctx')
- expert_down_grad: float32 [16, 3072, 768], P('exp', 'ctx')
The draws below stay inside these ranges and needn't reach their ends.
Inputs may be any that keep to these rules, and one draw needn't show every extreme that they name: `routes`: each token names 2 different experts. In every aligned block of 512 positions of one sequence in one micro-batch no expert is named more than 91 times, a bound that some block reaches. `doc_ids`: document numbers of a sequence never fall; a document has at most half of 1024 tokens.
All inputs are finite; a program needn't handle non-finite values.
Results may differ from the reference program's by a relative error of at most 0.013.
Values may be sent and summed in bfloat16 or wider, within the bound.
No kernel may reach another device: no remote copies, remote signals or barrier semaphores. Data moves between devices by JAX's collectives and lax.ppermute only.
A program may use at most 320 MiB of HBM per device.

```python
import math
import jax
import jax.numpy as jnp
import numpy as np
from jax import lax

D = 768
HEADS = 12
HEAD = 64
FF = 3072
BUCKETS = 32
TOP = 2
MICRO = 2
DOCS = 4
SEQ_LEN = 1024
BLK = 512
SEQS = 16
EXPERTS = 16
CAP = 91
N_CTX = 2


def block_scale(rng, dims, cuts, low, largest):
    loudness, own = 1.0, jax.random.fold_in(rng, 6)
    for dim, parts in cuts:
        draws = jnp.exp(jax.random.uniform(jax.random.fold_in(own, dim), (parts,), jnp.float32, low / len(cuts), largest / len(cuts)))
        loudness = loudness * jnp.repeat(draws, dims[dim] // parts).reshape([-1 if axis == dim else 1 for axis in range(len(dims))])
    return loudness


def split_up(amount, total, most, lean):
    weights = [(1 << 20) // math.isqrt(grade ** lean) + 1 for grade in range(2, amount + 1)]
    rest, holding = total - most - (amount - 1), [1] * (amount - 1)
    while rest > 0:
        candidates = [i for i in range(amount - 1) if holding[i] < most]
        mass, left = sum([weights[i] for i in candidates]), rest
        for i in candidates:
            extra = min(most - holding[i], max(1, left * weights[i] // mass), rest)
            holding[i] = holding[i] + extra
            rest = rest - extra
    return np.array([most] + holding)


def ragged_sizes(stream_key, number_of, total, bound, slope):
    if number_of == 2:
        one = jax.random.randint(stream_key, (), max(1, total - bound), min(bound, total - 1) + 1)
        return jnp.stack([one, total - one])
    lengths = jnp.asarray(split_up(number_of, total, bound, slope), jnp.int32)
    twos = (number_of - 1) // 2
    source_of, taker = lengths[1:1 + 2 * twos:2], lengths[2:2 + 2 * twos:2]
    slack = jnp.minimum(source_of - 1, bound - taker)
    moved = jax.random.randint(jax.random.fold_in(stream_key, 1), (twos,), 0, 1 << 20) % (slack + 1)
    lengths = lengths.at[1:1 + 2 * twos:2].set(source_of - moved).at[2:2 + 2 * twos:2].set(taker + moved)
    return lengths[jax.random.permutation(jax.random.fold_in(stream_key, 2), number_of)]


def deal_out(key, own, number, rows, number_of, top, most, slope):
    ranking = jax.random.permutation(key, number_of)
    packed, usual = shares(number_of, rows * top, most, slope, True), shares(number_of, rows * top, most, slope, False)
    places = jnp.arange(number_of)

    def named(tallies, rotation):
        used = int((tallies > 0).sum())
        fixed = max(1, used // 4)
        passed = fixed + (places - fixed + rotation * (used - fixed)) % max(1, number_of - fixed)
        return jnp.zeros((number_of,), jnp.int32).at[ranking[jnp.where(places < fixed, places, passed)]].set(jnp.asarray(tallies, jnp.int32))

    tallies = jnp.where(number % 4 == 0, named(packed, number // 4), named(usual, number - number // 4 - 1))
    mixed = jax.random.permutation(jax.random.fold_in(own, 3), number_of)
    source_of, taker = mixed[0:number_of // 2 * 2:2], mixed[1:number_of // 2 * 2:2]
    room = jnp.minimum(tallies[source_of] - 1, most - tallies[taker]) // 2
    room = jnp.where((source_of == ranking[0]) | (taker == ranking[0]) | (tallies[taker] == 0), 0, jnp.maximum(room, 0))
    passed = jax.random.randint(jax.random.fold_in(own, 4), (number_of // 2,), 0, 1 << 20) % (room + 1)
    tallies = tallies.at[source_of].add(-passed).at[taker].add(passed)
    items = jnp.searchsorted(jnp.cumsum(tallies), jnp.arange(rows * top), side="right").astype(jnp.int32)
    table = items.reshape(top, rows).T
    table = table[jax.random.permutation(jax.random.fold_in(own, 1), rows)]
    rotation = jax.random.randint(jax.random.fold_in(own, 2), (rows, 1), 0, top)
    return jnp.take_along_axis(table, (jnp.arange(top)[None, :] + rotation) % top, axis=1)


def shares(amount, total, bound, skew, full):
    weights = [(1 << 20) // math.isqrt(grade ** skew) + 1 for grade in range(1, amount + 1)]
    largest = bound if full else min(bound, max(-(-total // amount), total * weights[0] // sum(weights)))
    least = 1 if total - largest >= amount - 1 else 0
    given, surplus = [largest] + [least] * (amount - 1), total - largest - least * (amount - 1)
    while surplus > 0:
        candidates = [i for i in range(1, amount) if given[i] < largest] or [i for i in range(1, amount) if given[i] < bound]
        whole, remaining = sum([weights[i] for i in candidates]), surplus
        for i in candidates:
            addition = min(bound - given[i], max(1, remaining * weights[i] // whole), surplus)
            given[i] = given[i] + addition
            surplus = surplus - addition
    return np.array(given)


def normal_values(rng, dims, scale, reach, split=(), held_as=jnp.bfloat16):
    entries = jax.random.normal(rng, dims, jnp.float32) * scale
    if len(split) > 0:
        entries = block_scale(rng, dims, split, -0.22, 0.18) * entries
    return jnp.clip(entries, min=-reach, max=reach).astype(held_as)


def setup_inputs(seed: int = 0) -> dict:
    splits = jax.random.split(jax.random.key(seed), 13)
    inputs = normal_values(splits[0], (MICRO, SEQS, SEQ_LEN, D), 1.0, 6.0, ((1, 16), (2, 2)))
    cotangent = normal_values(splits[1], (MICRO, SEQS, SEQ_LEN, D), 1.0, 6.0, ((1, 16), (2, 2)))
    doc_ids = jax.vmap(lambda own: jnp.searchsorted(jnp.cumsum(ragged_sizes(own, DOCS, SEQ_LEN, SEQ_LEN // 2, 0)), jnp.arange(SEQ_LEN), side="right"))(jax.random.split(splits[2], MICRO * SEQS)).reshape((MICRO, SEQS, SEQ_LEN)).astype(jnp.int32)
    routes_keys = jax.random.split(jax.random.fold_in(splits[3], 1), MICRO * SEQS * SEQ_LEN // BLK)
    routes_turns = jax.random.permutation(jax.random.fold_in(splits[3], 3), MICRO * SEQS * SEQ_LEN // BLK)
    routes = jax.vmap(lambda own, number: deal_out(jax.random.fold_in(splits[3], 2), own, number, BLK, EXPERTS, TOP, CAP, 1))(routes_keys, routes_turns).reshape((MICRO, SEQS, SEQ_LEN, TOP))
    query_key_value_weight = normal_values(splits[4], (D, 3 * D), D ** -0.5, 0.21875, ((0, 32),))
    output_projection_weight = normal_values(splits[5], (D, D), (D // 16) ** -0.5, 0.875, ((0, 32),))
    router = normal_values(splits[6], (D, EXPERTS), (2 * D) ** -0.5, 0.15625, ((0, 32),))
    attn_gain = jnp.clip(1.0 + 0.1 * jax.random.normal(splits[7], (D,), jnp.float32), 0.5, 1.5).astype(jnp.bfloat16)
    expert_gain = jnp.clip(1.0 + 0.1 * jax.random.normal(splits[8], (D,), jnp.float32), 0.5, 1.5).astype(jnp.bfloat16)
    position_bias = normal_values(splits[9], (HEADS, BUCKETS), 0.5, 3.0)
    expert_up = normal_values(splits[10], (EXPERTS, D, FF), D ** -0.5, 0.21875, ((0, 16), (1, 2)))
    expert_down = normal_values(splits[11], (EXPERTS, FF, D), FF ** -0.5, 0.109375, ((0, 16), (1, 2)))
    return dict(inputs=inputs, cotangent=cotangent, doc_ids=doc_ids, routes=routes, query_key_value_weight=query_key_value_weight, output_projection_weight=output_projection_weight, router=router, attn_gain=attn_gain, expert_gain=expert_gain, position_bias=position_bias, expert_up=expert_up, expert_down=expert_down)


epsilon = 1e-06
highest_precision = lax.Precision.HIGHEST
thresholds = (19, 21, 24, 27, 31, 35, 40, 46, 52, 59, 67, 77, 87, 99, 113)

@jax.custom_vjp
def reduced_precision(v):
    return lax.optimization_barrier(v.astype(jnp.bfloat16)).astype(jnp.float32)

@jax.custom_vjp
def reduced_backward(v):
    return v

def low_keep(v):
    return (reduced_precision(v), None)

def low_pass(kept, grad):
    return (grad,)

def back_keep(v):
    return (v, None)

def back_low(kept, grad):
    return (reduced_precision(grad),)
reduced_precision.defvjp(low_keep, low_pass)
reduced_backward.defvjp(back_keep, back_low)

def bucket_of(distance):
    distance = jnp.maximum(distance, 0)
    beyond = jnp.zeros_like(distance)
    for threshold in thresholds:
        beyond = beyond + (distance >= threshold).astype(jnp.int32)
    return jnp.where(distance < 16, distance, 16 + beyond)

def rms_norm(values, gain_vec):
    return values * lax.rsqrt(lax.optimization_barrier(jnp.mean(values * values, axis=-1, keepdims=True)) + epsilon) * gain_vec

def softmax_last(scores):
    shifted = jnp.exp(scores - lax.optimization_barrier(jnp.max(scores, axis=-1, keepdims=True)))
    return shifted / lax.optimization_barrier(jnp.sum(shifted, axis=-1, keepdims=True))

def attend_sequence(query_key_value, seq_docs, bias_table):
    queries = query_key_value[:, :D].reshape(SEQ_LEN, HEADS, HEAD)
    key_heads = query_key_value[:, D:2 * D].reshape(SEQ_LEN, HEADS, HEAD)
    value_heads = query_key_value[:, 2 * D:].reshape(SEQ_LEN, HEADS, HEAD)
    raw_scores = jnp.einsum('qhd,khd->hqk', queries, key_heads, precision=highest_precision) * 0.125
    position = jnp.arange(SEQ_LEN, dtype=jnp.int32)
    distance = position[:, None] - position[None, :]
    raw_scores = raw_scores + bias_table[:, bucket_of(distance)]
    scores = reduced_backward(raw_scores)
    allowed = (distance >= 0) & (seq_docs[:, None] == seq_docs[None, :])
    probability = reduced_precision(softmax_last(jnp.where(allowed[None], scores, -1000000000.0)))
    return jnp.einsum('hqk,khd->qhd', probability, value_heads, precision=highest_precision).reshape(SEQ_LEN, D)

def mix_block(token_rows, batch_docs, batch_routes, query_key_value_weight, output_projection_weight, router, attn_gain, expert_gain, position_bias, expert_up, expert_down):
    normalized_input = reduced_precision(rms_norm(token_rows, attn_gain))
    query_key_value = reduced_precision(reduced_backward(jnp.einsum('nwq,qo->nwo', normalized_input, query_key_value_weight, precision=highest_precision)))

    def one_sequence(element):
        return attend_sequence(element[0], element[1], position_bias)
    attention_result = lax.map(jax.checkpoint(one_sequence), (query_key_value, batch_docs))
    attention_result = reduced_precision(reduced_backward(attention_result))
    hidden_state = token_rows + reduced_backward(jnp.einsum('zja,au->zju', attention_result, output_projection_weight, precision=highest_precision))
    shared = reduced_precision(rms_norm(hidden_state, expert_gain)).reshape(SEQS * SEQ_LEN, D)
    pieces = SEQS * N_CTX
    route_rows = batch_routes.reshape(pieces, BLK * TOP)
    counts = (route_rows[:, :, None] == jnp.arange(EXPERTS, dtype=jnp.int32)).astype(jnp.int32)
    slot_rank = lax.optimization_barrier(jnp.sum((jnp.cumsum(counts, axis=1) - 1) * counts, axis=2))
    slot_index = ((route_rows * pieces + jnp.arange(pieces, dtype=jnp.int32)[:, None]) * CAP + slot_rank).reshape(-1)
    token_index = jnp.repeat(jnp.arange(SEQS * SEQ_LEN, dtype=jnp.int32), TOP)
    filled = jnp.zeros((EXPERTS * pieces * CAP, D), jnp.float32).at[slot_index].set(reduced_backward(shared[token_index]))

    def expert_apply(element):
        arrived_rows, expert_in, expert_out = element
        pre_act = reduced_backward(jnp.dot(arrived_rows, expert_in, precision=highest_precision))
        activated = reduced_precision(jax.nn.gelu(pre_act))
        return reduced_precision(reduced_backward(jnp.dot(activated, expert_out, precision=highest_precision)))
    returned = lax.map(jax.checkpoint(expert_apply), (filled.reshape(EXPERTS, pieces * CAP, D), expert_up, expert_down)).reshape(-1, D)
    logits = reduced_backward(jnp.dot(shared, router, precision=highest_precision))
    chosen = jnp.take_along_axis(logits, batch_routes.reshape(-1, TOP), axis=1)
    gate_values = softmax_last(chosen)
    mixture = lax.optimization_barrier(jnp.sum(gate_values[:, :, None] * returned[slot_index].reshape(-1, TOP, D), axis=1))
    return hidden_state + mixture.reshape(SEQS, SEQ_LEN, D)

def reference(inputs, cotangent, doc_ids, routes, query_key_value_weight, output_projection_weight, router, attn_gain, expert_gain, position_bias, expert_up, expert_down):
    params = (query_key_value_weight.astype(jnp.float32), output_projection_weight.astype(jnp.float32), router.astype(jnp.float32), attn_gain.astype(jnp.float32), expert_gain.astype(jnp.float32), position_bias.astype(jnp.float32), expert_up.astype(jnp.float32), expert_down.astype(jnp.float32))

    def forward(token_rows, weights):

        def one_batch(element):
            return mix_block(element[0], element[1], element[2], weights[0], weights[1], weights[2], weights[3], weights[4], weights[5], weights[6], weights[7])
        return lax.map(jax.checkpoint(one_batch), (token_rows, doc_ids, routes))
    result, pullback = jax.vjp(forward, inputs.astype(jnp.float32), params)
    token_grad, weight_grads = pullback(cotangent.astype(jnp.float32))
    grad_qkv, grad_proj, grad_router, grad_attn, grad_expert, grad_bias, grad_up, grad_down = weight_grads
    return (result.astype(jnp.bfloat16), token_grad.astype(jnp.bfloat16), grad_qkv, grad_proj, grad_router, grad_attn, grad_expert, grad_bias, grad_up, grad_down)
```

```python
import functools

import jax
import jax.numpy as jnp
from jax import lax
from jax.experimental import pallas as pl
from jax.experimental.pallas import tpu as pltpu
from jax.sharding import PartitionSpec as P

HEADS = 12
HEAD = 64
PAIRS = HEADS // 2
TILE = 128
BACK = 512
SPAN = BACK // TILE + 1
MASKED = -1000000000.0

epsilon = 1e-06
thresholds = (19, 21, 24, 27, 31, 35, 40, 46, 52, 59, 67, 77, 87, 99, 113)
bf16 = jnp.bfloat16
f32 = jnp.float32


def bucket_of(distance):
    distance = jnp.maximum(distance, 0)
    beyond = jnp.zeros_like(distance)
    for threshold in thresholds:
        beyond = beyond + (distance >= threshold).astype(jnp.int32)
    return jnp.where(distance < 16, distance, 16 + beyond)


def mm(a, b, dims):
    return lax.dot_general(a, b, (dims, ((), ())), preferred_element_type=f32)


def stack_heads(rows):
    lane = lax.broadcasted_iota(jnp.int32, rows.shape, 1)
    zero = jnp.zeros_like(rows)
    return jnp.concatenate(
        [jnp.where(lane < HEAD, rows, zero), jnp.where(lane >= HEAD, rows, zero)], axis=0
    )


def fold_heads(wide):
    return jnp.concatenate([wide[:HEAD, :TILE], wide[HEAD:, TILE:]], axis=0)


def fill_mask(mask, qd_ref, kd_ref):
    for qi in range(qd_ref.shape[1] // TILE):
        docs_row = qd_ref[:, qi * TILE : (qi + 1) * TILE]
        for j in range(SPAN):
            kt = (qi + j) * TILE
            column = jnp.broadcast_to(kd_ref[:, kt : kt + TILE], (TILE, TILE)).T
            mask[qi, j * TILE : (j + 1) * TILE, :] = jnp.where(
                column == docs_row, 0.0, MASKED
            ).astype(f32)


def fill_bias(bias, bv_ref):
    for head in range(2):
        for d in range(2):
            row = jnp.broadcast_to(bv_ref[0, 2 * head + d : 2 * head + d + 1, :], (TILE, 2 * TILE))
            rolled = pltpu.roll(row, 0, 1, stride=1, stride_axis=0)
            bias[d, :, head * TILE : (head + 1) * TILE] = rolled[:, :TILE]


def masked_scores(scores, mask, bias, qi, tiles):
    parts = []
    for j in range(tiles):
        d = tiles - 1 - j
        off = (SPAN - tiles + j) * TILE
        m = mask[qi, off : off + TILE, :]
        x = scores[j * TILE : (j + 1) * TILE] + jnp.concatenate([m, m], axis=1)
        if d < 2:
            x = x + bias[d]
        parts.append(x)
    return parts


def fwd_kernel(tiles, q_ref, k_ref, v_ref, kp_ref, vp_ref, qd_ref, kd_ref, bv_ref, o_ref, lse_ref,
               kwin, vwin_t, bias, mask):
    @pl.when(pl.program_id(0) == 0)
    def _():
        fill_mask(mask, qd_ref, kd_ref)

    fill_bias(bias, bv_ref)
    kwin[:BACK] = kp_ref[...]
    kwin[BACK:] = k_ref[...]
    for t in range(BACK // TILE):
        vwin_t[:, t * TILE : (t + 1) * TILE] = vp_ref[t * TILE : (t + 1) * TILE, :].T
    for t in range(q_ref.shape[0] // TILE):
        at = BACK + t * TILE
        vwin_t[:, at : at + TILE] = v_ref[t * TILE : (t + 1) * TILE, :].T

    def step(qi, carry):
        q0 = pl.multiple_of(qi * TILE, TILE)
        q2 = stack_heads(q_ref[pl.ds(q0, TILE), :] * 0.125)

        def branch(count):
            def go():
                lo = pl.multiple_of((qi + SPAN - count) * TILE, TILE)
                keys = kwin[pl.ds(lo, count * TILE), :]
                parts = masked_scores(mm(keys, q2, ((1,), (1,))), mask, bias, qi, count)
                top = functools.reduce(jnp.maximum, parts)
                top = jnp.max(top, axis=0, keepdims=True)
                probs = [jnp.exp(x - top) for x in parts]
                total = jnp.sum(functools.reduce(jnp.add, probs), axis=0, keepdims=True)
                low = jnp.concatenate([p.astype(bf16) for p in probs], axis=0)
                out = fold_heads(mm(vwin_t[:, pl.ds(lo, count * TILE)], low, ((1,), (0,))))
                inv = 1.0 / total
                row = lax.broadcasted_iota(jnp.int32, (TILE, TILE), 0)
                out = out * jnp.where(row < HEAD, inv[:, :TILE], inv[:, TILE:])
                o_ref[pl.ds(q0, TILE), :] = out.T.astype(bf16)
                lse_ref[0, pl.ds(qi, 1), :] = top + jnp.log(total)
                return 0

            return go

        lax.switch(tiles[qi] - 1, [branch(c) for c in range(1, SPAN + 1)])
        return carry

    lax.fori_loop(0, q_ref.shape[0] // TILE, step, 0)


def bwd_kernel(tiles, q_ref, k_ref, v_ref, kp_ref, vp_ref, qd_ref, kd_ref, bv_ref, o_ref, do_ref,
               lse_ref, dq_ref, dk_ref, dv_ref, dkp_ref, dvp_ref, near_ref,
               kwin, kwin_t, vwin, dk, dv, near, bias, mask):
    @pl.when(pl.program_id(0) == 0)
    def _():
        fill_mask(mask, qd_ref, kd_ref)

    fill_bias(bias, bv_ref)
    kwin[:BACK] = kp_ref[...]
    kwin[BACK:] = k_ref[...]
    vwin[:BACK] = vp_ref[...]
    vwin[BACK:] = v_ref[...]
    for t in range(kwin.shape[0] // TILE):
        kwin_t[:, t * TILE : (t + 1) * TILE] = kwin[t * TILE : (t + 1) * TILE, :].T
    dk[...] = jnp.zeros_like(dk)
    dv[...] = jnp.zeros_like(dv)
    near[...] = jnp.zeros_like(near)

    def step(qi, carry):
        q0 = pl.multiple_of(qi * TILE, TILE)
        q2 = stack_heads(q_ref[pl.ds(q0, TILE), :] * 0.125)
        do = do_ref[pl.ds(q0, TILE), :]
        do2 = stack_heads(do)
        lse = lse_ref[0, pl.ds(qi, 1), :]
        prod = (do.astype(f32) * o_ref[pl.ds(q0, TILE), :].astype(f32)).T
        delta = jnp.concatenate(
            [jnp.sum(prod[:HEAD], axis=0, keepdims=True),
             jnp.sum(prod[HEAD:], axis=0, keepdims=True)],
            axis=1,
        )

        def branch(count):
            def go():
                lo = pl.multiple_of((qi + SPAN - count) * TILE, TILE)
                rows = pl.ds(lo, count * TILE)
                parts = masked_scores(
                    mm(kwin[rows, :], q2, ((1,), (1,))), mask, bias, qi, count
                )
                prob_grad = mm(vwin[rows, :], do2, ((1,), (1,)))
                lows = []
                grads = []
                for j in range(count):
                    prob = jnp.exp(parts[j] - lse)
                    grad = prob * (prob_grad[j * TILE : (j + 1) * TILE] - delta)
                    if j == count - 1:
                        near[...] += grad
                    elif j == count - 2:
                        r = lax.broadcasted_iota(jnp.int32, grad.shape, 0)
                        c = lax.broadcasted_iota(jnp.int32, grad.shape, 1)
                        c = jnp.where(c >= TILE, c - TILE, c)
                        near[...] += jnp.where(c < r, grad, 0.0)
                    lows.append(prob.astype(bf16))
                    grads.append(grad.astype(bf16))
                low = jnp.concatenate(lows, axis=0)
                score_grad = jnp.concatenate(grads, axis=0)
                dk[rows, :] += mm(score_grad, q2, ((1,), (0,)))
                dv[rows, :] += mm(low, do2, ((1,), (0,)))
                dq = fold_heads(mm(kwin_t[:, rows], score_grad, ((1,), (0,))))
                dq_ref[pl.ds(q0, TILE), :] = (dq.T * 0.125).astype(bf16)
                return 0

            return go

        lax.switch(tiles[qi] - 1, [branch(c) for c in range(1, SPAN + 1)])
        return carry

    lax.fori_loop(0, q_ref.shape[0] // TILE, step, 0)
    dkp_ref[...] = dk[:BACK].astype(bf16)
    dk_ref[...] = dk[BACK:].astype(bf16)
    dvp_ref[...] = dv[:BACK].astype(bf16)
    dv_ref[...] = dv[BACK:].astype(bf16)
    for head in range(2):
        at = slice(head * TILE, (head + 1) * TILE)
        turned = near[:, at]
        r = lax.broadcasted_iota(jnp.int32, turned.shape, 0)
        bit = 1
        while bit < TILE:
            turned = jnp.where((r & bit) > 0, pltpu.roll(turned, TILE - bit, 1), turned)
            bit *= 2
        near_ref[0, :, at] = jnp.sum(turned, axis=0, keepdims=True)


def attention_specs(length):
    full = lambda p, *_: (0, 0)
    lanes = lambda off: (lambda p, *_: (0, p + off))
    return [
        pl.BlockSpec((length, TILE), lanes(0)),
        pl.BlockSpec((length, TILE), lanes(PAIRS)),
        pl.BlockSpec((length, TILE), lanes(2 * PAIRS)),
        pl.BlockSpec((BACK, TILE), lanes(0)),
        pl.BlockSpec((BACK, TILE), lanes(PAIRS)),
        pl.BlockSpec((1, length), full),
        pl.BlockSpec((1, BACK + length), full),
        pl.BlockSpec((1, 4, 2 * TILE), lambda p, *_: (p, 0, 0)),
    ]


def attend(tiles, qkv, kv_back, query_docs, key_docs, bias_rows):
    length = qkv.shape[0]
    width = HEADS * HEAD
    blocks = length // TILE
    return pl.pallas_call(
        fwd_kernel,
        grid_spec=pltpu.PrefetchScalarGridSpec(
            num_scalar_prefetch=1,
            grid=(PAIRS,),
            in_specs=attention_specs(length),
            out_specs=[
                pl.BlockSpec((length, TILE), lambda p, *_: (0, p)),
                pl.BlockSpec((1, blocks, 2 * TILE), lambda p, *_: (p, 0, 0)),
            ],
            scratch_shapes=[
                pltpu.VMEM((BACK + length, TILE), bf16),
                pltpu.VMEM((TILE, BACK + length), bf16),
                pltpu.VMEM((2, TILE, 2 * TILE), f32),
                pltpu.VMEM((blocks, SPAN * TILE, TILE), f32),
            ],
        ),
        out_shape=[
            jax.ShapeDtypeStruct((length, width), bf16),
            jax.ShapeDtypeStruct((PAIRS, blocks, 2 * TILE), f32),
        ],
        compiler_params=pltpu.CompilerParams(vmem_limit_bytes=32 * 2**20),
        cost_estimate=pl.CostEstimate(
            flops=4 * 2 * HEADS * length * BACK * 128, bytes_accessed=6 * 2**20,
            transcendentals=HEADS * length * BACK,
        ),
        name="attend",
    )(tiles, qkv, qkv, qkv, kv_back, kv_back, query_docs, key_docs, bias_rows)


def attend_back(tiles, qkv, kv_back, query_docs, key_docs, bias_rows, out, out_grad, lse):
    length = qkv.shape[0]
    width = HEADS * HEAD
    blocks = length // TILE
    own = pl.BlockSpec((length, TILE), lambda p, *_: (0, p))
    back = pl.BlockSpec((BACK, TILE), lambda p, *_: (0, p))
    rows = jax.ShapeDtypeStruct((length, width), bf16)
    back_rows = jax.ShapeDtypeStruct((BACK, width), bf16)
    return pl.pallas_call(
        bwd_kernel,
        grid_spec=pltpu.PrefetchScalarGridSpec(
            num_scalar_prefetch=1,
            grid=(PAIRS,),
            in_specs=attention_specs(length)
            + [own, own, pl.BlockSpec((1, blocks, 2 * TILE), lambda p, *_: (p, 0, 0))],
            out_specs=[own, own, own, back, back,
                       pl.BlockSpec((1, 1, 2 * TILE), lambda p, *_: (p, 0, 0))],
            scratch_shapes=[
                pltpu.VMEM((BACK + length, TILE), bf16),
                pltpu.VMEM((TILE, BACK + length), bf16),
                pltpu.VMEM((BACK + length, TILE), bf16),
                pltpu.VMEM((BACK + length, TILE), f32),
                pltpu.VMEM((BACK + length, TILE), f32),
                pltpu.VMEM((TILE, 2 * TILE), f32),
                pltpu.VMEM((2, TILE, 2 * TILE), f32),
                pltpu.VMEM((blocks, SPAN * TILE, TILE), f32),
            ],
        ),
        out_shape=[rows, rows, rows, back_rows, back_rows,
                   jax.ShapeDtypeStruct((PAIRS, 1, 2 * TILE), f32)],
        compiler_params=pltpu.CompilerParams(vmem_limit_bytes=32 * 2**20),
        cost_estimate=pl.CostEstimate(
            flops=10 * 2 * HEADS * length * BACK * 128, bytes_accessed=12 * 2**20,
            transcendentals=HEADS * length * BACK,
        ),
        name="attend_back",
    )(tiles, qkv, qkv, qkv, kv_back, kv_back, query_docs, key_docs, bias_rows, out, out_grad, lse)


def is_power(n):
    return n & (n - 1) == 0


def rounds_of(size):
    bits = [1 << b for b in range(size.bit_length() - 1)]
    return bits[::-1]


def swap(x, axis, bit):
    size = lax.axis_size(axis)
    return lax.ppermute(x, axis, [(i, i ^ bit) for i in range(size)])


def gather_rows(x):
    if not (is_power(lax.axis_size("ctx")) and is_power(lax.axis_size("exp"))):
        return lax.all_gather(x, ("ctx", "exp"), axis=0, tiled=True)
    for axis in ("exp", "ctx"):
        me = lax.axis_index(axis)
        held = x[None]
        for bit in rounds_of(lax.axis_size(axis)):
            other = swap(held, axis, bit)
            high = (me & bit) > 0
            first, second = jnp.where(high, other, held), jnp.where(high, held, other)
            held = jnp.stack([first, second], axis=1).reshape((-1,) + x.shape)
        x = held.reshape((-1,) + x.shape[1:])
    return x


def pair_rows(x, axis):
    if lax.axis_size("ctx") != 2:
        return lax.all_gather(x, "ctx", axis=axis, tiled=True)
    other = swap(x, "ctx", 1)
    high = lax.axis_index("ctx") > 0
    return jnp.concatenate(
        [jnp.where(high, other, x), jnp.where(high, x, other)], axis=axis
    )


def send_half(x, axis):
    ways = lax.axis_size("ctx")
    if ways != 2:
        return lax.psum_scatter(x.astype(bf16), "ctx", scatter_dimension=axis, tiled=True).astype(f32)
    part = x.shape[axis] // 2
    me = lax.axis_index("ctx")
    mine = lax.dynamic_slice_in_dim(x, me * part, part, axis)
    theirs = lax.dynamic_slice_in_dim(x, (1 - me) * part, part, axis)
    return mine + swap(theirs.astype(bf16), "ctx", 1).astype(f32)


def scatter_sum(x):
    x = send_half(x, 0)
    ways = lax.axis_size("exp")
    parts = lax.all_to_all(x.astype(bf16), "exp", split_axis=0, concat_axis=0, tiled=True)
    return jnp.sum(parts.reshape(ways, -1, x.shape[1]).astype(f32), axis=0)


def shards(
    inputs,
    cotangent,
    doc_ids,
    routes,
    query_key_value_weight,
    output_projection_weight,
    router,
    attn_gain,
    expert_gain,
    position_bias,
    expert_up,
    expert_down,
):
    batches = inputs.shape[0]
    length = inputs.shape[2]
    width = inputs.shape[3]
    top = routes.shape[3]
    ways = lax.axis_size("ctx")
    experts = lax.axis_size("exp")
    capacity = max(2, top * length * 10 // (7 * experts))
    room = (capacity + 1 + 15) // 16 * 16
    slots = experts * room
    seq_len = doc_ids.shape[2]
    hidden_units = expert_up.shape[2]
    buckets = position_bias.shape[1]
    me = lax.axis_index("ctx")

    wide = 4 * width
    pad = -(experts + 2) % 128
    packed = jnp.concatenate(
        [
            query_key_value_weight,
            output_projection_weight,
            router,
            attn_gain[:, None],
            expert_gain[:, None],
            jnp.zeros((router.shape[0], pad), bf16),
        ],
        axis=1,
    )
    packed = gather_rows(packed)
    qkv_all = packed[:, : 3 * width]
    proj_all = packed[:, 3 * width : wide]
    router_all = packed[:, wide : wide + experts]
    gains = packed[:, wide + experts : wide + experts + 2].astype(f32)
    attn_scale = gains[:, 0]
    expert_scale = gains[:, 1]
    up_all = pair_rows(expert_up[0], 0)
    down_all = pair_rows(expert_down[0], 0)

    distance = jnp.arange(2 * TILE, dtype=jnp.int32)
    hot_bucket = (
        bucket_of(distance)[None, :] == jnp.arange(buckets, dtype=jnp.int32)[:, None]
    ).astype(f32)
    by_distance = jnp.sum(
        position_bias.astype(f32)[:, :, None] * hot_bucket[None], axis=1
    ) - position_bias.astype(f32)[:, buckets - 1 :]
    close = jnp.where(distance < TILE, by_distance, MASKED)
    beside = jnp.roll(by_distance, -TILE, axis=1)
    bias_rows = jnp.stack([close, beside], axis=1).reshape(PAIRS, 4, 2 * TILE)

    def norm_stats(values):
        return lax.rsqrt(jnp.mean(values * values, axis=-1, keepdims=True) + epsilon)

    earlier = jnp.tril(jnp.ones((length, length), bf16), -1)
    state = []
    for b in range(batches):
        rows = inputs[b, 0].astype(f32)
        inv_one = norm_stats(rows)
        normed = (rows * inv_one * attn_scale).astype(bf16)
        qkv = mm(normed, qkv_all, ((1,), (0,))).astype(bf16)
        own_kv = qkv[:, width:]
        docs = doc_ids[b, 0].astype(f32)
        padded = jnp.concatenate([jnp.full((BACK,), -1.0, f32), docs])
        key_docs = lax.dynamic_slice_in_dim(padded, me * length, BACK + length)
        query_docs = key_docs[BACK:]
        if ways == 2:
            kv_back = lax.ppermute(own_kv, "ctx", [(0, 1)])
        else:
            every = lax.all_gather(own_kv, "ctx", axis=0, tiled=True)
            every = jnp.concatenate([jnp.zeros((BACK, 2 * width), bf16), every], axis=0)
            kv_back = lax.dynamic_slice_in_dim(every, me * length, BACK, 0)
        firsts = query_docs[::TILE]
        start = jnp.sum((key_docs[None, :] < firsts[:, None]).astype(jnp.int32), axis=1)
        tiles = jnp.arange(length // TILE, dtype=jnp.int32) + SPAN - start // TILE
        tiles = jnp.clip(tiles, 1, SPAN)
        view = (tiles, qkv, kv_back, query_docs[None], key_docs[None], bias_rows)
        attended, lse = attend(*view)
        hidden = rows + mm(attended, proj_all, ((1,), (0,)))
        inv_two = norm_stats(hidden)
        shared = (hidden * inv_two * expert_scale).astype(bf16)
        logits = mm(shared, router_all, ((1,), (0,)))
        route_ids = routes[b, 0]
        hot = route_ids[:, :, None] == jnp.arange(experts, dtype=jnp.int32)[None, None, :]
        chosen = jnp.sum(jnp.where(hot, logits[:, None, :], 0.0), axis=2)
        gate_exp = jnp.exp(chosen - jnp.max(chosen, axis=1, keepdims=True))
        gates = gate_exp / jnp.sum(gate_exp, axis=1, keepdims=True)
        used = jnp.any(hot, axis=1)
        rank = mm(earlier, used.astype(bf16), ((1,), (0,))).astype(jnp.int32)
        slot = jnp.sum(jnp.where(hot, rank[:, None, :], 0), axis=2) + route_ids * room
        slot_rows = jnp.arange(slots, dtype=jnp.int32)
        holds = [slot[None, :, k] == slot_rows[:, None] for k in range(top)]
        spread = functools.reduce(jnp.logical_or, holds).astype(bf16)
        picks = [(slot[:, k : k + 1] == slot_rows[None, :]).astype(bf16) for k in range(top)]

        cot = cotangent[b, 0]
        cot_sent = mm(spread, cot, ((1,), (0,))).astype(bf16).reshape(experts, room, width)
        cot_here = lax.all_to_all(cot_sent, "exp", split_axis=0, concat_axis=0, tiled=True)

        gate_slots = sum(
            jnp.sum(jnp.where(holds[k], gates[None, :, k], 0.0), axis=1) for k in range(top)
        ).reshape(experts, 1, room)
        gate_high = gate_slots.astype(bf16)
        gate_low = (gate_slots - gate_high.astype(f32)).astype(bf16)
        gate_row = jnp.concatenate(
            [gate_high, gate_low, jnp.zeros((experts, 1, width - 2 * room), bf16)], axis=2
        )
        sent = mm(spread, shared, ((1,), (0,))).astype(bf16).reshape(experts, room, width)
        at_gate = lax.broadcasted_iota(jnp.int32, (1, room, 1), 1) == capacity
        sent = jnp.where(at_gate, gate_row, sent)
        here = lax.all_to_all(sent, "exp", split_axis=0, concat_axis=0, tiled=True)
        state.append(
            dict(rows=rows, inv_one=inv_one, normed=normed, view=view, attended=attended, lse=lse,
                 hidden=hidden, inv_two=inv_two, shared=shared, gates=gates, hot=hot,
                 spread=spread, picks=picks, cot=cot, cot_here=cot_here, here=here)
        )

    grad_up = jnp.zeros((width, hidden_units), f32)
    grad_down = jnp.zeros((hidden_units, width), f32)
    for s in state:
        packet = s["here"]
        gate_row = packet[:, capacity, : 2 * room].astype(f32)
        gate = (gate_row[:, :room] + gate_row[:, room:])[:, :, None]
        real = lax.broadcasted_iota(jnp.int32, (1, room, 1), 1) < capacity
        gate = jnp.where(real, gate, 0.0).reshape(slots, 1)
        x = packet.reshape(slots, width)
        up = s["cot_here"].reshape(slots, width).astype(f32)
        pre = mm(x, up_all, ((1,), (0,)))
        act = jax.nn.gelu(pre).astype(bf16)
        result = (mm(act, down_all, ((1,), (0,))) * gate).astype(bf16)
        s["back"] = lax.all_to_all(
            result.reshape(experts, room, width), "exp", split_axis=0, concat_axis=0, tiled=True
        )
        result_grad = (up * gate).astype(bf16)
        act_grad = mm(result_grad, down_all, ((1,), (1,)))
        pre_grad = jax.vjp(jax.nn.gelu, pre)[1](act_grad)[0].astype(bf16)
        route_grad = mm(pre_grad, up_all, ((1,), (1,))).astype(bf16)
        s["grad_back"] = lax.all_to_all(
            route_grad.reshape(experts, room, width), "exp", split_axis=0, concat_axis=0, tiled=True
        )
        grad_down = grad_down + mm(act, result_grad, ((0,), (0,)))
        grad_up = grad_up + mm(x, pre_grad, ((0,), (0,)))
    up_share = send_half(grad_up, 0)[None]
    down_share = send_half(grad_down, 0)[None]

    outputs = []
    input_grads = []
    grad_qkv = jnp.zeros((width, 3 * width), f32)
    grad_proj = jnp.zeros((width, width), f32)
    grad_router = jnp.zeros((width, experts), f32)
    grad_attn = jnp.zeros((width,), f32)
    grad_expert = jnp.zeros((width,), f32)
    grad_near = jnp.zeros((PAIRS, 1, 2 * TILE), f32)
    for s in state:
        upstream = s["cot"].astype(f32)
        returned = s["back"].reshape(slots, width)
        picked = [mm(p, returned, ((1,), (0,))) for p in s["picks"]]
        outputs.append((s["hidden"] + functools.reduce(jnp.add, picked)).astype(bf16))
        scaled = jnp.stack([jnp.sum(p * upstream, axis=1) for p in picked], axis=1)
        chosen_grad = scaled - s["gates"] * jnp.sum(scaled, axis=1, keepdims=True)
        logit_grad = jnp.sum(jnp.where(s["hot"], chosen_grad[:, :, None], 0.0), axis=1).astype(bf16)
        every_pick = functools.reduce(jnp.add, s["picks"])
        shared_grad = mm(every_pick, s["grad_back"].reshape(slots, width), ((1,), (0,)))
        shared_grad = shared_grad + mm(logit_grad, router_all, ((1,), (1,)))
        grad_router = grad_router + mm(s["shared"], logit_grad, ((0,), (0,)))
        unit = s["hidden"] * s["inv_two"]
        grad_expert = grad_expert + jnp.sum(shared_grad * unit, axis=0)
        inner = shared_grad * expert_scale
        hidden_grad = upstream + s["inv_two"] * (
            inner - unit * jnp.mean(inner * unit, axis=1, keepdims=True)
        )
        branch_grad = hidden_grad.astype(bf16)
        grad_proj = grad_proj + mm(s["attended"], branch_grad, ((0,), (0,)))
        attended_grad = mm(branch_grad, proj_all, ((1,), (1,))).astype(bf16)
        dq, dk, dv, dkp, dvp, near = attend_back(
            *s["view"], s["attended"], attended_grad, s["lse"]
        )
        grad_near = grad_near + near
        back = jnp.concatenate([dkp, dvp], axis=1)
        own = jnp.concatenate([dk, dv], axis=1).astype(f32)
        if ways == 2:
            own = own + lax.ppermute(back, "ctx", [(1, 0)]).astype(f32)
        else:
            every = jnp.zeros((BACK + seq_len, 2 * width), bf16)
            every = lax.dynamic_update_slice_in_dim(every, back, me * length, 0)
            own = own + lax.psum_scatter(
                every[BACK:], "ctx", scatter_dimension=0, tiled=True
            ).astype(f32)
        qkv_grad = jnp.concatenate([dq, own.astype(bf16)], axis=1)
        grad_qkv = grad_qkv + mm(s["normed"], qkv_grad, ((0,), (0,)))
        normed_grad = mm(qkv_grad, qkv_all, ((1,), (1,)))
        unit = s["rows"] * s["inv_one"]
        grad_attn = grad_attn + jnp.sum(normed_grad * unit, axis=0)
        inner = normed_grad * attn_scale
        input_part = s["inv_one"] * (inner - unit * jnp.mean(inner * unit, axis=1, keepdims=True))
        input_grads.append((hidden_grad + input_part).astype(bf16))

    by_distance = grad_near.reshape(HEADS, TILE)
    hot_near = jnp.where(
        jnp.arange(buckets)[:, None] < buckets - 1, hot_bucket[:, :TILE], 0.0
    )
    grad_bias = jnp.sum(by_distance[:, None, :] * hot_near[None], axis=2)
    far = jnp.where(jnp.arange(buckets) == buckets - 1, 1.0, 0.0)
    grad_bias = grad_bias - jnp.sum(grad_bias, axis=1, keepdims=True) * far
    bias_total = lax.psum(grad_bias, ("ctx", "exp"))
    total = scatter_sum(
        jnp.concatenate(
            [
                grad_qkv,
                grad_proj,
                grad_router,
                grad_attn[:, None],
                grad_expert[:, None],
                jnp.zeros((width, pad), f32),
            ],
            axis=1,
        )
    )
    return (
        jnp.stack(outputs)[:, None],
        jnp.stack(input_grads)[:, None],
        total[:, : 3 * width],
        total[:, 3 * width : wide],
        total[:, wide : wide + experts],
        total[:, wide + experts],
        total[:, wide + experts + 1],
        bias_total,
        up_share,
        down_share,
    )


def solution(mesh):
    placed = (
        P(None, "exp", "ctx", None),
        P(None, "exp", "ctx", None),
        P(None, "exp", None),
        P(None, "exp", "ctx", None),
        P(("ctx", "exp"), None),
        P(("ctx", "exp"), None),
        P(("ctx", "exp"), None),
        P(("ctx", "exp")),
        P(("ctx", "exp")),
        P(),
        P("exp", "ctx", None),
        P("exp", "ctx", None),
    )
    return jax.shard_map(
        shards,
        mesh=mesh,
        in_specs=placed,
        out_specs=(
            P(None, "exp", "ctx", None),
            P(None, "exp", "ctx", None),
            P(("ctx", "exp"), None),
            P(("ctx", "exp"), None),
            P(("ctx", "exp"), None),
            P(("ctx", "exp")),
            P(("ctx", "exp")),
            P(),
            P("exp", "ctx", None),
            P("exp", "ctx", None),
        ),
        check_vma=False,
    )
```

```python
import functools
import math

import jax
import jax.numpy as jnp
from jax import lax
from jax.experimental import pallas as pl
from jax.experimental.pallas import tpu as pltpu
from jax.sharding import PartitionSpec as P

HEADS = 12
HEAD = 64
PAIRS = HEADS // 2
TILE = 128
BACK = 512
SPAN = BACK // TILE + 1
MASKED = -1000000000.0

epsilon = 1e-06
thresholds = (19, 21, 24, 27, 31, 35, 40, 46, 52, 59, 67, 77, 87, 99, 113)
bf16 = jnp.bfloat16
f32 = jnp.float32


def bucket_of(distance):
    distance = jnp.maximum(distance, 0)
    beyond = jnp.zeros_like(distance)
    for threshold in thresholds:
        beyond = beyond + (distance >= threshold).astype(jnp.int32)
    return jnp.where(distance < 16, distance, 16 + beyond)


def mm(a, b, dims):
    return lax.dot_general(a, b, (dims, ((), ())), preferred_element_type=f32)


def stack_heads(rows):
    lane = lax.broadcasted_iota(jnp.int32, rows.shape, 1)
    zero = jnp.zeros_like(rows)
    return jnp.concatenate(
        [jnp.where(lane < HEAD, rows, zero), jnp.where(lane >= HEAD, rows, zero)], axis=0
    )


def fold_heads(wide):
    return jnp.concatenate([wide[:HEAD, :TILE], wide[HEAD:, TILE:]], axis=0)


def fill_mask(mask, qd_ref, kd_ref):
    for qi in range(qd_ref.shape[1] // TILE):
        docs_row = qd_ref[:, qi * TILE : (qi + 1) * TILE]
        for j in range(SPAN):
            kt = (qi + j) * TILE
            column = jnp.broadcast_to(kd_ref[:, kt : kt + TILE], (TILE, TILE)).T
            mask[qi, j * TILE : (j + 1) * TILE, :] = jnp.where(
                column == docs_row, 0.0, MASKED
            ).astype(f32)


def fill_bias(bias, bv_ref):
    for head in range(2):
        for d in range(2):
            row = jnp.broadcast_to(bv_ref[0, 2 * head + d : 2 * head + d + 1, :], (TILE, 2 * TILE))
            rolled = pltpu.roll(row, 0, 1, stride=1, stride_axis=0)
            bias[d, :, head * TILE : (head + 1) * TILE] = rolled[:, :TILE]


def masked_scores(scores, mask, bias, qi, tiles):
    parts = []
    for j in range(tiles):
        d = tiles - 1 - j
        off = (SPAN - tiles + j) * TILE
        m = mask[qi, off : off + TILE, :]
        x = scores[j * TILE : (j + 1) * TILE] + jnp.concatenate([m, m], axis=1)
        if d < 2:
            x = x + bias[d]
        parts.append(x)
    return parts


def fwd_kernel(tiles, q_ref, k_ref, v_ref, kp_ref, vp_ref, qd_ref, kd_ref, bv_ref, o_ref, lse_ref,
               kwin, vwin_t, bias, mask):
    @pl.when(pl.program_id(0) == 0)
    def _():
        fill_mask(mask, qd_ref, kd_ref)

    fill_bias(bias, bv_ref)
    kwin[:BACK] = kp_ref[...]
    kwin[BACK:] = k_ref[...]
    for t in range(BACK // TILE):
        vwin_t[:, t * TILE : (t + 1) * TILE] = vp_ref[t * TILE : (t + 1) * TILE, :].T
    for t in range(q_ref.shape[0] // TILE):
        at = BACK + t * TILE
        vwin_t[:, at : at + TILE] = v_ref[t * TILE : (t + 1) * TILE, :].T

    def step(qi, carry):
        q0 = pl.multiple_of(qi * TILE, TILE)
        q2 = stack_heads(q_ref[pl.ds(q0, TILE), :] * 0.125)

        def branch(count):
            def go():
                lo = pl.multiple_of((qi + SPAN - count) * TILE, TILE)
                keys = kwin[pl.ds(lo, count * TILE), :]
                parts = masked_scores(mm(keys, q2, ((1,), (1,))), mask, bias, qi, count)
                top = functools.reduce(jnp.maximum, parts)
                top = jnp.max(top, axis=0, keepdims=True)
                probs = [jnp.exp(x - top) for x in parts]
                total = jnp.sum(functools.reduce(jnp.add, probs), axis=0, keepdims=True)
                low = jnp.concatenate([p.astype(bf16) for p in probs], axis=0)
                out = fold_heads(mm(vwin_t[:, pl.ds(lo, count * TILE)], low, ((1,), (0,))))
                inv = 1.0 / total
                row = lax.broadcasted_iota(jnp.int32, (TILE, TILE), 0)
                out = out * jnp.where(row < HEAD, inv[:, :TILE], inv[:, TILE:])
                o_ref[pl.ds(q0, TILE), :] = out.T.astype(bf16)
                lse_ref[0, pl.ds(qi, 1), :] = top + jnp.log(total)
                return 0

            return go

        lax.switch(tiles[qi] - 1, [branch(c) for c in range(1, SPAN + 1)])
        return carry

    lax.fori_loop(0, q_ref.shape[0] // TILE, step, 0)


def bwd_kernel(tiles, q_ref, k_ref, v_ref, kp_ref, vp_ref, qd_ref, kd_ref, bv_ref, o_ref, do_ref,
               lse_ref, dq_ref, own_ref, back_ref, near_ref,
               kwin, kwin_t, vwin, dk, dv, near, bias, mask):
    @pl.when(pl.program_id(0) == 0)
    def _():
        fill_mask(mask, qd_ref, kd_ref)

    fill_bias(bias, bv_ref)
    kwin[:BACK] = kp_ref[...]
    kwin[BACK:] = k_ref[...]
    vwin[:BACK] = vp_ref[...]
    vwin[BACK:] = v_ref[...]
    for t in range(kwin.shape[0] // TILE):
        kwin_t[:, t * TILE : (t + 1) * TILE] = kwin[t * TILE : (t + 1) * TILE, :].T
    dk[...] = jnp.zeros_like(dk)
    dv[...] = jnp.zeros_like(dv)
    near[...] = jnp.zeros_like(near)

    def step(qi, carry):
        q0 = pl.multiple_of(qi * TILE, TILE)
        q2 = stack_heads(q_ref[pl.ds(q0, TILE), :] * 0.125)
        do = do_ref[pl.ds(q0, TILE), :]
        do2 = stack_heads(do)
        lse = lse_ref[0, pl.ds(qi, 1), :]
        prod = (do.astype(f32) * o_ref[pl.ds(q0, TILE), :].astype(f32)).T
        delta = jnp.concatenate(
            [jnp.sum(prod[:HEAD], axis=0, keepdims=True),
             jnp.sum(prod[HEAD:], axis=0, keepdims=True)],
            axis=1,
        )

        def branch(count):
            def go():
                lo = pl.multiple_of((qi + SPAN - count) * TILE, TILE)
                rows = pl.ds(lo, count * TILE)
                parts = masked_scores(
                    mm(kwin[rows, :], q2, ((1,), (1,))), mask, bias, qi, count
                )
                prob_grad = mm(vwin[rows, :], do2, ((1,), (1,)))
                lows = []
                grads = []
                for j in range(count):
                    prob = jnp.exp(parts[j] - lse)
                    grad = prob * (prob_grad[j * TILE : (j + 1) * TILE] - delta)
                    if j == count - 1:
                        near[...] += grad
                    elif j == count - 2:
                        r = lax.broadcasted_iota(jnp.int32, grad.shape, 0)
                        c = lax.broadcasted_iota(jnp.int32, grad.shape, 1)
                        c = jnp.where(c >= TILE, c - TILE, c)
                        near[...] += jnp.where(c < r, grad, 0.0)
                    lows.append(prob.astype(bf16))
                    grads.append(grad.astype(bf16))
                low = jnp.concatenate(lows, axis=0)
                score_grad = jnp.concatenate(grads, axis=0)
                dk[rows, :] += mm(score_grad, q2, ((1,), (0,)))
                dv[rows, :] += mm(low, do2, ((1,), (0,)))
                dq = fold_heads(mm(kwin_t[:, rows], score_grad, ((1,), (0,))))
                dq_ref[pl.ds(q0, TILE), :] = (dq.T * 0.125).astype(bf16)
                return 0

            return go

        lax.switch(tiles[qi] - 1, [branch(c) for c in range(1, SPAN + 1)])
        return carry

    lax.fori_loop(0, q_ref.shape[0] // TILE, step, 0)
    for i, total in enumerate((dk, dv)):
        back_ref[i] = total[:BACK].astype(bf16)
        own_ref[i] = total[BACK:].astype(bf16)
    for head in range(2):
        at = slice(head * TILE, (head + 1) * TILE)
        turned = near[:, at]
        r = lax.broadcasted_iota(jnp.int32, turned.shape, 0)
        bit = 1
        while bit < TILE:
            turned = jnp.where((r & bit) > 0, pltpu.roll(turned, TILE - bit, 1), turned)
            bit *= 2
        near_ref[0, :, at] = jnp.sum(turned, axis=0, keepdims=True)


def attention_specs(length):
    full = lambda p, *_: (0, 0)
    lanes = lambda off: (lambda p, *_: (0, p + off))
    return [
        pl.BlockSpec((length, TILE), lanes(0)),
        pl.BlockSpec((length, TILE), lanes(0)),
        pl.BlockSpec((length, TILE), lanes(PAIRS)),
        pl.BlockSpec((BACK, TILE), lanes(0)),
        pl.BlockSpec((BACK, TILE), lanes(PAIRS)),
        pl.BlockSpec((1, length), full),
        pl.BlockSpec((1, BACK + length), full),
        pl.BlockSpec((1, 4, 2 * TILE), lambda p, *_: (p, 0, 0)),
    ]


def attend(tiles, queries, kv, kv_back, query_docs, key_docs, bias_rows):
    length = queries.shape[0]
    width = HEADS * HEAD
    blocks = length // TILE
    return pl.pallas_call(
        fwd_kernel,
        grid_spec=pltpu.PrefetchScalarGridSpec(
            num_scalar_prefetch=1,
            grid=(PAIRS,),
            in_specs=attention_specs(length),
            out_specs=[
                pl.BlockSpec((length, TILE), lambda p, *_: (0, p)),
                pl.BlockSpec((1, blocks, 2 * TILE), lambda p, *_: (p, 0, 0)),
            ],
            scratch_shapes=[
                pltpu.VMEM((BACK + length, TILE), bf16),
                pltpu.VMEM((TILE, BACK + length), bf16),
                pltpu.VMEM((2, TILE, 2 * TILE), f32),
                pltpu.VMEM((blocks, SPAN * TILE, TILE), f32),
            ],
        ),
        out_shape=[
            jax.ShapeDtypeStruct((length, width), bf16),
            jax.ShapeDtypeStruct((PAIRS, blocks, 2 * TILE), f32),
        ],
        compiler_params=pltpu.CompilerParams(vmem_limit_bytes=32 * 2**20),
        cost_estimate=pl.CostEstimate(
            flops=4 * 2 * HEADS * length * BACK * 128, bytes_accessed=6 * 2**20,
            transcendentals=HEADS * length * BACK,
        ),
        name="attend",
    )(tiles, queries, kv, kv, kv_back, kv_back, query_docs, key_docs, bias_rows)


def attend_back(tiles, queries, kv, kv_back, query_docs, key_docs, bias_rows, out, out_grad, lse):
    length = queries.shape[0]
    width = HEADS * HEAD
    blocks = length // TILE
    own = pl.BlockSpec((length, TILE), lambda p, *_: (0, p))
    both = lambda n: pl.BlockSpec((2, n, TILE), lambda p, *_: (0, 0, p))
    return pl.pallas_call(
        bwd_kernel,
        grid_spec=pltpu.PrefetchScalarGridSpec(
            num_scalar_prefetch=1,
            grid=(PAIRS,),
            in_specs=attention_specs(length)
            + [own, own, pl.BlockSpec((1, blocks, 2 * TILE), lambda p, *_: (p, 0, 0))],
            out_specs=[own, both(length), both(BACK),
                       pl.BlockSpec((1, 1, 2 * TILE), lambda p, *_: (p, 0, 0))],
            scratch_shapes=[
                pltpu.VMEM((BACK + length, TILE), bf16),
                pltpu.VMEM((TILE, BACK + length), bf16),
                pltpu.VMEM((BACK + length, TILE), bf16),
                pltpu.VMEM((BACK + length, TILE), f32),
                pltpu.VMEM((BACK + length, TILE), f32),
                pltpu.VMEM((TILE, 2 * TILE), f32),
                pltpu.VMEM((2, TILE, 2 * TILE), f32),
                pltpu.VMEM((blocks, SPAN * TILE, TILE), f32),
            ],
        ),
        out_shape=[
            jax.ShapeDtypeStruct((length, width), bf16),
            jax.ShapeDtypeStruct((2, length, width), bf16),
            jax.ShapeDtypeStruct((2, BACK, width), bf16),
            jax.ShapeDtypeStruct((PAIRS, 1, 2 * TILE), f32),
        ],
        compiler_params=pltpu.CompilerParams(vmem_limit_bytes=32 * 2**20),
        cost_estimate=pl.CostEstimate(
            flops=10 * 2 * HEADS * length * BACK * 128, bytes_accessed=12 * 2**20,
            transcendentals=HEADS * length * BACK,
        ),
        name="attend_back",
    )(tiles, queries, kv, kv, kv_back, kv_back, query_docs, key_docs, bias_rows, out, out_grad, lse)


GELU_A = 0.7978845608028654
GELU_B = 0.044715


def expert_kernel(more, capacity, room, chunk, x_ref, cot_ref, up_ref, down_ref, *refs):
    if more:
        up_before, down_before, *refs = refs
    out_ref, du_ref, dd_ref, y_sum, back_sum, x, result_grad, gate, act_all, pre_grad_all = refs
    rows, width = x.shape
    step = pl.program_id(0)

    @pl.when(step == 0)
    def _():
        lane = lax.broadcasted_iota(jnp.int32, (1, TILE), 1)
        for e in range(rows // room):
            at = e * room
            x[at : at + room, :] = x_ref[e]
            line = x_ref[e, capacity : capacity + 1, : 2 * TILE].astype(f32)
            line = jnp.where(lane < capacity, line[:, :TILE] + line[:, TILE:], 0.0)
            column = jnp.broadcast_to(line, (TILE, TILE)).T[:room]
            gate[at : at + room, :] = column
            for c in range(0, width, TILE):
                result_grad[at : at + room, c : c + TILE] = (
                    cot_ref[e, :, c : c + TILE].astype(f32) * column
                ).astype(bf16)
        y_sum[...] = jnp.zeros_like(y_sum)
        back_sum[...] = jnp.zeros_like(back_sum)

    def part(i, carry):
        r = pl.ds(pl.multiple_of(i * chunk, chunk), chunk)
        pre = mm(x[r, :], up_ref[...], ((1,), (0,)))
        act_grad = mm(result_grad[r, :], down_ref[...], ((1,), (1,)))
        square = pre * pre
        half = 0.5 + 0.5 * jnp.tanh(pre * (GELU_A + (GELU_A * GELU_B) * square))
        act = (pre * half).astype(bf16)
        slope = 2.0 * GELU_A + (6.0 * GELU_A * GELU_B) * square
        pre_grad = (act_grad * (half * (1.0 + pre * (1.0 - half) * slope))).astype(bf16)
        act_all[r, :] = act
        pre_grad_all[r, :] = pre_grad
        y_sum[r, :] += mm(act, down_ref[...], ((1,), (0,)))
        back_sum[r, :] += mm(pre_grad, up_ref[...], ((1,), (1,)))
        return carry

    lax.fori_loop(0, rows // chunk, part, 0)
    dd = mm(act_all[...], result_grad[...], ((0,), (0,)))
    du = mm(x[...], pre_grad_all[...], ((0,), (0,)))
    if more:
        dd = dd + down_before[...]
        du = du + up_before[...]
    dd_ref[...] = dd
    du_ref[...] = du

    @pl.when(step == pl.num_programs(0) - 1)
    def _():
        for e in range(rows // room):
            at = e * room
            for c in range(0, width, TILE):
                scaled = y_sum[at : at + room, c : c + TILE] * gate[at : at + room, :]
                out_ref[e, :room, c : c + TILE] = scaled.astype(bf16)
            out_ref[e, room:, :] = back_sum[at : at + room, :].astype(bf16)


def run_experts(x, cot, batch, up, down, before, capacity):
    sources, room, width = x.shape
    rows = sources * room
    hidden = up.shape[1]
    part = math.gcd(hidden, 512)
    chunk = rows // 2 if rows % 32 == 0 else rows
    once = pl.Buffered(1)
    columns = pl.BlockSpec((width, part), lambda t: (0, t))
    lines = pl.BlockSpec((part, width), lambda t: (t, 0))
    more = len(before) > 0
    return pl.pallas_call(
        functools.partial(expert_kernel, more, capacity, room, chunk),
        grid=(hidden // part,),
        in_specs=[
            pl.BlockSpec((sources, room, width), lambda t: (0, 0, 0), pipeline_mode=once),
            pl.BlockSpec((sources, room, width), lambda t: (0, batch, 0), pipeline_mode=once),
            columns,
            lines,
        ]
        + ([columns, lines] if more else []),
        out_specs=[
            pl.BlockSpec((sources, 2 * room, width), lambda t: (0, 0, 0), pipeline_mode=once),
            columns,
            lines,
        ],
        out_shape=[
            jax.ShapeDtypeStruct((sources, 2 * room, width), bf16),
            jax.ShapeDtypeStruct((width, hidden), f32),
            jax.ShapeDtypeStruct((hidden, width), f32),
        ],
        scratch_shapes=[
            pltpu.VMEM((rows, width), f32),
            pltpu.VMEM((rows, width), f32),
            pltpu.VMEM((rows, width), bf16),
            pltpu.VMEM((rows, width), bf16),
            pltpu.VMEM((rows, TILE), f32),
            pltpu.VMEM((rows, part), bf16),
            pltpu.VMEM((rows, part), bf16),
        ],
        input_output_aliases={4: 1, 5: 2} if more else {},
        compiler_params=pltpu.CompilerParams(vmem_limit_bytes=60 * 2**20),
        cost_estimate=pl.CostEstimate(
            flops=12 * rows * width * hidden, bytes_accessed=40 * 2**20,
            transcendentals=rows * hidden,
        ),
        name="experts",
    )(x, cot, up, down, *before)


def bits_of(axis):
    return [1 << b for b in range(lax.axis_size(axis).bit_length() - 1)][::-1]


def power_of_two(axis):
    size = lax.axis_size(axis)
    return size & (size - 1) == 0


def swap(x, axis, bit):
    size = lax.axis_size(axis)
    return lax.ppermute(x, axis, [(i, i ^ bit) for i in range(size)])


def ordered(x, other, axis, bit):
    high = (lax.axis_index(axis) & bit) > 0
    return jnp.where(high, other, x), jnp.where(high, x, other)


def after(x, *others):
    return lax.optimization_barrier((x, *others))[0]


def gather_rows(left, right):
    if not (power_of_two("ctx") and power_of_two("exp")):
        return [lax.all_gather(x, ("ctx", "exp"), axis=0, tiled=True) for x in (left, right)]
    bits = bits_of("exp")
    last = bits[-2:]
    parts = [left, right]
    held = [x[None] for x in parts]
    for bit in bits[:-2]:
        got = [swap(h, "exp", bit) for h in held]
        held = [
            jnp.stack(ordered(h, g, "exp", bit), axis=1).reshape((-1,) + h.shape[1:])
            for h, g in zip(held, got)
        ]
    got = [swap(h, "exp", bit) for h, bit in zip(held, last)]
    held = [jnp.stack(ordered(h, g, "exp", bit), axis=1) for h, g, bit in zip(held, got, last)]
    got = [swap(h, "exp", bit) for h, bit in zip(held, last[::-1])]
    held = [
        jnp.stack(ordered(h, g, "exp", bit), axis=at)
        for h, g, bit, at in zip(held, got, last[::-1], (2, 1))
    ]
    held = [h.reshape(-1, h.shape[-1]) for h in held]
    for bit in bits_of("ctx"):
        got = [swap(h, "ctx", bit) for h in held]
        held = [
            jnp.stack(ordered(h, g, "ctx", bit), axis=0).reshape(-1, h.shape[-1])
            for h, g in zip(held, got)
        ]
    return held


def pair_rows(x, axis):
    if lax.axis_size("ctx") != 2:
        return lax.all_gather(x, "ctx", axis=axis, tiled=True)
    return jnp.concatenate(ordered(x, swap(x, "ctx", 1), "ctx", 1), axis=axis)


def send_half(x, axis):
    ways = lax.axis_size("ctx")
    if ways != 2:
        return lax.psum_scatter(x.astype(bf16), "ctx", scatter_dimension=axis, tiled=True).astype(f32)
    part = x.shape[axis] // 2
    me = lax.axis_index("ctx")
    mine = lax.dynamic_slice_in_dim(x, me * part, part, axis)
    theirs = lax.dynamic_slice_in_dim(x, (1 - me) * part, part, axis)
    return mine + swap(theirs.astype(bf16), "ctx", 1).astype(f32)


def halve(x, axis, bit, dim):
    side = ((lax.axis_index(axis) & bit) > 0).astype(jnp.int32)
    mine = lax.dynamic_index_in_dim(x, side, dim, keepdims=False)
    theirs = lax.dynamic_index_in_dim(x, 1 - side, dim, keepdims=False)
    return mine + swap(theirs.astype(bf16), axis, bit).astype(f32)


def scatter_sum(left, right):
    if not (power_of_two("exp") and lax.axis_size("ctx") == 2 and lax.axis_size("exp") > 3):
        return [
            lax.psum_scatter(x, ("ctx", "exp"), scatter_dimension=0, tiled=True)
            for x in (left, right)
        ]
    bits = bits_of("exp")
    held = [send_half(x, 0) for x in (left, right)]
    held = [h.reshape((-1, 2, 2, h.shape[0] // lax.axis_size("exp"), h.shape[1])) for h in held]
    high, low = bits[-2:]
    held = [halve(held[0], "exp", high, 1), halve(held[1], "exp", low, 2)]
    held = [halve(held[0], "exp", low, 1), halve(held[1], "exp", high, 1)]
    for bit in bits[:-2][::-1]:
        held = [halve(h.reshape((-1, 2) + h.shape[1:]), "exp", bit, 1) for h in held]
    return [h.reshape(h.shape[-2:]) for h in held]


def total_of(x):
    if not (power_of_two("ctx") and power_of_two("exp")):
        return lax.psum(x, ("ctx", "exp"))
    for axis in ("ctx", "exp"):
        for bit in bits_of(axis):
            x = x + swap(x, axis, bit)
    return x


def shards(
    inputs,
    cotangent,
    doc_ids,
    routes,
    query_key_value_weight,
    output_projection_weight,
    router,
    attn_gain,
    expert_gain,
    position_bias,
    expert_up,
    expert_down,
):
    batches = inputs.shape[0]
    length = inputs.shape[2]
    width = inputs.shape[3]
    top = routes.shape[3]
    ways = lax.axis_size("ctx")
    experts = lax.axis_size("exp")
    capacity = max(2, top * length * 10 // (7 * experts))
    room = (capacity + 1 + 15) // 16 * 16
    slots = experts * room
    seq_len = doc_ids.shape[2]
    buckets = position_bias.shape[1]
    me = lax.axis_index("ctx")

    expert_ids = jnp.arange(experts, dtype=jnp.int32)
    slot_rows = jnp.arange(slots, dtype=jnp.int32)
    earlier = jnp.tril(jnp.ones((length, length), bf16), -1)
    hots, slot_of, holds, spreads = [], [], [], []
    for b in range(batches):
        route_ids = routes[b, 0]
        hot = route_ids[:, :, None] == expert_ids[None, None, :]
        used = jnp.any(hot, axis=1)
        rank = mm(earlier, used.astype(bf16), ((1,), (0,))).astype(jnp.int32)
        slot = jnp.sum(jnp.where(hot, rank[:, None, :], 0), axis=2) + route_ids * room
        hold = [slot[None, :, k] == slot_rows[:, None] for k in range(top)]
        hots.append(hot)
        slot_of.append(slot)
        holds.append(hold)
        spreads.append(functools.reduce(jnp.logical_or, hold).astype(bf16))

    def dispatch(b, rows):
        sent = mm(spreads[b], rows, ((1,), (0,))).astype(bf16)
        return sent.reshape(experts, room, width)

    def cross(x):
        return lax.all_to_all(x, "exp", split_axis=0, concat_axis=0, tiled=True)

    pad = -(experts + 2) % 128
    left, right = gather_rows(
        jnp.concatenate([query_key_value_weight[:, :width], output_projection_weight], axis=1),
        jnp.concatenate(
            [
                query_key_value_weight[:, width:],
                router,
                attn_gain[:, None],
                expert_gain[:, None],
                jnp.zeros((router.shape[0], pad), bf16),
            ],
            axis=1,
        ),
    )
    query_weight = left[:, :width]
    proj_weight = left[:, width:]
    kv_weight = right[:, : 2 * width]
    router_all = right[:, 2 * width : 2 * width + experts]
    gains = right[:, 2 * width + experts : 2 * width + experts + 2].astype(f32)
    attn_scale = gains[:, 0]
    expert_scale = gains[:, 1]
    up_all = pair_rows(expert_up[0], 0)
    down_all = pair_rows(expert_down[0], 0)

    cots = [cotangent[b, 0] for b in range(batches)]
    sent = jnp.concatenate([dispatch(b, cots[b]) for b in range(batches)], axis=1)
    cot_here = cross(after(sent, left, right))

    distance = jnp.arange(2 * TILE, dtype=jnp.int32)
    hot_bucket = (
        bucket_of(distance)[None, :] == jnp.arange(buckets, dtype=jnp.int32)[:, None]
    ).astype(f32)
    by_distance = jnp.sum(
        position_bias.astype(f32)[:, :, None] * hot_bucket[None], axis=1
    ) - position_bias.astype(f32)[:, buckets - 1 :]
    close = jnp.where(distance < TILE, by_distance, MASKED)
    beside = jnp.roll(by_distance, -TILE, axis=1)
    bias_rows = jnp.stack([close, beside], axis=1).reshape(PAIRS, 4, 2 * TILE)

    def norm_stats(values):
        return lax.rsqrt(jnp.mean(values * values, axis=-1, keepdims=True) + epsilon)

    state = []
    for b in range(batches):
        rows = inputs[b, 0].astype(f32)
        inv_one = norm_stats(rows)
        normed = (rows * inv_one * attn_scale).astype(bf16)
        kv = mm(normed, kv_weight, ((1,), (0,))).astype(bf16)
        queries = mm(normed, query_weight, ((1,), (0,))).astype(bf16)
        docs = doc_ids[b, 0].astype(f32)
        padded = jnp.concatenate([jnp.full((BACK,), -1.0, f32), docs])
        key_docs = lax.dynamic_slice_in_dim(padded, me * length, BACK + length)
        query_docs = key_docs[BACK:]
        if ways == 2:
            kv_back = lax.ppermute(kv, "ctx", [(0, 1)])
        else:
            every = lax.all_gather(kv, "ctx", axis=0, tiled=True)
            every = jnp.concatenate([jnp.zeros((BACK, 2 * width), bf16), every], axis=0)
            kv_back = lax.dynamic_slice_in_dim(every, me * length, BACK, 0)
        firsts = query_docs[::TILE]
        start = jnp.sum((key_docs[None, :] < firsts[:, None]).astype(jnp.int32), axis=1)
        tiles = jnp.arange(length // TILE, dtype=jnp.int32) + SPAN - start // TILE
        tiles = jnp.clip(tiles, 1, SPAN)
        view = (tiles, queries, kv, kv_back, query_docs[None], key_docs[None], bias_rows)
        state.append(dict(rows=rows, inv_one=inv_one, normed=normed, view=view))

    last = cot_here
    for b, s in enumerate(state):
        attended, lse = attend(*s["view"])
        hidden = s["rows"] + mm(attended, proj_weight, ((1,), (0,)))
        inv_two = norm_stats(hidden)
        shared = (hidden * inv_two * expert_scale).astype(bf16)
        logits = mm(shared, router_all, ((1,), (0,)))
        hot = hots[b]
        chosen = jnp.sum(jnp.where(hot, logits[:, None, :], 0.0), axis=2)
        gate_exp = jnp.exp(chosen - jnp.max(chosen, axis=1, keepdims=True))
        gates = gate_exp / jnp.sum(gate_exp, axis=1, keepdims=True)
        gate_slots = sum(
            jnp.sum(jnp.where(holds[b][k], gates[None, :, k], 0.0), axis=1) for k in range(top)
        ).reshape(experts, 1, room)
        gate_slots = jnp.pad(gate_slots, ((0, 0), (0, 0), (0, TILE - room)))
        gate_high = gate_slots.astype(bf16)
        gate_low = (gate_slots - gate_high.astype(f32)).astype(bf16)
        gate_row = jnp.concatenate(
            [gate_high, gate_low, jnp.zeros((experts, 1, width - 2 * TILE), bf16)], axis=2
        )
        at_gate = lax.broadcasted_iota(jnp.int32, (1, room, 1), 1) == capacity
        sent = jnp.where(at_gate, gate_row, dispatch(b, shared))
        s.update(attended=attended, lse=lse, hidden=hidden, inv_two=inv_two, shared=shared,
                 gates=gates, here=cross(after(sent, last)))
        last = s["here"]

    grads = ()
    for b, s in enumerate(state):
        out, *grads = run_experts(s["here"], cot_here, b, up_all, down_all, grads, capacity)
        s["back"] = cross(after(out, last))
        last = s["back"]
    grad_up, grad_down = grads
    up_share = send_half(grad_up, 0)[None]
    down_share = send_half(grad_down, 0)[None]

    outputs = []
    input_grads = []
    parts = []
    for b, s in enumerate(state):
        upstream = cots[b].astype(f32)
        packet = after(s["back"], *input_grads)
        returned = packet[:, :room].reshape(slots, width)
        grad_rows = packet[:, room:].reshape(slots, width)
        slot = slot_of[b]
        picks = [(slot[:, k : k + 1] == slot_rows[None, :]).astype(bf16) for k in range(top)]
        picked = [mm(p, returned, ((1,), (0,))) for p in picks]
        outputs.append((s["hidden"] + functools.reduce(jnp.add, picked)).astype(bf16))
        scaled = jnp.stack([jnp.sum(p * upstream, axis=1) for p in picked], axis=1)
        chosen_grad = scaled - s["gates"] * jnp.sum(scaled, axis=1, keepdims=True)
        logit_grad = jnp.sum(jnp.where(hots[b], chosen_grad[:, :, None], 0.0), axis=1).astype(bf16)
        shared_grad = mm(functools.reduce(jnp.add, picks), grad_rows, ((1,), (0,)))
        shared_grad = shared_grad + mm(logit_grad, router_all, ((1,), (1,)))
        grad_router = mm(s["shared"], logit_grad, ((0,), (0,)))
        unit = s["hidden"] * s["inv_two"]
        grad_expert = jnp.sum(shared_grad * unit, axis=0)
        inner = shared_grad * expert_scale
        hidden_grad = upstream + s["inv_two"] * (
            inner - unit * jnp.mean(inner * unit, axis=1, keepdims=True)
        )
        branch_grad = hidden_grad.astype(bf16)
        grad_proj = mm(s["attended"], branch_grad, ((0,), (0,)))
        attended_grad = mm(branch_grad, proj_weight, ((1,), (1,))).astype(bf16)
        dq, own, back, near = attend_back(*s["view"], s["attended"], attended_grad, s["lse"])
        if ways == 2:
            got = lax.ppermute(back, "ctx", [(1, 0)])
        else:
            every = jnp.zeros((2, BACK + seq_len, width), bf16)
            every = lax.dynamic_update_slice_in_dim(every, back, me * length, 1)
            got = lax.psum_scatter(every[:, BACK:], "ctx", scatter_dimension=1, tiled=True)
        both = (own.astype(f32) + got.astype(f32)).astype(bf16)
        dkv = jnp.concatenate([both[0], both[1]], axis=1)
        normed = s["normed"]
        grad_query = mm(normed, dq, ((0,), (0,)))
        grad_kv = mm(normed, dkv, ((0,), (0,)))
        normed_grad = mm(dq, query_weight, ((1,), (1,))) + mm(dkv, kv_weight, ((1,), (1,)))
        unit = s["rows"] * s["inv_one"]
        grad_attn = jnp.sum(normed_grad * unit, axis=0)
        inner = normed_grad * attn_scale
        input_part = s["inv_one"] * (inner - unit * jnp.mean(inner * unit, axis=1, keepdims=True))
        input_grads.append((hidden_grad + input_part).astype(bf16))
        parts.append((grad_query, grad_kv, grad_proj, grad_router, grad_attn, grad_expert, near))

    grad_query, grad_kv, grad_proj, grad_router, grad_attn, grad_expert, near = (
        functools.reduce(jnp.add, p) for p in zip(*parts)
    )
    hot_near = jnp.where(
        jnp.arange(buckets)[:, None] < buckets - 1, hot_bucket[:, :TILE], 0.0
    )
    grad_bias = jnp.sum(near.reshape(HEADS, 1, TILE) * hot_near[None], axis=2)
    far = jnp.where(jnp.arange(buckets) == buckets - 1, 1.0, 0.0)
    bias_total = total_of(grad_bias - jnp.sum(grad_bias, axis=1, keepdims=True) * far)
    left, right = scatter_sum(
        jnp.concatenate([grad_query, grad_proj], axis=1),
        jnp.concatenate(
            [
                grad_kv,
                grad_router,
                grad_attn[:, None],
                grad_expert[:, None],
                jnp.zeros((width, pad), f32),
            ],
            axis=1,
        ),
    )
    return (
        jnp.stack(outputs)[:, None],
        jnp.stack(input_grads)[:, None],
        jnp.concatenate([left[:, :width], right[:, : 2 * width]], axis=1),
        left[:, width:],
        right[:, 2 * width : 2 * width + experts],
        right[:, 2 * width + experts],
        right[:, 2 * width + experts + 1],
        bias_total,
        up_share,
        down_share,
    )


def solution(mesh):
    placed = (
        P(None, "exp", "ctx", None),
        P(None, "exp", "ctx", None),
        P(None, "exp", None),
        P(None, "exp", "ctx", None),
        P(("ctx", "exp"), None),
        P(("ctx", "exp"), None),
        P(("ctx", "exp"), None),
        P(("ctx", "exp")),
        P(("ctx", "exp")),
        P(),
        P("exp", "ctx", None),
        P("exp", "ctx", None),
    )
    return jax.shard_map(
        shards,
        mesh=mesh,
        in_specs=placed,
        out_specs=(
            P(None, "exp", "ctx", None),
            P(None, "exp", "ctx", None),
            P(("ctx", "exp"), None),
            P(("ctx", "exp"), None),
            P(("ctx", "exp"), None),
            P(("ctx", "exp")),
            P(("ctx", "exp")),
            P(),
            P("exp", "ctx", None),
            P("exp", "ctx", None),
        ),
        check_vma=False,
    )
```

```python
import functools
import math

import jax
import jax.numpy as jnp
from jax import lax
from jax.experimental import pallas as pl
from jax.experimental.pallas import tpu as pltpu
from jax.sharding import PartitionSpec as P

HEADS = 12
HEAD = 64
PAIRS = HEADS // 2
TILE = 128
BACK = 512
SPAN = BACK // TILE + 1
MASKED = -1000000000.0

epsilon = 1e-06
thresholds = (19, 21, 24, 27, 31, 35, 40, 46, 52, 59, 67, 77, 87, 99, 113)
bf16 = jnp.bfloat16
f32 = jnp.float32


def bucket_of(distance):
    distance = jnp.maximum(distance, 0)
    beyond = jnp.zeros_like(distance)
    for threshold in thresholds:
        beyond = beyond + (distance >= threshold).astype(jnp.int32)
    return jnp.where(distance < 16, distance, 16 + beyond)


def mm(a, b, dims):
    return lax.dot_general(a, b, (dims, ((), ())), preferred_element_type=f32)


def stack_heads(rows):
    lane = lax.broadcasted_iota(jnp.int32, rows.shape, 1)
    zero = jnp.zeros_like(rows)
    return jnp.concatenate(
        [jnp.where(lane < HEAD, rows, zero), jnp.where(lane >= HEAD, rows, zero)], axis=0
    )


def fold_heads(wide):
    return jnp.concatenate([wide[:HEAD, :TILE], wide[HEAD:, TILE:]], axis=0)


def fill_mask(mask, qd_ref, kd_ref):
    for qi in range(qd_ref.shape[1] // TILE):
        docs_row = qd_ref[:, qi * TILE : (qi + 1) * TILE]
        for j in range(SPAN):
            kt = (qi + j) * TILE
            column = jnp.broadcast_to(kd_ref[:, kt : kt + TILE], (TILE, TILE)).T
            mask[qi, j * TILE : (j + 1) * TILE, :] = jnp.where(
                column == docs_row, 0.0, MASKED
            ).astype(f32)


def fill_bias(bias, bv_ref):
    for head in range(2):
        for d in range(2):
            row = jnp.broadcast_to(bv_ref[0, 2 * head + d : 2 * head + d + 1, :], (TILE, 2 * TILE))
            rolled = pltpu.roll(row, 0, 1, stride=1, stride_axis=0)
            bias[d, :, head * TILE : (head + 1) * TILE] = rolled[:, :TILE]


def masked_scores(scores, mask, bias, qi, tiles):
    parts = []
    for j in range(tiles):
        d = tiles - 1 - j
        off = (SPAN - tiles + j) * TILE
        m = mask[qi, off : off + TILE, :]
        x = scores[j * TILE : (j + 1) * TILE] + jnp.concatenate([m, m], axis=1)
        if d < 2:
            x = x + bias[d]
        parts.append(x)
    return parts


def fwd_kernel(tiles, q_ref, k_ref, v_ref, kp_ref, vp_ref, qd_ref, kd_ref, bv_ref, o_ref, lse_ref,
               kwin, vwin_t, bias, mask):
    @pl.when(pl.program_id(0) == 0)
    def _():
        fill_mask(mask, qd_ref, kd_ref)

    fill_bias(bias, bv_ref)
    kwin[:BACK] = kp_ref[...]
    kwin[BACK:] = k_ref[...]
    for t in range(BACK // TILE):
        vwin_t[:, t * TILE : (t + 1) * TILE] = vp_ref[t * TILE : (t + 1) * TILE, :].T
    for t in range(q_ref.shape[0] // TILE):
        at = BACK + t * TILE
        vwin_t[:, at : at + TILE] = v_ref[t * TILE : (t + 1) * TILE, :].T

    def step(qi, carry):
        q0 = pl.multiple_of(qi * TILE, TILE)
        q2 = stack_heads(q_ref[pl.ds(q0, TILE), :] * 0.125)

        def branch(count):
            def go():
                lo = pl.multiple_of((qi + SPAN - count) * TILE, TILE)
                keys = kwin[pl.ds(lo, count * TILE), :]
                parts = masked_scores(mm(keys, q2, ((1,), (1,))), mask, bias, qi, count)
                top = functools.reduce(jnp.maximum, parts)
                top = jnp.max(top, axis=0, keepdims=True)
                probs = [jnp.exp(x - top) for x in parts]
                total = jnp.sum(functools.reduce(jnp.add, probs), axis=0, keepdims=True)
                low = jnp.concatenate([p.astype(bf16) for p in probs], axis=0)
                out = fold_heads(mm(vwin_t[:, pl.ds(lo, count * TILE)], low, ((1,), (0,))))
                inv = 1.0 / total
                row = lax.broadcasted_iota(jnp.int32, (TILE, TILE), 0)
                out = out * jnp.where(row < HEAD, inv[:, :TILE], inv[:, TILE:])
                o_ref[pl.ds(q0, TILE), :] = out.T.astype(bf16)
                lse_ref[0, pl.ds(qi, 1), :] = top + jnp.log(total)
                return 0

            return go

        lax.switch(tiles[qi] - 1, [branch(c) for c in range(1, SPAN + 1)])
        return carry

    lax.fori_loop(0, q_ref.shape[0] // TILE, step, 0)


def bwd_kernel(tiles, q_ref, k_ref, v_ref, kp_ref, vp_ref, qd_ref, kd_ref, bv_ref, o_ref, do_ref,
               lse_ref, dq_ref, own_ref, back_ref, near_ref,
               kwin, kwin_t, vwin, dk, dv, near, bias, mask):
    @pl.when(pl.program_id(0) == 0)
    def _():
        fill_mask(mask, qd_ref, kd_ref)

    fill_bias(bias, bv_ref)
    kwin[:BACK] = kp_ref[...]
    kwin[BACK:] = k_ref[...]
    vwin[:BACK] = vp_ref[...]
    vwin[BACK:] = v_ref[...]
    for t in range(kwin.shape[0] // TILE):
        kwin_t[:, t * TILE : (t + 1) * TILE] = kwin[t * TILE : (t + 1) * TILE, :].T
    dk[...] = jnp.zeros_like(dk)
    dv[...] = jnp.zeros_like(dv)
    near[...] = jnp.zeros_like(near)

    def step(qi, carry):
        q0 = pl.multiple_of(qi * TILE, TILE)
        q2 = stack_heads(q_ref[pl.ds(q0, TILE), :] * 0.125)
        do = do_ref[pl.ds(q0, TILE), :]
        do2 = stack_heads(do)
        lse = lse_ref[0, pl.ds(qi, 1), :]
        prod = (do.astype(f32) * o_ref[pl.ds(q0, TILE), :].astype(f32)).T
        delta = jnp.concatenate(
            [jnp.sum(prod[:HEAD], axis=0, keepdims=True),
             jnp.sum(prod[HEAD:], axis=0, keepdims=True)],
            axis=1,
        )

        def branch(count):
            def go():
                lo = pl.multiple_of((qi + SPAN - count) * TILE, TILE)
                rows = pl.ds(lo, count * TILE)
                parts = masked_scores(
                    mm(kwin[rows, :], q2, ((1,), (1,))), mask, bias, qi, count
                )
                prob_grad = mm(vwin[rows, :], do2, ((1,), (1,)))
                lows = []
                grads = []
                for j in range(count):
                    prob = jnp.exp(parts[j] - lse)
                    grad = prob * (prob_grad[j * TILE : (j + 1) * TILE] - delta)
                    if j == count - 1:
                        near[...] += grad
                    elif j == count - 2:
                        r = lax.broadcasted_iota(jnp.int32, grad.shape, 0)
                        c = lax.broadcasted_iota(jnp.int32, grad.shape, 1)
                        c = jnp.where(c >= TILE, c - TILE, c)
                        near[...] += jnp.where(c < r, grad, 0.0)
                    lows.append(prob.astype(bf16))
                    grads.append(grad.astype(bf16))
                low = jnp.concatenate(lows, axis=0)
                score_grad = jnp.concatenate(grads, axis=0)
                dk[rows, :] += mm(score_grad, q2, ((1,), (0,)))
                dv[rows, :] += mm(low, do2, ((1,), (0,)))
                dq = fold_heads(mm(kwin_t[:, rows], score_grad, ((1,), (0,))))
                dq_ref[pl.ds(q0, TILE), :] = (dq.T * 0.125).astype(bf16)
                return 0

            return go

        lax.switch(tiles[qi] - 1, [branch(c) for c in range(1, SPAN + 1)])
        return carry

    lax.fori_loop(0, q_ref.shape[0] // TILE, step, 0)
    for i, total in enumerate((dk, dv)):
        back_ref[i] = total[:BACK].astype(bf16)
        own_ref[i] = total[BACK:].astype(bf16)
    for head in range(2):
        at = slice(head * TILE, (head + 1) * TILE)
        turned = near[:, at]
        r = lax.broadcasted_iota(jnp.int32, turned.shape, 0)
        bit = 1
        while bit < TILE:
            turned = jnp.where((r & bit) > 0, pltpu.roll(turned, TILE - bit, 1), turned)
            bit *= 2
        near_ref[0, :, at] = jnp.sum(turned, axis=0, keepdims=True)


def attention_specs(length):
    full = lambda p, *_: (0, 0)
    lanes = lambda off: (lambda p, *_: (0, p + off))
    return [
        pl.BlockSpec((length, TILE), lanes(0)),
        pl.BlockSpec((length, TILE), lanes(0)),
        pl.BlockSpec((length, TILE), lanes(PAIRS)),
        pl.BlockSpec((BACK, TILE), lanes(0)),
        pl.BlockSpec((BACK, TILE), lanes(PAIRS)),
        pl.BlockSpec((1, length), full),
        pl.BlockSpec((1, BACK + length), full),
        pl.BlockSpec((1, 4, 2 * TILE), lambda p, *_: (p, 0, 0)),
    ]


def attend(tiles, queries, kv, kv_back, query_docs, key_docs, bias_rows):
    length = queries.shape[0]
    width = HEADS * HEAD
    blocks = length // TILE
    return pl.pallas_call(
        fwd_kernel,
        grid_spec=pltpu.PrefetchScalarGridSpec(
            num_scalar_prefetch=1,
            grid=(PAIRS,),
            in_specs=attention_specs(length),
            out_specs=[
                pl.BlockSpec((length, TILE), lambda p, *_: (0, p)),
                pl.BlockSpec((1, blocks, 2 * TILE), lambda p, *_: (p, 0, 0)),
            ],
            scratch_shapes=[
                pltpu.VMEM((BACK + length, TILE), bf16),
                pltpu.VMEM((TILE, BACK + length), bf16),
                pltpu.VMEM((2, TILE, 2 * TILE), f32),
                pltpu.VMEM((blocks, SPAN * TILE, TILE), f32),
            ],
        ),
        out_shape=[
            jax.ShapeDtypeStruct((length, width), bf16),
            jax.ShapeDtypeStruct((PAIRS, blocks, 2 * TILE), f32),
        ],
        compiler_params=pltpu.CompilerParams(vmem_limit_bytes=32 * 2**20),
        cost_estimate=pl.CostEstimate(
            flops=4 * 2 * HEADS * length * BACK * 128, bytes_accessed=6 * 2**20,
            transcendentals=HEADS * length * BACK,
        ),
        name="attend",
    )(tiles, queries, kv, kv, kv_back, kv_back, query_docs, key_docs, bias_rows)


def attend_back(tiles, queries, kv, kv_back, query_docs, key_docs, bias_rows, out, out_grad, lse):
    length = queries.shape[0]
    width = HEADS * HEAD
    blocks = length // TILE
    own = pl.BlockSpec((length, TILE), lambda p, *_: (0, p))
    both = lambda n: pl.BlockSpec((2, n, TILE), lambda p, *_: (0, 0, p))
    return pl.pallas_call(
        bwd_kernel,
        grid_spec=pltpu.PrefetchScalarGridSpec(
            num_scalar_prefetch=1,
            grid=(PAIRS,),
            in_specs=attention_specs(length)
            + [own, own, pl.BlockSpec((1, blocks, 2 * TILE), lambda p, *_: (p, 0, 0))],
            out_specs=[own, both(length), both(BACK),
                       pl.BlockSpec((1, 1, 2 * TILE), lambda p, *_: (p, 0, 0))],
            scratch_shapes=[
                pltpu.VMEM((BACK + length, TILE), bf16),
                pltpu.VMEM((TILE, BACK + length), bf16),
                pltpu.VMEM((BACK + length, TILE), bf16),
                pltpu.VMEM((BACK + length, TILE), f32),
                pltpu.VMEM((BACK + length, TILE), f32),
                pltpu.VMEM((TILE, 2 * TILE), f32),
                pltpu.VMEM((2, TILE, 2 * TILE), f32),
                pltpu.VMEM((blocks, SPAN * TILE, TILE), f32),
            ],
        ),
        out_shape=[
            jax.ShapeDtypeStruct((length, width), bf16),
            jax.ShapeDtypeStruct((2, length, width), bf16),
            jax.ShapeDtypeStruct((2, BACK, width), bf16),
            jax.ShapeDtypeStruct((PAIRS, 1, 2 * TILE), f32),
        ],
        compiler_params=pltpu.CompilerParams(vmem_limit_bytes=32 * 2**20),
        cost_estimate=pl.CostEstimate(
            flops=10 * 2 * HEADS * length * BACK * 128, bytes_accessed=12 * 2**20,
            transcendentals=HEADS * length * BACK,
        ),
        name="attend_back",
    )(tiles, queries, kv, kv, kv_back, kv_back, query_docs, key_docs, bias_rows, out, out_grad, lse)


GELU_A = 0.7978845608028654
GELU_B = 0.044715


def expert_kernel(more, halves, split, capacity, room, chunk, ctx, x_ref, cot_ref, up_ref, down_ref, *refs):
    refs = list(refs)
    take = lambda n: [refs.pop(0) for _ in range(n)]
    if more:
        _, up_before, down_before = take(3)
    y_ref, back_ref = take(2)
    sums = take(4 if split else 2)
    y_sum, back_sum, x, result_grad, gate, act_all, pre_grad_all = take(7)
    rows, width = x.shape
    step = pl.program_id(0)
    pieces = 2 if halves else 1
    piece = width // pieces

    def columns(i):
        return pl.ds(pl.multiple_of((ctx[0] + i) % pieces * piece, TILE), piece)

    @pl.when(step == 0)
    def _():
        lane = lax.broadcasted_iota(jnp.int32, (1, TILE), 1)
        for e in range(rows // room):
            at = e * room
            for i in range(pieces):
                x[at : at + room, i * piece : (i + 1) * piece] = x_ref[e, :, columns(i)]
            line = x_ref[e, capacity : capacity + 1, : 2 * TILE].astype(f32)
            line = jnp.where(lane < capacity, line[:, :TILE] + line[:, TILE:], 0.0)
            column = jnp.broadcast_to(line, (TILE, TILE)).T[:room]
            gate[at : at + room, :] = column
            for c in range(0, width, TILE):
                result_grad[at : at + room, c : c + TILE] = (
                    cot_ref[e, :, c : c + TILE].astype(f32) * column
                ).astype(bf16)
        y_sum[...] = jnp.zeros_like(y_sum)
        back_sum[...] = jnp.zeros_like(back_sum)

    def part(i, carry):
        r = pl.ds(pl.multiple_of(i * chunk, chunk), chunk)
        pre = mm(x[r, :], up_ref[...], ((1,), (0,)))
        act_grad = mm(result_grad[r, :], down_ref[...], ((1,), (1,)))
        square = pre * pre
        half = 0.5 + 0.5 * jnp.tanh(pre * (GELU_A + (GELU_A * GELU_B) * square))
        act = (pre * half).astype(bf16)
        slope = 2.0 * GELU_A + (6.0 * GELU_A * GELU_B) * square
        pre_grad = (act_grad * (half * (1.0 + pre * (1.0 - half) * slope))).astype(bf16)
        act_all[r, :] = act
        pre_grad_all[r, :] = pre_grad
        y_sum[r, :] += mm(act, down_ref[...], ((1,), (0,)))
        back_sum[r, :] += mm(pre_grad, up_ref[...], ((1,), (1,)))
        return carry

    lax.fori_loop(0, rows // chunk, part, 0)

    def up_grad():
        grad = mm(x[...], pre_grad_all[...], ((0,), (0,)))
        return grad + up_before[...] if more else grad

    def down_grad():
        grad = mm(act_all[...], result_grad[...], ((0,), (0,)))
        return grad + down_before[...] if more else grad

    if split:
        mine, theirs, down_mine, down_theirs = sums
        early = step < pl.num_programs(0) // 2

        @pl.when(early)
        def _():
            down_mine[...] = down_grad()

        @pl.when(jnp.logical_not(early))
        def _():
            down_theirs[...] = down_grad().astype(bf16)

        grad = up_grad()
        mine[...] = grad[:piece]
        theirs[...] = grad[piece:].astype(bf16)
    else:
        sums[1][...] = down_grad()
        sums[0][...] = up_grad()

    @pl.when(step == pl.num_programs(0) - 1)
    def _():
        row = lax.broadcasted_iota(jnp.int32, (room, 1), 0)
        for e in range(rows // room):
            at = e * room
            dots = jnp.zeros((room, TILE), f32)
            for c in range(0, width, TILE):
                scaled = y_sum[at : at + room, c : c + TILE] * gate[at : at + room, :]
                y_ref[e, :, c : c + TILE] = scaled.astype(bf16)
                dots = dots + scaled * cot_ref[e, :, c : c + TILE].astype(f32)
            if room < TILE:
                dots = jnp.concatenate([dots, jnp.zeros((TILE - room, TILE), f32)], axis=0)
            line = jnp.sum(dots.T, axis=0, keepdims=True)
            high = line.astype(bf16).astype(f32)
            line = jnp.concatenate(
                [high, line - high, jnp.zeros((1, width - 2 * TILE), f32)], axis=1
            )
            for i in range(pieces):
                back_ref[e, :, columns(i)] = back_sum[
                    at : at + room, i * piece : (i + 1) * piece
                ].astype(bf16)
            back_ref[e] = jnp.where(row == capacity, line.astype(bf16), back_ref[e])


def run_experts(ctx, x, cot, batch, up, down, made, capacity, halves, split):
    sources, room, width = x.shape
    rows = sources * room
    hidden = up.shape[1]
    part = math.gcd(hidden // 2, 512)
    steps = hidden // part
    ahead = steps // 2 if halves else 0
    chunk = rows // 2 if rows % 32 == 0 else rows
    more = len(made) > 0
    once = pl.Buffered(1)
    columns = pl.BlockSpec((width, part), lambda t, c: (0, (t + c[0] * ahead) % steps))
    lines = pl.BlockSpec((part, width), lambda t, c: (t, 0))
    cot_rows = pl.BlockSpec((sources, room, width), lambda t, c: (0, batch, 0), pipeline_mode=once)
    whole = pl.BlockSpec((sources, room, width), lambda t, c: (0, 0, 0), pipeline_mode=once)
    if split:
        half = pl.BlockSpec((width // 2, part), lambda t, c: (0, (t + c[0] * ahead) % steps))
        sums = [
            (half, (width // 2, hidden), f32),
            (half, (width // 2, hidden), bf16),
            (pl.BlockSpec((part, width), lambda t, c: (jnp.minimum(t, ahead - 1), 0)),
             (hidden // 2, width), f32),
            (pl.BlockSpec((part, width), lambda t, c: (jnp.maximum(t - ahead, 0), 0)),
             (hidden // 2, width), bf16),
        ]
    else:
        sums = [(columns, up.shape, f32), (lines, down.shape, f32)]
    aliases = {5: 0} if split else {5: 0, 6: 2, 7: 3}
    return pl.pallas_call(
        functools.partial(expert_kernel, more, halves, split, capacity, room, chunk),
        grid_spec=pltpu.PrefetchScalarGridSpec(
            num_scalar_prefetch=1,
            grid=(steps,),
            in_specs=[whole, cot_rows, columns, lines]
            + ([pl.BlockSpec(memory_space=pl.ANY), columns, lines] if more else []),
            out_specs=[cot_rows, whole]
            + [spec for spec, _, _ in sums],
            scratch_shapes=[
                pltpu.VMEM((rows, width), f32),
                pltpu.VMEM((rows, width), f32),
                pltpu.VMEM((rows, width), bf16),
                pltpu.VMEM((rows, width), bf16),
                pltpu.VMEM((rows, TILE), f32),
                pltpu.VMEM((rows, part), bf16),
                pltpu.VMEM((rows, part), bf16),
            ]
        ),
        out_shape=[
            jax.ShapeDtypeStruct(cot.shape, bf16),
            jax.ShapeDtypeStruct((sources, room, width), bf16),
        ]
        + [jax.ShapeDtypeStruct(shape, kind) for _, shape, kind in sums],
        input_output_aliases=aliases if more else {},
        compiler_params=pltpu.CompilerParams(vmem_limit_bytes=60 * 2**20),
        cost_estimate=pl.CostEstimate(
            flops=18 * rows * width * hidden, bytes_accessed=40 * 2**20,
            transcendentals=rows * hidden,
        ),
        name="experts",
    )(ctx, x, cot, up, down, *made)


def bits_of(axis):
    return [1 << b for b in range(lax.axis_size(axis).bit_length() - 1)][::-1]


def power_of_two(axis):
    size = lax.axis_size(axis)
    return size & (size - 1) == 0


def swap(x, axis, bit):
    size = lax.axis_size(axis)
    return lax.ppermute(x, axis, [(i, i ^ bit) for i in range(size)])


def ordered(x, other, axis, bit):
    high = (lax.axis_index(axis) & bit) > 0
    return jnp.where(high, other, x), jnp.where(high, x, other)


def after(x, *others):
    return lax.optimization_barrier((x, *others))[0]


def gather_rows(left, right, early):
    if not (power_of_two("ctx") and power_of_two("exp")):
        return [lax.all_gather(x, ("ctx", "exp"), axis=0, tiled=True) for x in (left, right)]
    bits = bits_of("exp")
    last = bits[-2:]
    parts = [left, right]
    held = [x[None] for x in parts]
    for bit in bits[:-2]:
        got = [swap(h, "exp", bit) for h in held]
        held = [
            jnp.stack(ordered(h, g, "exp", bit), axis=1).reshape((-1,) + h.shape[1:])
            for h, g in zip(held, got)
        ]
    held = [after(h, early) for h in held]
    got = [swap(h, "exp", bit) for h, bit in zip(held, last)]
    held = [jnp.stack(ordered(h, g, "exp", bit), axis=1) for h, g, bit in zip(held, got, last)]
    got = [swap(h, "exp", bit) for h, bit in zip(held, last[::-1])]
    held = [
        jnp.stack(ordered(h, g, "exp", bit), axis=at)
        for h, g, bit, at in zip(held, got, last[::-1], (2, 1))
    ]
    held = [h.reshape(-1, h.shape[-1]) for h in held]
    for bit in bits_of("ctx"):
        got = [swap(h, "ctx", bit) for h in held]
        held = [
            jnp.stack(ordered(h, g, "ctx", bit), axis=0).reshape(-1, h.shape[-1])
            for h, g in zip(held, got)
        ]
    return held


def pair_rows(x):
    if lax.axis_size("ctx") != 2:
        return lax.all_gather(x, "ctx", axis=0, tiled=True)
    return jnp.concatenate([x, swap(x, "ctx", 1)], axis=0)


def halve(x, axis, bit, dim):
    side = ((lax.axis_index(axis) & bit) > 0).astype(jnp.int32)
    mine = lax.dynamic_index_in_dim(x, side, dim, keepdims=False)
    theirs = lax.dynamic_index_in_dim(x, 1 - side, dim, keepdims=False)
    return mine + swap(theirs.astype(bf16), axis, bit).astype(f32)


def scatter_sum(grads, width, late):
    if not (power_of_two("exp") and lax.axis_size("ctx") == 2 and lax.axis_size("exp") > 3):
        whole = grads(lambda x, axis: x)
        sums = [
            lax.psum_scatter(x, ("ctx", "exp"), scatter_dimension=0, tiled=True) for x in whole
        ]
        return [*sums, sums[0]]
    me = lax.axis_index("ctx")
    part = width // 2
    theirs = grads(lambda x, axis: lax.dynamic_slice_in_dim(x, (1 - me) * part, part, axis))
    got = [swap(x.astype(bf16), "ctx", 1) for x in theirs]
    mine = grads(lambda x, axis: lax.dynamic_slice_in_dim(x, me * part, part, axis))
    begun = got[1]
    bits = bits_of("exp")
    held = [after(m + g.astype(f32), late) for m, g in zip(mine, got)]
    held = [h.reshape((-1, 2, 2, h.shape[0] // lax.axis_size("exp"), h.shape[1])) for h in held]
    high, low = bits[-2:]
    held = [halve(held[0], "exp", high, 1), halve(held[1], "exp", low, 2)]
    held = [halve(held[0], "exp", low, 1), halve(held[1], "exp", high, 1)]
    for bit in bits[:-2][::-1]:
        held = [halve(h.reshape((-1, 2) + h.shape[1:]), "exp", bit, 1) for h in held]
    return [*(h.reshape(h.shape[-2:]) for h in held), begun]


def total_of(x):
    if not (power_of_two("ctx") and power_of_two("exp")):
        return lax.psum(x, ("ctx", "exp"))
    for axis in ("ctx", "exp"):
        for bit in bits_of(axis):
            x = x + swap(x, axis, bit)
    return x


def shards(
    inputs,
    cotangent,
    doc_ids,
    routes,
    query_key_value_weight,
    output_projection_weight,
    router,
    attn_gain,
    expert_gain,
    position_bias,
    expert_up,
    expert_down,
):
    batches = inputs.shape[0]
    length = inputs.shape[2]
    width = inputs.shape[3]
    top = routes.shape[3]
    ways = lax.axis_size("ctx")
    experts = lax.axis_size("exp")
    capacity = max(2, top * length * 10 // (7 * experts))
    room = (capacity + 1 + 15) // 16 * 16
    slots = experts * room
    seq_len = doc_ids.shape[2]
    buckets = position_bias.shape[1]
    me = lax.axis_index("ctx")

    expert_ids = jnp.arange(experts, dtype=jnp.int32)
    slot_rows = jnp.arange(slots, dtype=jnp.int32)
    earlier = jnp.tril(jnp.ones((length, length), bf16), -1)
    hots, slot_of, holds, spreads = [], [], [], []
    for b in range(batches):
        route_ids = routes[b, 0]
        hot = route_ids[:, :, None] == expert_ids[None, None, :]
        used = jnp.any(hot, axis=1)
        rank = mm(earlier, used.astype(bf16), ((1,), (0,))).astype(jnp.int32)
        slot = jnp.sum(jnp.where(hot, rank[:, None, :], 0), axis=2) + route_ids * room
        hold = [slot[None, :, k] == slot_rows[:, None] for k in range(top)]
        hots.append(hot)
        slot_of.append(slot)
        holds.append(hold)
        spreads.append(functools.reduce(jnp.logical_or, hold).astype(bf16))

    def dispatch(b, rows):
        sent = mm(spreads[b], rows, ((1,), (0,))).astype(bf16)
        return sent.reshape(experts, room, width)

    def cross(x):
        return lax.all_to_all(x, "exp", split_axis=0, concat_axis=0, tiled=True)

    cots = [cotangent[b, 0] for b in range(batches)]
    cot_sent = jnp.concatenate([dispatch(b, cots[b]) for b in range(batches)], axis=1)

    pad = -(experts + 2) % 128
    left, right = gather_rows(
        jnp.concatenate([query_key_value_weight[:, :width], output_projection_weight], axis=1),
        jnp.concatenate(
            [
                query_key_value_weight[:, width:],
                router,
                attn_gain[:, None],
                expert_gain[:, None],
                jnp.zeros((router.shape[0], pad), bf16),
            ],
            axis=1,
        ),
        cot_sent,
    )
    query_weight = left[:, :width]
    proj_weight = left[:, width:]
    kv_weight = right[:, : 2 * width]
    router_all = right[:, 2 * width : 2 * width + experts]
    gains = right[:, 2 * width + experts : 2 * width + experts + 2].astype(f32)
    attn_scale = gains[:, 0]
    expert_scale = gains[:, 1]
    expert_weights = [pair_rows(w[0]) for w in (expert_up, expert_down)]

    distance = jnp.arange(2 * TILE, dtype=jnp.int32)
    hot_bucket = (
        bucket_of(distance)[None, :] == jnp.arange(buckets, dtype=jnp.int32)[:, None]
    ).astype(f32)
    by_distance = jnp.sum(
        position_bias.astype(f32)[:, :, None] * hot_bucket[None], axis=1
    ) - position_bias.astype(f32)[:, buckets - 1 :]
    close = jnp.where(distance < TILE, by_distance, MASKED)
    beside = jnp.roll(by_distance, -TILE, axis=1)
    bias_rows = jnp.stack([close, beside], axis=1).reshape(PAIRS, 4, 2 * TILE)

    def norm_stats(values):
        return lax.rsqrt(jnp.mean(values * values, axis=-1, keepdims=True) + epsilon)

    state = []
    for b in range(batches):
        rows = inputs[b, 0].astype(f32)
        inv_one = norm_stats(rows)
        normed = (rows * inv_one * attn_scale).astype(bf16)
        kv = mm(normed, kv_weight, ((1,), (0,))).astype(bf16)
        queries = mm(normed, query_weight, ((1,), (0,))).astype(bf16)
        docs = doc_ids[b, 0].astype(f32)
        padded = jnp.concatenate([jnp.full((BACK,), -1.0, f32), docs])
        key_docs = lax.dynamic_slice_in_dim(padded, me * length, BACK + length)
        query_docs = key_docs[BACK:]
        if ways == 2:
            kv_back = lax.ppermute(kv, "ctx", [(0, 1)])
        else:
            every = lax.all_gather(kv, "ctx", axis=0, tiled=True)
            every = jnp.concatenate([jnp.zeros((BACK, 2 * width), bf16), every], axis=0)
            kv_back = lax.dynamic_slice_in_dim(every, me * length, BACK, 0)
        firsts = query_docs[::TILE]
        start = jnp.sum((key_docs[None, :] < firsts[:, None]).astype(jnp.int32), axis=1)
        tiles = jnp.arange(length // TILE, dtype=jnp.int32) + SPAN - start // TILE
        tiles = jnp.clip(tiles, 1, SPAN)
        view = (tiles, queries, kv, kv_back, query_docs[None], key_docs[None], bias_rows)
        state.append(dict(rows=rows, inv_one=inv_one, normed=normed, view=view))

    cot_here = cross(after(cot_sent, left, right))
    sent = ()
    for b, s in enumerate(state):
        s["view"] = (after(s["view"][0], *sent),) + s["view"][1:]
        attended, lse = attend(*s["view"])
        hidden = s["rows"] + mm(attended, proj_weight, ((1,), (0,)))
        inv_two = norm_stats(hidden)
        shared = (hidden * inv_two * expert_scale).astype(bf16)
        logits = mm(shared, router_all, ((1,), (0,)))
        hot = hots[b]
        chosen = jnp.sum(jnp.where(hot, logits[:, None, :], 0.0), axis=2)
        gate_exp = jnp.exp(chosen - jnp.max(chosen, axis=1, keepdims=True))
        gates = gate_exp / jnp.sum(gate_exp, axis=1, keepdims=True)
        gate_slots = sum(
            jnp.sum(jnp.where(holds[b][k], gates[None, :, k], 0.0), axis=1) for k in range(top)
        ).reshape(experts, 1, room)
        gate_slots = jnp.pad(gate_slots, ((0, 0), (0, 0), (0, TILE - room)))
        gate_high = gate_slots.astype(bf16)
        gate_low = (gate_slots - gate_high.astype(f32)).astype(bf16)
        gate_row = jnp.concatenate(
            [gate_high, gate_low, jnp.zeros((experts, 1, width - 2 * TILE), bf16)], axis=2
        )
        at_gate = lax.broadcasted_iota(jnp.int32, (1, room, 1), 1) == capacity
        sent = (jnp.where(at_gate, gate_row, dispatch(b, shared)),)
        s.update(attended=attended, lse=lse, hidden=hidden, inv_two=inv_two, shared=shared,
                 gates=gates, sent=sent[0])

    made = ()
    last = (cot_here, *(s["sent"] for s in state))
    for s in state:
        s["here"] = cross(after(s["sent"], *last))
        last = (s["here"],)
    for b, s in enumerate(state):
        y, back, *sums = run_experts(
            me[None].astype(jnp.int32), s["here"], cot_here, b, *expert_weights, made, capacity,
            ways == 2, ways == 2 and b == batches - 1,
        )
        made = (y, *sums)
        s["back"] = cross(after(back, *last))
        last = (s["back"],)
    results = cross(after(y, *last))
    if ways == 2:
        up_share, down_share = (
            (mine + swap(theirs, "ctx", 1).astype(f32))[None]
            for mine, theirs in zip(sums[::2], sums[1::2])
        )
    else:
        up_share, down_share = (
            lax.psum_scatter(g.astype(bf16), "ctx", scatter_dimension=0, tiled=True).astype(f32)[None]
            for g in sums
        )

    input_grads = []
    parts = []
    picks = []
    before = ()
    for b, s in enumerate(state):
        upstream = cots[b].astype(f32)
        packet = after(s["back"], *before)
        dots = packet[:, capacity, : 2 * TILE].astype(f32)
        dots = (dots[:, :room] + dots[:, TILE : TILE + room]).reshape(1, slots)
        slot = slot_of[b]
        pick = [slot[:, k : k + 1] == slot_rows[None, :] for k in range(top)]
        picks.append(functools.reduce(jnp.logical_or, pick).astype(bf16))
        scaled = jnp.stack([jnp.sum(jnp.where(p, dots, 0.0), axis=1) for p in pick], axis=1)
        chosen_grad = scaled - s["gates"] * jnp.sum(scaled, axis=1, keepdims=True)
        logit_grad = jnp.sum(jnp.where(hots[b], chosen_grad[:, :, None], 0.0), axis=1).astype(bf16)
        shared_grad = mm(picks[b], packet.reshape(slots, width), ((1,), (0,)))
        shared_grad = shared_grad + mm(logit_grad, router_all, ((1,), (1,)))
        unit = s["hidden"] * s["inv_two"]
        grad_expert = jnp.sum(shared_grad * unit, axis=0)
        inner = shared_grad * expert_scale
        hidden_grad = upstream + s["inv_two"] * (
            inner - unit * jnp.mean(inner * unit, axis=1, keepdims=True)
        )
        branch_grad = hidden_grad.astype(bf16)
        attended_grad = mm(branch_grad, proj_weight, ((1,), (1,))).astype(bf16)
        dq, own, back, near = attend_back(*s["view"], s["attended"], attended_grad, s["lse"])
        before = (dq,)
        if ways == 2:
            got = lax.ppermute(back, "ctx", [(1, 0)])
        else:
            every = jnp.zeros((2, BACK + seq_len, width), bf16)
            every = lax.dynamic_update_slice_in_dim(every, back, me * length, 1)
            got = lax.psum_scatter(every[:, BACK:], "ctx", scatter_dimension=1, tiled=True)
        both = (own.astype(f32) + got.astype(f32)).astype(bf16)
        dkv = jnp.concatenate([both[0], both[1]], axis=1)
        normed = s["normed"]
        normed_grad = mm(dq, query_weight, ((1,), (1,))) + mm(dkv, kv_weight, ((1,), (1,)))
        unit = s["rows"] * s["inv_one"]
        grad_attn = jnp.sum(normed_grad * unit, axis=0)
        inner = normed_grad * attn_scale
        input_part = s["inv_one"] * (inner - unit * jnp.mean(inner * unit, axis=1, keepdims=True))
        input_grads.append((hidden_grad + input_part).astype(bf16))
        parts.append((near, grad_attn, grad_expert))
        s.update(dq=dq, dkv=dkv, branch_grad=branch_grad, logit_grad=logit_grad)

    outputs = []
    for b, s in enumerate(state):
        mine = results[:, b * room : (b + 1) * room].reshape(slots, width)
        outputs.append((s["hidden"] + mm(picks[b], mine, ((1,), (0,)))).astype(bf16))

    near, grad_attn, grad_expert = (functools.reduce(jnp.add, p) for p in zip(*parts))

    def weight_grads(rows):
        def total(left, right):
            return functools.reduce(
                jnp.add, [mm(rows(s[left], 1), s[right], ((0,), (0,))) for s in state]
            )

        small = total("shared", "logit_grad")
        return (
            jnp.concatenate([total("normed", "dq"), total("attended", "branch_grad")], axis=1),
            jnp.concatenate(
                [
                    total("normed", "dkv"),
                    small,
                    rows(grad_attn, 0)[:, None],
                    rows(grad_expert, 0)[:, None],
                    jnp.zeros((small.shape[0], pad), f32),
                ],
                axis=1,
            ),
        )

    left, right, begun = scatter_sum(weight_grads, width, results)
    hot_near = jnp.where(
        jnp.arange(buckets)[:, None] < buckets - 1, hot_bucket[:, :TILE], 0.0
    )
    grad_bias = jnp.sum(near.reshape(HEADS, 1, TILE) * hot_near[None], axis=2)
    far = jnp.where(jnp.arange(buckets) == buckets - 1, 1.0, 0.0)
    grad_bias = grad_bias - jnp.sum(grad_bias, axis=1, keepdims=True) * far
    bias_total = total_of(after(grad_bias, begun))
    return (
        jnp.stack(outputs)[:, None],
        jnp.stack(input_grads)[:, None],
        jnp.concatenate([left[:, :width], right[:, : 2 * width]], axis=1),
        left[:, width:],
        right[:, 2 * width : 2 * width + experts],
        right[:, 2 * width + experts],
        right[:, 2 * width + experts + 1],
        bias_total,
        up_share,
        down_share,
    )


def solution(mesh):
    placed = (
        P(None, "exp", "ctx", None),
        P(None, "exp", "ctx", None),
        P(None, "exp", None),
        P(None, "exp", "ctx", None),
        P(("ctx", "exp"), None),
        P(("ctx", "exp"), None),
        P(("ctx", "exp"), None),
        P(("ctx", "exp")),
        P(("ctx", "exp")),
        P(),
        P("exp", "ctx", None),
        P("exp", "ctx", None),
    )
    return jax.shard_map(
        shards,
        mesh=mesh,
        in_specs=placed,
        out_specs=(
            P(None, "exp", "ctx", None),
            P(None, "exp", "ctx", None),
            P(("ctx", "exp"), None),
            P(("ctx", "exp"), None),
            P(("ctx", "exp"), None),
            P(("ctx", "exp")),
            P(("ctx", "exp")),
            P(),
            P("exp", "ctx", None),
            P("exp", "ctx", None),
        ),
        check_vma=False,
    )
```

```python
import functools
import math

import jax
import jax.numpy as jnp
from jax import lax
from jax.experimental import pallas as pl
from jax.experimental.pallas import tpu as pltpu
from jax.sharding import PartitionSpec as P

HEADS = 12
HEAD = 64
PAIRS = HEADS // 2
TILE = 128
BACK = 512
SPAN = BACK // TILE + 1
MASKED = -1000000000.0

epsilon = 1e-06
thresholds = (19, 21, 24, 27, 31, 35, 40, 46, 52, 59, 67, 77, 87, 99, 113)
bf16 = jnp.bfloat16
f32 = jnp.float32


def bucket_of(distance):
    distance = jnp.maximum(distance, 0)
    beyond = jnp.zeros_like(distance)
    for threshold in thresholds:
        beyond = beyond + (distance >= threshold).astype(jnp.int32)
    return jnp.where(distance < 16, distance, 16 + beyond)


def mm(a, b, dims):
    return lax.dot_general(a, b, (dims, ((), ())), preferred_element_type=f32)


def stack_heads(rows):
    lane = lax.broadcasted_iota(jnp.int32, rows.shape, 1)
    zero = jnp.zeros_like(rows)
    return jnp.concatenate(
        [jnp.where(lane < HEAD, rows, zero), jnp.where(lane >= HEAD, rows, zero)], axis=0
    )


def fold_heads(wide):
    return jnp.concatenate([wide[:HEAD, :TILE], wide[HEAD:, TILE:]], axis=0)


def fill_mask(mask, qd_ref, kd_ref):
    for qi in range(qd_ref.shape[1] // TILE):
        docs_row = qd_ref[:, qi * TILE : (qi + 1) * TILE]
        for j in range(SPAN):
            kt = (qi + j) * TILE
            column = jnp.broadcast_to(kd_ref[:, kt : kt + TILE], (TILE, TILE)).T
            mask[qi, j * TILE : (j + 1) * TILE, :] = jnp.where(
                column == docs_row, 0.0, MASKED
            ).astype(f32)


def fill_bias(bias, bv_ref):
    for head in range(2):
        for d in range(2):
            row = jnp.broadcast_to(bv_ref[0, 2 * head + d : 2 * head + d + 1, :], (TILE, 2 * TILE))
            rolled = pltpu.roll(row, 0, 1, stride=1, stride_axis=0)
            bias[d, :, head * TILE : (head + 1) * TILE] = rolled[:, :TILE]


def masked_scores(scores, mask, bias, qi, tiles):
    parts = []
    for j in range(tiles):
        d = tiles - 1 - j
        off = (SPAN - tiles + j) * TILE
        m = mask[qi, off : off + TILE, :]
        x = scores[j * TILE : (j + 1) * TILE] + jnp.concatenate([m, m], axis=1)
        if d < 2:
            x = x + bias[d]
        parts.append(x)
    return parts


def fwd_kernel(tiles, q_ref, k_ref, v_ref, kp_ref, vp_ref, qd_ref, kd_ref, bv_ref, o_ref, lse_ref,
               kwin, vwin_t, bias, mask):
    @pl.when(pl.program_id(0) == 0)
    def _():
        fill_mask(mask, qd_ref, kd_ref)

    fill_bias(bias, bv_ref)
    kwin[:BACK] = kp_ref[...]
    kwin[BACK:] = k_ref[...]
    for t in range(BACK // TILE):
        vwin_t[:, t * TILE : (t + 1) * TILE] = vp_ref[t * TILE : (t + 1) * TILE, :].T
    for t in range(q_ref.shape[0] // TILE):
        at = BACK + t * TILE
        vwin_t[:, at : at + TILE] = v_ref[t * TILE : (t + 1) * TILE, :].T

    def step(qi, carry):
        q0 = pl.multiple_of(qi * TILE, TILE)
        q2 = stack_heads(q_ref[pl.ds(q0, TILE), :] * 0.125)

        def branch(count):
            def go():
                lo = pl.multiple_of((qi + SPAN - count) * TILE, TILE)
                keys = kwin[pl.ds(lo, count * TILE), :]
                parts = masked_scores(mm(keys, q2, ((1,), (1,))), mask, bias, qi, count)
                top = functools.reduce(jnp.maximum, parts)
                top = jnp.max(top, axis=0, keepdims=True)
                probs = [jnp.exp(x - top) for x in parts]
                total = jnp.sum(functools.reduce(jnp.add, probs), axis=0, keepdims=True)
                low = jnp.concatenate([p.astype(bf16) for p in probs], axis=0)
                out = fold_heads(mm(vwin_t[:, pl.ds(lo, count * TILE)], low, ((1,), (0,))))
                inv = 1.0 / total
                row = lax.broadcasted_iota(jnp.int32, (TILE, TILE), 0)
                out = out * jnp.where(row < HEAD, inv[:, :TILE], inv[:, TILE:])
                o_ref[pl.ds(q0, TILE), :] = out.T.astype(bf16)
                lse_ref[0, pl.ds(qi, 1), :] = top + jnp.log(total)
                return 0

            return go

        lax.switch(tiles[qi] - 1, [branch(c) for c in range(1, SPAN + 1)])
        return carry

    lax.fori_loop(0, q_ref.shape[0] // TILE, step, 0)


def bwd_kernel(tiles, q_ref, k_ref, v_ref, kp_ref, vp_ref, qd_ref, kd_ref, bv_ref, o_ref, do_ref,
               lse_ref, dq_ref, own_ref, back_ref, near_ref,
               kwin, kwin_t, vwin, dk, dv, near, bias, mask):
    @pl.when(pl.program_id(0) == 0)
    def _():
        fill_mask(mask, qd_ref, kd_ref)

    fill_bias(bias, bv_ref)
    kwin[:BACK] = kp_ref[...]
    kwin[BACK:] = k_ref[...]
    vwin[:BACK] = vp_ref[...]
    vwin[BACK:] = v_ref[...]
    for t in range(kwin.shape[0] // TILE):
        kwin_t[:, t * TILE : (t + 1) * TILE] = kwin[t * TILE : (t + 1) * TILE, :].T
    dk[...] = jnp.zeros_like(dk)
    dv[...] = jnp.zeros_like(dv)
    near[...] = jnp.zeros_like(near)

    def step(qi, carry):
        q0 = pl.multiple_of(qi * TILE, TILE)
        q2 = stack_heads(q_ref[pl.ds(q0, TILE), :] * 0.125)
        do = do_ref[pl.ds(q0, TILE), :]
        do2 = stack_heads(do)
        lse = lse_ref[0, pl.ds(qi, 1), :]
        prod = (do.astype(f32) * o_ref[pl.ds(q0, TILE), :].astype(f32)).T
        delta = jnp.concatenate(
            [jnp.sum(prod[:HEAD], axis=0, keepdims=True),
             jnp.sum(prod[HEAD:], axis=0, keepdims=True)],
            axis=1,
        )

        def branch(count):
            def go():
                lo = pl.multiple_of((qi + SPAN - count) * TILE, TILE)
                rows = pl.ds(lo, count * TILE)
                parts = masked_scores(
                    mm(kwin[rows, :], q2, ((1,), (1,))), mask, bias, qi, count
                )
                prob_grad = mm(vwin[rows, :], do2, ((1,), (1,)))
                lows = []
                grads = []
                for j in range(count):
                    prob = jnp.exp(parts[j] - lse)
                    grad = prob * (prob_grad[j * TILE : (j + 1) * TILE] - delta)
                    if j == count - 1:
                        near[...] += grad
                    elif j == count - 2:
                        r = lax.broadcasted_iota(jnp.int32, grad.shape, 0)
                        c = lax.broadcasted_iota(jnp.int32, grad.shape, 1)
                        c = jnp.where(c >= TILE, c - TILE, c)
                        near[...] += jnp.where(c < r, grad, 0.0)
                    lows.append(prob.astype(bf16))
                    grads.append(grad.astype(bf16))
                low = jnp.concatenate(lows, axis=0)
                score_grad = jnp.concatenate(grads, axis=0)
                dk[rows, :] += mm(score_grad, q2, ((1,), (0,)))
                dv[rows, :] += mm(low, do2, ((1,), (0,)))
                dq = fold_heads(mm(kwin_t[:, rows], score_grad, ((1,), (0,))))
                dq_ref[pl.ds(q0, TILE), :] = (dq.T * 0.125).astype(bf16)
                return 0

            return go

        lax.switch(tiles[qi] - 1, [branch(c) for c in range(1, SPAN + 1)])
        return carry

    lax.fori_loop(0, q_ref.shape[0] // TILE, step, 0)
    for i, total in enumerate((dk, dv)):
        back_ref[i] = total[:BACK].astype(bf16)
        own_ref[i] = total[BACK:].astype(bf16)
    for head in range(2):
        at = slice(head * TILE, (head + 1) * TILE)
        turned = near[:, at]
        r = lax.broadcasted_iota(jnp.int32, turned.shape, 0)
        bit = 1
        while bit < TILE:
            turned = jnp.where((r & bit) > 0, pltpu.roll(turned, TILE - bit, 1), turned)
            bit *= 2
        near_ref[0, :, at] = jnp.sum(turned, axis=0, keepdims=True)


def attention_specs(length):
    full = lambda p, *_: (0, 0)
    lanes = lambda off: (lambda p, *_: (0, p + off))
    return [
        pl.BlockSpec((length, TILE), lanes(0)),
        pl.BlockSpec((length, TILE), lanes(0)),
        pl.BlockSpec((length, TILE), lanes(PAIRS)),
        pl.BlockSpec((BACK, TILE), lanes(0)),
        pl.BlockSpec((BACK, TILE), lanes(PAIRS)),
        pl.BlockSpec((1, length), full),
        pl.BlockSpec((1, BACK + length), full),
        pl.BlockSpec((1, 4, 2 * TILE), lambda p, *_: (p, 0, 0)),
    ]


def attend(tiles, queries, kv, kv_back, query_docs, key_docs, bias_rows):
    length = queries.shape[0]
    width = HEADS * HEAD
    blocks = length // TILE
    return pl.pallas_call(
        fwd_kernel,
        grid_spec=pltpu.PrefetchScalarGridSpec(
            num_scalar_prefetch=1,
            grid=(PAIRS,),
            in_specs=attention_specs(length),
            out_specs=[
                pl.BlockSpec((length, TILE), lambda p, *_: (0, p)),
                pl.BlockSpec((1, blocks, 2 * TILE), lambda p, *_: (p, 0, 0)),
            ],
            scratch_shapes=[
                pltpu.VMEM((BACK + length, TILE), bf16),
                pltpu.VMEM((TILE, BACK + length), bf16),
                pltpu.VMEM((2, TILE, 2 * TILE), f32),
                pltpu.VMEM((blocks, SPAN * TILE, TILE), f32),
            ],
        ),
        out_shape=[
            jax.ShapeDtypeStruct((length, width), bf16),
            jax.ShapeDtypeStruct((PAIRS, blocks, 2 * TILE), f32),
        ],
        compiler_params=pltpu.CompilerParams(vmem_limit_bytes=32 * 2**20),
        cost_estimate=pl.CostEstimate(
            flops=4 * 2 * HEADS * length * BACK * 128, bytes_accessed=6 * 2**20,
            transcendentals=HEADS * length * BACK,
        ),
        name="attend",
    )(tiles, queries, kv, kv, kv_back, kv_back, query_docs, key_docs, bias_rows)


def attend_back(tiles, queries, kv, kv_back, query_docs, key_docs, bias_rows, out, out_grad, lse):
    length = queries.shape[0]
    width = HEADS * HEAD
    blocks = length // TILE
    own = pl.BlockSpec((length, TILE), lambda p, *_: (0, p))
    both = lambda n: pl.BlockSpec((2, n, TILE), lambda p, *_: (0, 0, p))
    return pl.pallas_call(
        bwd_kernel,
        grid_spec=pltpu.PrefetchScalarGridSpec(
            num_scalar_prefetch=1,
            grid=(PAIRS,),
            in_specs=attention_specs(length)
            + [own, own, pl.BlockSpec((1, blocks, 2 * TILE), lambda p, *_: (p, 0, 0))],
            out_specs=[own, both(length), both(BACK),
                       pl.BlockSpec((1, 1, 2 * TILE), lambda p, *_: (p, 0, 0))],
            scratch_shapes=[
                pltpu.VMEM((BACK + length, TILE), bf16),
                pltpu.VMEM((TILE, BACK + length), bf16),
                pltpu.VMEM((BACK + length, TILE), bf16),
                pltpu.VMEM((BACK + length, TILE), f32),
                pltpu.VMEM((BACK + length, TILE), f32),
                pltpu.VMEM((TILE, 2 * TILE), f32),
                pltpu.VMEM((2, TILE, 2 * TILE), f32),
                pltpu.VMEM((blocks, SPAN * TILE, TILE), f32),
            ],
        ),
        out_shape=[
            jax.ShapeDtypeStruct((length, width), bf16),
            jax.ShapeDtypeStruct((2, length, width), bf16),
            jax.ShapeDtypeStruct((2, BACK, width), bf16),
            jax.ShapeDtypeStruct((PAIRS, 1, 2 * TILE), f32),
        ],
        compiler_params=pltpu.CompilerParams(vmem_limit_bytes=32 * 2**20),
        cost_estimate=pl.CostEstimate(
            flops=2**20, bytes_accessed=2**20, transcendentals=0,
        ),
        name="attend_back",
    )(tiles, queries, kv, kv, kv_back, kv_back, query_docs, key_docs, bias_rows, out, out_grad, lse)


GELU_A = 0.7978845608028654
GELU_B = 0.044715


def expert_kernel(more, halves, split, capacity, room, chunk, ctx, x_ref, cot_ref, up_ref, down_ref, *refs):
    refs = list(refs)
    take = lambda n: [refs.pop(0) for _ in range(n)]
    if more:
        _, up_before, down_before = take(3)
    y_ref, back_ref = take(2)
    sums = take(4 if split else 2)
    y_sum, back_sum, x, result_grad, gate, act_all, pre_grad_all = take(7)
    rows, width = x.shape
    step = pl.program_id(0)
    pieces = 2 if halves else 1
    piece = width // pieces

    def columns(i):
        return pl.ds(pl.multiple_of((ctx[0] + i) % pieces * piece, TILE), piece)

    @pl.when(step == 0)
    def _():
        lane = lax.broadcasted_iota(jnp.int32, (1, TILE), 1)
        for e in range(rows // room):
            at = e * room
            for i in range(pieces):
                x[at : at + room, i * piece : (i + 1) * piece] = x_ref[e, :, columns(i)]
            line = x_ref[e, capacity : capacity + 1, : 2 * TILE].astype(f32)
            line = jnp.where(lane < capacity, line[:, :TILE] + line[:, TILE:], 0.0)
            column = jnp.broadcast_to(line, (TILE, TILE)).T[:room]
            gate[at : at + room, :] = column
            for c in range(0, width, TILE):
                result_grad[at : at + room, c : c + TILE] = (
                    cot_ref[e, :, c : c + TILE].astype(f32) * column
                ).astype(bf16)
        y_sum[...] = jnp.zeros_like(y_sum)
        back_sum[...] = jnp.zeros_like(back_sum)

    def part(i, carry):
        r = pl.ds(pl.multiple_of(i * chunk, chunk), chunk)
        pre = mm(x[r, :], up_ref[...], ((1,), (0,)))
        act_grad = mm(result_grad[r, :], down_ref[...], ((1,), (1,)))
        square = pre * pre
        half = 0.5 + 0.5 * jnp.tanh(pre * (GELU_A + (GELU_A * GELU_B) * square))
        act = (pre * half).astype(bf16)
        slope = 2.0 * GELU_A + (6.0 * GELU_A * GELU_B) * square
        pre_grad = (act_grad * (half * (1.0 + pre * (1.0 - half) * slope))).astype(bf16)
        act_all[r, :] = act
        pre_grad_all[r, :] = pre_grad
        y_sum[r, :] += mm(act, down_ref[...], ((1,), (0,)))
        back_sum[r, :] += mm(pre_grad, up_ref[...], ((1,), (1,)))
        return carry

    lax.fori_loop(0, rows // chunk, part, 0)

    def up_grad():
        grad = mm(x[...], pre_grad_all[...], ((0,), (0,)))
        return grad + up_before[...] if more else grad

    def down_grad():
        grad = mm(act_all[...], result_grad[...], ((0,), (0,)))
        return grad + down_before[...] if more else grad

    if split:
        mine, theirs, down_mine, down_theirs = sums
        early = step < pl.num_programs(0) // 2

        @pl.when(early)
        def _():
            down_mine[...] = down_grad()

        @pl.when(jnp.logical_not(early))
        def _():
            down_theirs[...] = down_grad().astype(bf16)

        grad = up_grad()
        mine[...] = grad[:piece]
        theirs[...] = grad[piece:].astype(bf16)
    else:
        sums[1][...] = down_grad()
        sums[0][...] = up_grad()

    @pl.when(step == pl.num_programs(0) - 1)
    def _():
        row = lax.broadcasted_iota(jnp.int32, (room, 1), 0)
        for e in range(rows // room):
            at = e * room
            dots = jnp.zeros((room, TILE), f32)
            for c in range(0, width, TILE):
                scaled = y_sum[at : at + room, c : c + TILE] * gate[at : at + room, :]
                y_ref[e, :, c : c + TILE] = scaled.astype(bf16)
                dots = dots + scaled * cot_ref[e, :, c : c + TILE].astype(f32)
            if room < TILE:
                dots = jnp.concatenate([dots, jnp.zeros((TILE - room, TILE), f32)], axis=0)
            line = jnp.sum(dots.T, axis=0, keepdims=True)
            high = line.astype(bf16).astype(f32)
            line = jnp.concatenate(
                [high, line - high, jnp.zeros((1, width - 2 * TILE), f32)], axis=1
            )
            for i in range(pieces):
                back_ref[e, :, columns(i)] = back_sum[
                    at : at + room, i * piece : (i + 1) * piece
                ].astype(bf16)
            back_ref[e] = jnp.where(row == capacity, line.astype(bf16), back_ref[e])


def run_experts(ctx, x, cot, batch, up, down, made, capacity, halves, split):
    sources, room, width = x.shape
    rows = sources * room
    hidden = up.shape[1]
    part = math.gcd(hidden // 2, 512)
    steps = hidden // part
    ahead = steps // 2 if halves else 0
    chunk = rows // 2 if rows % 32 == 0 else rows
    more = len(made) > 0
    once = pl.Buffered(1)
    columns = pl.BlockSpec((width, part), lambda t, c: (0, (t + c[0] * ahead) % steps))
    lines = pl.BlockSpec((part, width), lambda t, c: (t, 0))
    cot_rows = pl.BlockSpec((sources, room, width), lambda t, c: (0, batch, 0), pipeline_mode=once)
    whole = pl.BlockSpec((sources, room, width), lambda t, c: (0, 0, 0), pipeline_mode=once)
    if split:
        half = pl.BlockSpec((width // 2, part), lambda t, c: (0, (t + c[0] * ahead) % steps))
        sums = [
            (half, (width // 2, hidden), f32),
            (half, (width // 2, hidden), bf16),
            (pl.BlockSpec((part, width), lambda t, c: (jnp.minimum(t, ahead - 1), 0)),
             (hidden // 2, width), f32),
            (pl.BlockSpec((part, width), lambda t, c: (jnp.maximum(t - ahead, 0), 0)),
             (hidden // 2, width), bf16),
        ]
    else:
        sums = [(columns, up.shape, f32), (lines, down.shape, f32)]
    aliases = {5: 0} if split else {5: 0, 6: 2, 7: 3}
    return pl.pallas_call(
        functools.partial(expert_kernel, more, halves, split, capacity, room, chunk),
        grid_spec=pltpu.PrefetchScalarGridSpec(
            num_scalar_prefetch=1,
            grid=(steps,),
            in_specs=[whole, cot_rows, columns, lines]
            + ([pl.BlockSpec(memory_space=pl.ANY), columns, lines] if more else []),
            out_specs=[cot_rows, whole]
            + [spec for spec, _, _ in sums],
            scratch_shapes=[
                pltpu.VMEM((rows, width), f32),
                pltpu.VMEM((rows, width), f32),
                pltpu.VMEM((rows, width), bf16),
                pltpu.VMEM((rows, width), bf16),
                pltpu.VMEM((rows, TILE), f32),
                pltpu.VMEM((rows, part), bf16),
                pltpu.VMEM((rows, part), bf16),
            ]
        ),
        out_shape=[
            jax.ShapeDtypeStruct(cot.shape, bf16),
            jax.ShapeDtypeStruct((sources, room, width), bf16),
        ]
        + [jax.ShapeDtypeStruct(shape, kind) for _, shape, kind in sums],
        input_output_aliases=aliases if more else {},
        compiler_params=pltpu.CompilerParams(vmem_limit_bytes=60 * 2**20),
        cost_estimate=pl.CostEstimate(
            flops=18 * rows * width * hidden, bytes_accessed=40 * 2**20,
            transcendentals=rows * hidden,
        ),
        name="experts",
    )(ctx, x, cot, up, down, *made)


def bits_of(axis):
    return [1 << b for b in range(lax.axis_size(axis).bit_length() - 1)][::-1]


def power_of_two(axis):
    size = lax.axis_size(axis)
    return size & (size - 1) == 0


def swap(x, axis, bit):
    size = lax.axis_size(axis)
    return lax.ppermute(x, axis, [(i, i ^ bit) for i in range(size)])


def ordered(x, other, axis, bit):
    high = (lax.axis_index(axis) & bit) > 0
    return jnp.where(high, other, x), jnp.where(high, x, other)


def after(x, *others):
    return lax.optimization_barrier((x, *others))[0]


def gather_rows(left, right):
    if not (power_of_two("ctx") and power_of_two("exp")):
        every = [lax.all_gather(x, ("ctx", "exp"), axis=0, tiled=True) for x in (left, right)]
        return [*every, every, every]
    bits = bits_of("exp")
    last = bits[-2:]
    parts = [left, right]
    held = [x[None] for x in parts]
    for bit in bits[:-2]:
        got = [swap(h, "exp", bit) for h in held]
        held = [
            jnp.stack(ordered(h, g, "exp", bit), axis=1).reshape((-1,) + h.shape[1:])
            for h, g in zip(held, got)
        ]
    got = [swap(h, "exp", bit) for h, bit in zip(held, last)]
    held = [jnp.stack(ordered(h, g, "exp", bit), axis=1) for h, g, bit in zip(held, got, last)]
    begun = held
    got = [swap(h, "exp", bit) for h, bit in zip(held, last[::-1])]
    held = [
        jnp.stack(ordered(h, g, "exp", bit), axis=at)
        for h, g, bit, at in zip(held, got, last[::-1], (2, 1))
    ]
    held = [h.reshape(-1, h.shape[-1]) for h in held]
    over_exp = held
    for bit in bits_of("ctx"):
        got = [swap(h, "ctx", bit) for h in held]
        held = [
            jnp.stack(ordered(h, g, "ctx", bit), axis=0).reshape(-1, h.shape[-1])
            for h, g in zip(held, got)
        ]
    return [*held, begun, over_exp]


def pair_rows(x):
    if lax.axis_size("ctx") != 2:
        return lax.all_gather(x, "ctx", axis=0, tiled=True)
    return jnp.concatenate([x, swap(x, "ctx", 1)], axis=0)


def add_received(mine, got, even):
    column = lax.broadcasted_iota(jnp.int32, mine.shape, mine.ndim - 1)
    rounded = lax.reduce_precision(mine, 8, 7)
    return jnp.where(column < even, mine, rounded) + got.astype(f32)


def halve(x, axis, bit, dim, even):
    side = ((lax.axis_index(axis) & bit) > 0).astype(jnp.int32)
    mine = lax.dynamic_index_in_dim(x, side, dim, keepdims=False)
    theirs = lax.dynamic_index_in_dim(x, 1 - side, dim, keepdims=False)
    return add_received(mine, swap(theirs.astype(bf16), axis, bit), even)


def scatter_sum(grads, width, late, small):
    blocks = lax.axis_size("exp")
    part = width // 2
    depth = part // blocks
    if not (
        power_of_two("exp") and lax.axis_size("ctx") == 2 and blocks > 3
        and small.shape[0] <= depth and small.shape[1] <= TILE
    ):
        whole = grads(lambda x, axis: x)
        sums = [
            lax.psum_scatter(x, ("ctx", "exp"), scatter_dimension=0, tiled=True) for x in whole
        ]
        return [*sums, lax.psum(small, ("ctx", "exp"))]
    me = lax.axis_index("ctx")
    rows, columns = small.shape
    small = jnp.pad(small, ((0, depth - rows), (0, TILE - columns)))
    small = jnp.broadcast_to(small[None], (blocks, depth, TILE)).reshape(part, TILE)

    def half_of(side):
        left, right = grads(lambda x, axis: lax.dynamic_slice_in_dim(x, side * part, part, axis))
        return jnp.concatenate([left, small], axis=1), right

    theirs = half_of(1 - me)
    even = [theirs[0].shape[1] - TILE, theirs[1].shape[1]]
    got = [swap(x.astype(bf16), "ctx", 1) for x in theirs]
    mine = half_of(me)
    bits = bits_of("exp")
    held = [after(add_received(m, g, e), late) for m, g, e in zip(mine, got, even)]
    held = [h.reshape((-1, 2, 2, depth, h.shape[1])) for h in held]
    high, low = bits[-2:]
    held = [halve(held[0], "exp", high, 1, even[0]), halve(held[1], "exp", low, 2, even[1])]
    held = [halve(held[0], "exp", low, 1, even[0]), halve(held[1], "exp", high, 1, even[1])]
    for bit in bits[:-2][::-1]:
        held = [
            halve(h.reshape((-1, 2) + h.shape[1:]), "exp", bit, 1, e) for h, e in zip(held, even)
        ]
    left, right = (h.reshape(h.shape[-2:]) for h in held)
    return [left[:, : even[0]], right, left[:rows, even[0] : even[0] + columns]]


def shards(
    inputs,
    cotangent,
    doc_ids,
    routes,
    query_key_value_weight,
    output_projection_weight,
    router,
    attn_gain,
    expert_gain,
    position_bias,
    expert_up,
    expert_down,
):
    batches = inputs.shape[0]
    length = inputs.shape[2]
    width = inputs.shape[3]
    top = routes.shape[3]
    ways = lax.axis_size("ctx")
    experts = lax.axis_size("exp")
    capacity = max(2, top * length * 10 // (7 * experts))
    room = (capacity + 1 + 15) // 16 * 16
    slots = experts * room
    seq_len = doc_ids.shape[2]
    buckets = position_bias.shape[1]
    me = lax.axis_index("ctx")

    expert_ids = jnp.arange(experts, dtype=jnp.int32)
    slot_rows = jnp.arange(slots, dtype=jnp.int32)
    earlier = jnp.tril(jnp.ones((length, length), bf16), -1)
    hots, slot_of, holds, spreads = [], [], [], []
    for b in range(batches):
        route_ids = routes[b, 0]
        hot = route_ids[:, :, None] == expert_ids[None, None, :]
        used = jnp.any(hot, axis=1)
        rank = mm(earlier, used.astype(bf16), ((1,), (0,))).astype(jnp.int32)
        slot = jnp.sum(jnp.where(hot, rank[:, None, :], 0), axis=2) + route_ids * room
        hold = [slot[None, :, k] == slot_rows[:, None] for k in range(top)]
        hots.append(hot)
        slot_of.append(slot)
        holds.append(hold)
        spreads.append(functools.reduce(jnp.logical_or, hold).astype(bf16))

    def dispatch(b, rows):
        sent = mm(spreads[b], rows, ((1,), (0,))).astype(bf16)
        return sent.reshape(experts, room, width)

    def cross(x):
        return lax.all_to_all(x, "exp", split_axis=0, concat_axis=0, tiled=True)

    cots = [cotangent[b, 0] for b in range(batches)]
    pad = -(experts + 2) % 128
    left, right, begun, over_exp = gather_rows(
        jnp.concatenate([query_key_value_weight[:, :width], output_projection_weight], axis=1),
        jnp.concatenate(
            [
                query_key_value_weight[:, width:],
                router,
                attn_gain[:, None],
                expert_gain[:, None],
                jnp.zeros((router.shape[0], pad), bf16),
            ],
            axis=1,
        ),
    )
    query_weight = left[:, :width]
    proj_weight = left[:, width:]
    kv_weight = right[:, : 2 * width]
    router_all = right[:, 2 * width : 2 * width + experts]
    gains = right[:, 2 * width + experts : 2 * width + experts + 2].astype(f32)
    attn_scale = gains[:, 0]
    expert_scale = gains[:, 1]
    expert_weights = [pair_rows(w[0]) for w in (expert_up, expert_down)]

    distance = jnp.arange(2 * TILE, dtype=jnp.int32)
    hot_bucket = (
        bucket_of(distance)[None, :] == jnp.arange(buckets, dtype=jnp.int32)[:, None]
    ).astype(f32)
    by_distance = jnp.sum(
        position_bias.astype(f32)[:, :, None] * hot_bucket[None], axis=1
    ) - position_bias.astype(f32)[:, buckets - 1 :]
    close = jnp.where(distance < TILE, by_distance, MASKED)
    beside = jnp.roll(by_distance, -TILE, axis=1)
    bias_rows = jnp.stack([close, beside], axis=1).reshape(PAIRS, 4, 2 * TILE)

    def norm_stats(values):
        return lax.rsqrt(jnp.mean(values * values, axis=-1, keepdims=True) + epsilon)

    state = []
    for b in range(batches):
        rows = inputs[b, 0].astype(f32)
        inv_one = norm_stats(rows)
        normed = (rows * inv_one * attn_scale).astype(bf16)
        kv = mm(normed, kv_weight, ((1,), (0,))).astype(bf16)
        queries = mm(normed, query_weight, ((1,), (0,))).astype(bf16)
        docs = doc_ids[b, 0].astype(f32)
        padded = jnp.concatenate([jnp.full((BACK,), -1.0, f32), docs])
        key_docs = lax.dynamic_slice_in_dim(padded, me * length, BACK + length)
        query_docs = key_docs[BACK:]
        if ways == 2:
            kv_back = lax.ppermute(kv, "ctx", [(0, 1)])
        else:
            every = lax.all_gather(kv, "ctx", axis=0, tiled=True)
            every = jnp.concatenate([jnp.zeros((BACK, 2 * width), bf16), every], axis=0)
            kv_back = lax.dynamic_slice_in_dim(every, me * length, BACK, 0)
        firsts = query_docs[::TILE]
        start = jnp.sum((key_docs[None, :] < firsts[:, None]).astype(jnp.int32), axis=1)
        tiles = jnp.arange(length // TILE, dtype=jnp.int32) + SPAN - start // TILE
        tiles = jnp.clip(tiles, 1, SPAN)
        view = (tiles, queries, kv, kv_back, query_docs[None], key_docs[None], bias_rows)
        state.append(dict(rows=rows, inv_one=inv_one, normed=normed, view=view))

    cot_rows = [after(c, *begun) for c in cots]
    cot_sent = jnp.concatenate([dispatch(b, cot_rows[b]) for b in range(batches)], axis=1)
    cot_here = cross(after(cot_sent, *over_exp))
    sent = ()
    for b, s in enumerate(state):
        s["view"] = (after(s["view"][0], *sent),) + s["view"][1:]
        attended, lse = attend(*s["view"])
        hidden = s["rows"] + mm(attended, proj_weight, ((1,), (0,)))
        inv_two = norm_stats(hidden)
        shared = (hidden * inv_two * expert_scale).astype(bf16)
        logits = mm(shared, router_all, ((1,), (0,)))
        hot = hots[b]
        chosen = jnp.sum(jnp.where(hot, logits[:, None, :], 0.0), axis=2)
        gate_exp = jnp.exp(chosen - jnp.max(chosen, axis=1, keepdims=True))
        gates = gate_exp / jnp.sum(gate_exp, axis=1, keepdims=True)
        gate_slots = sum(
            jnp.sum(jnp.where(holds[b][k], gates[None, :, k], 0.0), axis=1) for k in range(top)
        ).reshape(experts, 1, room)
        gate_slots = jnp.pad(gate_slots, ((0, 0), (0, 0), (0, TILE - room)))
        gate_high = gate_slots.astype(bf16)
        gate_low = (gate_slots - gate_high.astype(f32)).astype(bf16)
        gate_row = jnp.concatenate(
            [gate_high, gate_low, jnp.zeros((experts, 1, width - 2 * TILE), bf16)], axis=2
        )
        at_gate = lax.broadcasted_iota(jnp.int32, (1, room, 1), 1) == capacity
        sent = (jnp.where(at_gate, gate_row, dispatch(b, shared)),)
        s.update(attended=attended, lse=lse, hidden=hidden, inv_two=inv_two, shared=shared,
                 gates=gates, sent=sent[0])

    made = ()
    last = (cot_here, *(s["sent"] for s in state))
    for s in state:
        s["here"] = cross(after(s["sent"], *last))
        last = (s["here"],)
    for b, s in enumerate(state):
        y, back, *sums = run_experts(
            me[None].astype(jnp.int32), s["here"], cot_here, b, *expert_weights, made, capacity,
            ways == 2, ways == 2 and b == batches - 1,
        )
        made = (y, *sums)
        s["back"] = cross(after(back, *last))
        last = (s["back"],)
    results = cross(after(y, *last))
    if ways == 2:
        up_share, down_share = (
            (mine + swap(theirs, "ctx", 1).astype(f32))[None]
            for mine, theirs in zip(sums[::2], sums[1::2])
        )
    else:
        up_share, down_share = (
            lax.psum_scatter(g.astype(bf16), "ctx", scatter_dimension=0, tiled=True).astype(f32)[None]
            for g in sums
        )

    input_grads = []
    parts = []
    picks = []
    before = ()
    for b, s in enumerate(state):
        upstream = cots[b].astype(f32)
        packet = after(s["back"], *before)
        dots = packet[:, capacity, : 2 * TILE].astype(f32)
        dots = (dots[:, :room] + dots[:, TILE : TILE + room]).reshape(1, slots)
        slot = slot_of[b]
        pick = [slot[:, k : k + 1] == slot_rows[None, :] for k in range(top)]
        picks.append(functools.reduce(jnp.logical_or, pick).astype(bf16))
        scaled = jnp.stack([jnp.sum(jnp.where(p, dots, 0.0), axis=1) for p in pick], axis=1)
        chosen_grad = scaled - s["gates"] * jnp.sum(scaled, axis=1, keepdims=True)
        logit_grad = jnp.sum(jnp.where(hots[b], chosen_grad[:, :, None], 0.0), axis=1).astype(bf16)
        shared_grad = mm(picks[b], packet.reshape(slots, width), ((1,), (0,)))
        shared_grad = shared_grad + mm(logit_grad, router_all, ((1,), (1,)))
        unit = s["hidden"] * s["inv_two"]
        grad_expert = jnp.sum(shared_grad * unit, axis=0)
        inner = shared_grad * expert_scale
        hidden_grad = upstream + s["inv_two"] * (
            inner - unit * jnp.mean(inner * unit, axis=1, keepdims=True)
        )
        branch_grad = hidden_grad.astype(bf16)
        attended_grad = mm(branch_grad, proj_weight, ((1,), (1,))).astype(bf16)
        dq, own, back, near = attend_back(*s["view"], s["attended"], attended_grad, s["lse"])
        before = (dq,)
        if ways == 2:
            got = lax.ppermute(back, "ctx", [(1, 0)])
        else:
            every = jnp.zeros((2, BACK + seq_len, width), bf16)
            every = lax.dynamic_update_slice_in_dim(every, back, me * length, 1)
            got = lax.psum_scatter(every[:, BACK:], "ctx", scatter_dimension=1, tiled=True)
        both = (own.astype(f32) + got.astype(f32)).astype(bf16)
        dkv = jnp.concatenate([both[0], both[1]], axis=1)
        normed = s["normed"]
        normed_grad = mm(dq, query_weight, ((1,), (1,))) + mm(dkv, kv_weight, ((1,), (1,)))
        unit = s["rows"] * s["inv_one"]
        grad_attn = jnp.sum(normed_grad * unit, axis=0)
        inner = normed_grad * attn_scale
        input_part = s["inv_one"] * (inner - unit * jnp.mean(inner * unit, axis=1, keepdims=True))
        input_grads.append((hidden_grad + input_part).astype(bf16))
        parts.append((near, grad_attn, grad_expert))
        s.update(dq=dq, dkv=dkv, branch_grad=branch_grad, logit_grad=logit_grad)

    outputs = []
    for b, s in enumerate(state):
        mine = results[:, b * room : (b + 1) * room].reshape(slots, width)
        outputs.append((s["hidden"] + mm(picks[b], mine, ((1,), (0,)))).astype(bf16))

    near, grad_attn, grad_expert = (functools.reduce(jnp.add, p) for p in zip(*parts))

    def weight_grads(rows):
        def total(left, right):
            return functools.reduce(
                jnp.add, [mm(rows(s[left], 1), s[right], ((0,), (0,))) for s in state]
            )

        small = total("shared", "logit_grad")
        return (
            jnp.concatenate([total("normed", "dq"), total("attended", "branch_grad")], axis=1),
            jnp.concatenate(
                [
                    total("normed", "dkv"),
                    small,
                    rows(grad_attn, 0)[:, None],
                    rows(grad_expert, 0)[:, None],
                    jnp.zeros((small.shape[0], pad), f32),
                ],
                axis=1,
            ),
        )

    hot_near = jnp.where(
        jnp.arange(buckets)[:, None] < buckets - 1, hot_bucket[:, :TILE], 0.0
    )
    grad_bias = jnp.sum(near.reshape(HEADS, 1, TILE) * hot_near[None], axis=2)
    far = jnp.where(jnp.arange(buckets) == buckets - 1, 1.0, 0.0)
    grad_bias = grad_bias - jnp.sum(grad_bias, axis=1, keepdims=True) * far
    left, right, bias_total = scatter_sum(weight_grads, width, results, grad_bias)
    return (
        jnp.stack(outputs)[:, None],
        jnp.stack(input_grads)[:, None],
        jnp.concatenate([left[:, :width], right[:, : 2 * width]], axis=1),
        left[:, width:],
        right[:, 2 * width : 2 * width + experts],
        right[:, 2 * width + experts],
        right[:, 2 * width + experts + 1],
        bias_total,
        up_share,
        down_share,
    )


def solution(mesh):
    placed = (
        P(None, "exp", "ctx", None),
        P(None, "exp", "ctx", None),
        P(None, "exp", None),
        P(None, "exp", "ctx", None),
        P(("ctx", "exp"), None),
        P(("ctx", "exp"), None),
        P(("ctx", "exp"), None),
        P(("ctx", "exp")),
        P(("ctx", "exp")),
        P(),
        P("exp", "ctx", None),
        P("exp", "ctx", None),
    )
    return jax.shard_map(
        shards,
        mesh=mesh,
        in_specs=placed,
        out_specs=(
            P(None, "exp", "ctx", None),
            P(None, "exp", "ctx", None),
            P(("ctx", "exp"), None),
            P(("ctx", "exp"), None),
            P(("ctx", "exp"), None),
            P(("ctx", "exp")),
            P(("ctx", "exp")),
            P(),
            P("exp", "ctx", None),
            P("exp", "ctx", None),
        ),
        check_vma=False,
    )
```

```python
import functools
import math

import jax
import jax.numpy as jnp
from jax import lax
from jax.experimental import pallas as pl
from jax.experimental.pallas import tpu as pltpu
from jax.sharding import PartitionSpec as P

HEADS = 12
HEAD = 64
PAIRS = HEADS // 2
GROUP = 3
TILE = 128
BACK = 512
SPAN = BACK // TILE + 1
MASKED = -1000000000.0

epsilon = 1e-06
thresholds = (19, 21, 24, 27, 31, 35, 40, 46, 52, 59, 67, 77, 87, 99, 113)
bf16 = jnp.bfloat16
f32 = jnp.float32


def bucket_of(distance):
    distance = jnp.maximum(distance, 0)
    beyond = jnp.zeros_like(distance)
    for threshold in thresholds:
        beyond = beyond + (distance >= threshold).astype(jnp.int32)
    return jnp.where(distance < 16, distance, 16 + beyond)


def mm(a, b, dims):
    return lax.dot_general(a, b, (dims, ((), ())), preferred_element_type=f32)


def stack_heads(rows):
    lane = lax.broadcasted_iota(jnp.int32, rows.shape, 1)
    zero = jnp.zeros_like(rows)
    return jnp.concatenate(
        [jnp.where(lane < HEAD, rows, zero), jnp.where(lane >= HEAD, rows, zero)], axis=0
    )


def fold_heads(wide):
    return jnp.concatenate([wide[:HEAD, :TILE], wide[HEAD:, TILE:]], axis=0)


def fill_mask(mask, qd_ref, kd_ref):
    for qi in range(qd_ref.shape[1] // TILE):
        docs_row = qd_ref[:, qi * TILE : (qi + 1) * TILE]
        for j in range(SPAN):
            kt = (qi + j) * TILE
            column = jnp.broadcast_to(kd_ref[:, kt : kt + TILE], (TILE, TILE)).T
            mask[qi, j * TILE : (j + 1) * TILE, :] = jnp.where(
                column == docs_row, 0.0, MASKED
            ).astype(f32)


def fill_bias(bias, bv_ref):
    for g in range(GROUP):
        for head in range(2):
            for d in range(2):
                row = bv_ref[g, 2 * head + d : 2 * head + d + 1, :]
                rolled = pltpu.roll(
                    jnp.broadcast_to(row, (TILE, 2 * TILE)), 0, 1, stride=1, stride_axis=0
                )
                bias[g, d, :, head * TILE : (head + 1) * TILE] = rolled[:, :TILE]


def lanes_of(g):
    return slice(g * TILE, (g + 1) * TILE)


def masked_scores(scores, mask, bias, g, qi, tiles):
    parts = []
    for j in range(tiles):
        d = tiles - 1 - j
        off = (SPAN - tiles + j) * TILE
        m = mask[qi, off : off + TILE, :]
        x = scores[j * TILE : (j + 1) * TILE] + jnp.concatenate([m, m], axis=1)
        if d < 2:
            x = x + bias[g, d]
        parts.append(x)
    return parts


def transpose_tiles(out, at, rows_ref):
    for g in range(GROUP):
        for t in range(0, rows_ref.shape[0], TILE):
            out[g, :, at + t : at + t + TILE] = rows_ref[t : t + TILE, lanes_of(g)].T


def fwd_kernel(tiles, q_ref, k_ref, v_ref, kp_ref, vp_ref, qd_ref, kd_ref, bv_ref, o_ref, lse_ref,
               kwin, vwin_t, bias, mask):
    @pl.when(pl.program_id(0) == 0)
    def _():
        fill_mask(mask, qd_ref, kd_ref)

    fill_bias(bias, bv_ref)
    kwin[:BACK] = kp_ref[...]
    kwin[BACK:] = k_ref[...]
    transpose_tiles(vwin_t, 0, vp_ref)
    transpose_tiles(vwin_t, BACK, v_ref)
    groups = range(GROUP)

    def step(qi, carry):
        q0 = pl.multiple_of(qi * TILE, TILE)
        q2 = [stack_heads(q_ref[pl.ds(q0, TILE), lanes_of(g)] * 0.125) for g in groups]

        def branch(count):
            def go():
                lo = pl.multiple_of((qi + SPAN - count) * TILE, TILE)
                rows = pl.ds(lo, count * TILE)
                raw = [mm(kwin[rows, lanes_of(g)], q2[g], ((1,), (1,))) for g in groups]
                lows, tops, totals = [], [], []
                for g in groups:
                    parts = masked_scores(raw[g], mask, bias, g, qi, count)
                    top = functools.reduce(jnp.maximum, parts)
                    top = jnp.max(top, axis=0, keepdims=True)
                    probs = [jnp.exp(x - top) for x in parts]
                    totals.append(
                        jnp.sum(functools.reduce(jnp.add, probs), axis=0, keepdims=True)
                    )
                    tops.append(top)
                    lows.append(jnp.concatenate([p.astype(bf16) for p in probs], axis=0))
                outs = [mm(vwin_t[g, :, rows], lows[g], ((1,), (0,))) for g in groups]
                row = lax.broadcasted_iota(jnp.int32, (TILE, TILE), 0)
                for g in groups:
                    inv = 1.0 / totals[g]
                    out = fold_heads(outs[g]) * jnp.where(
                        row < HEAD, inv[:, :TILE], inv[:, TILE:]
                    )
                    o_ref[pl.ds(q0, TILE), lanes_of(g)] = out.T.astype(bf16)
                    lse_ref[g, pl.ds(qi, 1), :] = tops[g] + jnp.log(totals[g])
                return 0

            return go

        lax.switch(tiles[qi] - 1, [branch(c) for c in range(1, SPAN + 1)])
        return carry

    lax.fori_loop(0, q_ref.shape[0] // TILE, step, 0)


def bwd_kernel(tiles, q_ref, k_ref, v_ref, kp_ref, vp_ref, qd_ref, kd_ref, bv_ref, o_ref, do_ref,
               lse_ref, dq_ref, own_ref, back_ref, near_ref,
               kwin, kwin_t, vwin, dk, dv, near, bias, mask):
    @pl.when(pl.program_id(0) == 0)
    def _():
        fill_mask(mask, qd_ref, kd_ref)

    fill_bias(bias, bv_ref)
    kwin[:BACK] = kp_ref[...]
    kwin[BACK:] = k_ref[...]
    vwin[:BACK] = vp_ref[...]
    vwin[BACK:] = v_ref[...]
    transpose_tiles(kwin_t, 0, kp_ref)
    transpose_tiles(kwin_t, BACK, k_ref)
    dk[...] = jnp.zeros_like(dk)
    dv[...] = jnp.zeros_like(dv)
    near[...] = jnp.zeros_like(near)
    groups = range(GROUP)

    def step(qi, carry):
        q0 = pl.multiple_of(qi * TILE, TILE)
        q2, do2, lse, delta = [], [], [], []
        for g in groups:
            q2.append(stack_heads(q_ref[pl.ds(q0, TILE), lanes_of(g)] * 0.125))
            do = do_ref[pl.ds(q0, TILE), lanes_of(g)]
            do2.append(stack_heads(do))
            lse.append(lse_ref[g, pl.ds(qi, 1), :])
            prod = (do.astype(f32) * o_ref[pl.ds(q0, TILE), lanes_of(g)].astype(f32)).T
            delta.append(
                jnp.concatenate(
                    [jnp.sum(prod[:HEAD], axis=0, keepdims=True),
                     jnp.sum(prod[HEAD:], axis=0, keepdims=True)],
                    axis=1,
                )
            )

        def branch(count):
            def go():
                lo = pl.multiple_of((qi + SPAN - count) * TILE, TILE)
                rows = pl.ds(lo, count * TILE)
                raw = [mm(kwin[rows, lanes_of(g)], q2[g], ((1,), (1,))) for g in groups]
                prob_grad = [mm(vwin[rows, lanes_of(g)], do2[g], ((1,), (1,))) for g in groups]
                low, score_grad = [], []
                for g in groups:
                    parts = masked_scores(raw[g], mask, bias, g, qi, count)
                    lows, grads = [], []
                    for j in range(count):
                        prob = jnp.exp(parts[j] - lse[g])
                        grad = prob * (prob_grad[g][j * TILE : (j + 1) * TILE] - delta[g])
                        if j == count - 1:
                            near[g] += grad
                        elif j == count - 2:
                            r = lax.broadcasted_iota(jnp.int32, grad.shape, 0)
                            c = lax.broadcasted_iota(jnp.int32, grad.shape, 1)
                            c = jnp.where(c >= TILE, c - TILE, c)
                            near[g] += jnp.where(c < r, grad, 0.0)
                        lows.append(prob.astype(bf16))
                        grads.append(grad.astype(bf16))
                    low.append(jnp.concatenate(lows, axis=0))
                    score_grad.append(jnp.concatenate(grads, axis=0))
                for g in groups:
                    dv[rows, lanes_of(g)] += mm(low[g], do2[g], ((1,), (0,)))
                    dk[rows, lanes_of(g)] += mm(score_grad[g], q2[g], ((1,), (0,)))
                for g in groups:
                    dq = fold_heads(mm(kwin_t[g, :, rows], score_grad[g], ((1,), (0,))))
                    dq_ref[pl.ds(q0, TILE), lanes_of(g)] = (dq.T * 0.125).astype(bf16)
                return 0

            return go

        lax.switch(tiles[qi] - 1, [branch(c) for c in range(1, SPAN + 1)])
        return carry

    lax.fori_loop(0, q_ref.shape[0] // TILE, step, 0)
    for i, total in enumerate((dk, dv)):
        back_ref[i] = total[:BACK].astype(bf16)
        own_ref[i] = total[BACK:].astype(bf16)
    for g in groups:
        for head in range(2):
            turned = near[g, :, lanes_of(head)]
            r = lax.broadcasted_iota(jnp.int32, turned.shape, 0)
            bit = 1
            while bit < TILE:
                turned = jnp.where((r & bit) > 0, pltpu.roll(turned, TILE - bit, 1), turned)
                bit *= 2
            near_ref[g, :, lanes_of(head)] = jnp.sum(turned, axis=0, keepdims=True)


def attention_specs(length):
    full = lambda p, *_: (0, 0)
    lanes = lambda off: (lambda p, *_: (0, p + off))
    return [
        pl.BlockSpec((length, GROUP * TILE), lanes(0)),
        pl.BlockSpec((length, GROUP * TILE), lanes(0)),
        pl.BlockSpec((length, GROUP * TILE), lanes(PAIRS // GROUP)),
        pl.BlockSpec((BACK, GROUP * TILE), lanes(0)),
        pl.BlockSpec((BACK, GROUP * TILE), lanes(PAIRS // GROUP)),
        pl.BlockSpec((1, length), full),
        pl.BlockSpec((1, BACK + length), full),
        pl.BlockSpec((GROUP, 4, 2 * TILE), lambda p, *_: (p, 0, 0)),
    ]


def attend(tiles, queries, kv, kv_back, query_docs, key_docs, bias_rows):
    length = queries.shape[0]
    width = HEADS * HEAD
    blocks = length // TILE
    return pl.pallas_call(
        fwd_kernel,
        grid_spec=pltpu.PrefetchScalarGridSpec(
            num_scalar_prefetch=1,
            grid=(PAIRS // GROUP,),
            in_specs=attention_specs(length),
            out_specs=[
                pl.BlockSpec((length, GROUP * TILE), lambda p, *_: (0, p)),
                pl.BlockSpec((GROUP, blocks, 2 * TILE), lambda p, *_: (p, 0, 0)),
            ],
            scratch_shapes=[
                pltpu.VMEM((BACK + length, GROUP * TILE), bf16),
                pltpu.VMEM((GROUP, TILE, BACK + length), bf16),
                pltpu.VMEM((GROUP, 2, TILE, 2 * TILE), f32),
                pltpu.VMEM((blocks, SPAN * TILE, TILE), f32),
            ],
        ),
        out_shape=[
            jax.ShapeDtypeStruct((length, width), bf16),
            jax.ShapeDtypeStruct((PAIRS, blocks, 2 * TILE), f32),
        ],
        compiler_params=pltpu.CompilerParams(vmem_limit_bytes=32 * 2**20),
        cost_estimate=pl.CostEstimate(
            flops=4 * 2 * HEADS * length * BACK * 128, bytes_accessed=6 * 2**20,
            transcendentals=HEADS * length * BACK,
        ),
        name="attend",
    )(tiles, queries, kv, kv, kv_back, kv_back, query_docs, key_docs, bias_rows)


def attend_back(tiles, queries, kv, kv_back, query_docs, key_docs, bias_rows, out, out_grad, lse):
    length = queries.shape[0]
    width = HEADS * HEAD
    blocks = length // TILE
    own = pl.BlockSpec((length, GROUP * TILE), lambda p, *_: (0, p))
    both = lambda n: pl.BlockSpec((2, n, GROUP * TILE), lambda p, *_: (0, 0, p))
    return pl.pallas_call(
        bwd_kernel,
        grid_spec=pltpu.PrefetchScalarGridSpec(
            num_scalar_prefetch=1,
            grid=(PAIRS // GROUP,),
            in_specs=attention_specs(length)
            + [own, own, pl.BlockSpec((GROUP, blocks, 2 * TILE), lambda p, *_: (p, 0, 0))],
            out_specs=[own, both(length), both(BACK),
                       pl.BlockSpec((GROUP, 1, 2 * TILE), lambda p, *_: (p, 0, 0))],
            scratch_shapes=[
                pltpu.VMEM((BACK + length, GROUP * TILE), bf16),
                pltpu.VMEM((GROUP, TILE, BACK + length), bf16),
                pltpu.VMEM((BACK + length, GROUP * TILE), bf16),
                pltpu.VMEM((BACK + length, GROUP * TILE), f32),
                pltpu.VMEM((BACK + length, GROUP * TILE), f32),
                pltpu.VMEM((GROUP, TILE, 2 * TILE), f32),
                pltpu.VMEM((GROUP, 2, TILE, 2 * TILE), f32),
                pltpu.VMEM((blocks, SPAN * TILE, TILE), f32),
            ],
        ),
        out_shape=[
            jax.ShapeDtypeStruct((length, width), bf16),
            jax.ShapeDtypeStruct((2, length, width), bf16),
            jax.ShapeDtypeStruct((2, BACK, width), bf16),
            jax.ShapeDtypeStruct((PAIRS, 1, 2 * TILE), f32),
        ],
        compiler_params=pltpu.CompilerParams(vmem_limit_bytes=32 * 2**20),
        cost_estimate=pl.CostEstimate(
            flops=2**20, bytes_accessed=2**20, transcendentals=0,
        ),
        name="attend_back",
    )(tiles, queries, kv, kv, kv_back, kv_back, query_docs, key_docs, bias_rows, out, out_grad, lse)


GELU_A = 0.7978845608028654
GELU_B = 0.044715


def expert_kernel(more, halves, split, capacity, room, chunk, ctx, x_ref, cot_ref, up_ref, down_ref, *refs):
    refs = list(refs)
    take = lambda n: [refs.pop(0) for _ in range(n)]
    if more:
        _, up_before, down_before = take(3)
    y_ref, back_ref = take(2)
    sums = take(4 if split else 2)
    y_sum, back_sum, x, result_grad, gate, act_all, pre_grad_all = take(7)
    rows, width = x.shape
    step = pl.program_id(0)
    pieces = 2 if halves else 1
    piece = width // pieces

    def columns(i):
        return pl.ds(pl.multiple_of((ctx[0] + i) % pieces * piece, TILE), piece)

    @pl.when(step == 0)
    def _():
        lane = lax.broadcasted_iota(jnp.int32, (1, TILE), 1)
        for e in range(rows // room):
            at = e * room
            for i in range(pieces):
                x[at : at + room, i * piece : (i + 1) * piece] = x_ref[e, :, columns(i)]
            line = x_ref[e, capacity : capacity + 1, : 2 * TILE].astype(f32)
            line = jnp.where(lane < capacity, line[:, :TILE] + line[:, TILE:], 0.0)
            column = jnp.broadcast_to(line, (TILE, TILE)).T[:room]
            gate[at : at + room, :] = column
            for c in range(0, width, TILE):
                result_grad[at : at + room, c : c + TILE] = (
                    cot_ref[e, :, c : c + TILE].astype(f32) * column
                ).astype(bf16)
        y_sum[...] = jnp.zeros_like(y_sum)
        back_sum[...] = jnp.zeros_like(back_sum)

    def part(i, carry):
        r = pl.ds(pl.multiple_of(i * chunk, chunk), chunk)
        pre = mm(x[r, :], up_ref[...], ((1,), (0,)))
        act_grad = mm(result_grad[r, :], down_ref[...], ((1,), (1,)))
        square = pre * pre
        half = 0.5 + 0.5 * jnp.tanh(pre * (GELU_A + (GELU_A * GELU_B) * square))
        act = (pre * half).astype(bf16)
        slope = 2.0 * GELU_A + (6.0 * GELU_A * GELU_B) * square
        pre_grad = (act_grad * (half * (1.0 + pre * (1.0 - half) * slope))).astype(bf16)
        act_all[r, :] = act
        pre_grad_all[r, :] = pre_grad
        y_sum[r, :] += mm(act, down_ref[...], ((1,), (0,)))
        back_sum[r, :] += mm(pre_grad, up_ref[...], ((1,), (1,)))
        return carry

    lax.fori_loop(0, rows // chunk, part, 0)

    def up_grad():
        grad = mm(x[...], pre_grad_all[...], ((0,), (0,)))
        return grad + up_before[...] if more else grad

    def down_grad():
        grad = mm(act_all[...], result_grad[...], ((0,), (0,)))
        return grad + down_before[...] if more else grad

    if split:
        mine, theirs, down_mine, down_theirs = sums
        early = step < pl.num_programs(0) // 2

        @pl.when(early)
        def _():
            down_mine[...] = down_grad()

        @pl.when(jnp.logical_not(early))
        def _():
            down_theirs[...] = down_grad().astype(bf16)

        grad = up_grad()
        mine[...] = grad[:piece]
        theirs[...] = grad[piece:].astype(bf16)
    else:
        sums[1][...] = down_grad()
        sums[0][...] = up_grad()

    @pl.when(step == pl.num_programs(0) - 1)
    def _():
        row = lax.broadcasted_iota(jnp.int32, (room, 1), 0)
        for e in range(rows // room):
            at = e * room
            dots = jnp.zeros((room, TILE), f32)
            for c in range(0, width, TILE):
                scaled = y_sum[at : at + room, c : c + TILE] * gate[at : at + room, :]
                y_ref[e, :, c : c + TILE] = scaled.astype(bf16)
                dots = dots + scaled * cot_ref[e, :, c : c + TILE].astype(f32)
            if room < TILE:
                dots = jnp.concatenate([dots, jnp.zeros((TILE - room, TILE), f32)], axis=0)
            line = jnp.sum(dots.T, axis=0, keepdims=True)
            high = line.astype(bf16).astype(f32)
            line = jnp.concatenate(
                [high, line - high, jnp.zeros((1, width - 2 * TILE), f32)], axis=1
            )
            for i in range(pieces):
                back_ref[e, :, columns(i)] = back_sum[
                    at : at + room, i * piece : (i + 1) * piece
                ].astype(bf16)
            back_ref[e] = jnp.where(row == capacity, line.astype(bf16), back_ref[e])


def run_experts(ctx, x, cot, batch, up, down, made, capacity, halves, split):
    sources, room, width = x.shape
    rows = sources * room
    hidden = up.shape[1]
    part = math.gcd(hidden // 2, 512)
    steps = hidden // part
    ahead = steps // 2 if halves else 0
    chunk = rows // 2 if rows % 32 == 0 else rows
    more = len(made) > 0
    once = pl.Buffered(1)
    columns = pl.BlockSpec((width, part), lambda t, c: (0, (t + c[0] * ahead) % steps))
    lines = pl.BlockSpec((part, width), lambda t, c: (t, 0))
    cot_rows = pl.BlockSpec((sources, room, width), lambda t, c: (0, batch, 0), pipeline_mode=once)
    whole = pl.BlockSpec((sources, room, width), lambda t, c: (0, 0, 0), pipeline_mode=once)
    if split:
        half = pl.BlockSpec((width // 2, part), lambda t, c: (0, (t + c[0] * ahead) % steps))
        sums = [
            (half, (width // 2, hidden), f32),
            (half, (width // 2, hidden), bf16),
            (pl.BlockSpec((part, width), lambda t, c: (jnp.minimum(t, ahead - 1), 0)),
             (hidden // 2, width), f32),
            (pl.BlockSpec((part, width), lambda t, c: (jnp.maximum(t - ahead, 0), 0)),
             (hidden // 2, width), bf16),
        ]
    else:
        sums = [(columns, up.shape, f32), (lines, down.shape, f32)]
    aliases = {5: 0} if split else {5: 0, 6: 2, 7: 3}
    return pl.pallas_call(
        functools.partial(expert_kernel, more, halves, split, capacity, room, chunk),
        grid_spec=pltpu.PrefetchScalarGridSpec(
            num_scalar_prefetch=1,
            grid=(steps,),
            in_specs=[whole, cot_rows, columns, lines]
            + ([pl.BlockSpec(memory_space=pl.ANY), columns, lines] if more else []),
            out_specs=[cot_rows, whole]
            + [spec for spec, _, _ in sums],
            scratch_shapes=[
                pltpu.VMEM((rows, width), f32),
                pltpu.VMEM((rows, width), f32),
                pltpu.VMEM((rows, width), bf16),
                pltpu.VMEM((rows, width), bf16),
                pltpu.VMEM((rows, TILE), f32),
                pltpu.VMEM((rows, part), bf16),
                pltpu.VMEM((rows, part), bf16),
            ]
        ),
        out_shape=[
            jax.ShapeDtypeStruct(cot.shape, bf16),
            jax.ShapeDtypeStruct((sources, room, width), bf16),
        ]
        + [jax.ShapeDtypeStruct(shape, kind) for _, shape, kind in sums],
        input_output_aliases=aliases if more else {},
        compiler_params=pltpu.CompilerParams(vmem_limit_bytes=60 * 2**20),
        cost_estimate=pl.CostEstimate(
            flops=18 * rows * width * hidden, bytes_accessed=40 * 2**20,
            transcendentals=rows * hidden,
        ),
        name="experts",
    )(ctx, x, cot, up, down, *made)


def bits_of(axis):
    return [1 << b for b in range(lax.axis_size(axis).bit_length() - 1)][::-1]


def power_of_two(axis):
    size = lax.axis_size(axis)
    return size & (size - 1) == 0


def swap(x, axis, bit):
    size = lax.axis_size(axis)
    return lax.ppermute(x, axis, [(i, i ^ bit) for i in range(size)])


def ordered(x, other, axis, bit):
    high = (lax.axis_index(axis) & bit) > 0
    return jnp.where(high, other, x), jnp.where(high, x, other)


def after(x, *others):
    return lax.optimization_barrier((x, *others))[0]


def gather_rows(left, right):
    if not (power_of_two("ctx") and power_of_two("exp")):
        every = [lax.all_gather(x, ("ctx", "exp"), axis=0, tiled=True) for x in (left, right)]
        return [*every, every, every]
    bits = bits_of("exp")
    last = bits[-2:]
    parts = [left, right]
    held = [x[None] for x in parts]
    for bit in bits[:-2]:
        got = [swap(h, "exp", bit) for h in held]
        held = [
            jnp.stack(ordered(h, g, "exp", bit), axis=1).reshape((-1,) + h.shape[1:])
            for h, g in zip(held, got)
        ]
    got = [swap(h, "exp", bit) for h, bit in zip(held, last)]
    held = [jnp.stack(ordered(h, g, "exp", bit), axis=1) for h, g, bit in zip(held, got, last)]
    begun = held
    got = [swap(h, "exp", bit) for h, bit in zip(held, last[::-1])]
    held = [
        jnp.stack(ordered(h, g, "exp", bit), axis=at)
        for h, g, bit, at in zip(held, got, last[::-1], (2, 1))
    ]
    held = [h.reshape(-1, h.shape[-1]) for h in held]
    over_exp = held
    for bit in bits_of("ctx"):
        got = [swap(h, "ctx", bit) for h in held]
        held = [
            jnp.stack(ordered(h, g, "ctx", bit), axis=0).reshape(-1, h.shape[-1])
            for h, g in zip(held, got)
        ]
    return [*held, begun, over_exp]


def pair_rows(x):
    if lax.axis_size("ctx") != 2:
        return lax.all_gather(x, "ctx", axis=0, tiled=True)
    return jnp.concatenate([x, swap(x, "ctx", 1)], axis=0)


def add_received(mine, got, even):
    column = lax.broadcasted_iota(jnp.int32, mine.shape, mine.ndim - 1)
    rounded = lax.reduce_precision(mine, 8, 7)
    return jnp.where(column < even, mine, rounded) + got.astype(f32)


def halve(x, axis, bit, dim, even):
    side = ((lax.axis_index(axis) & bit) > 0).astype(jnp.int32)
    mine = lax.dynamic_index_in_dim(x, side, dim, keepdims=False)
    theirs = lax.dynamic_index_in_dim(x, 1 - side, dim, keepdims=False)
    return add_received(mine, swap(theirs.astype(bf16), axis, bit), even)


def scatter_sum(grads, width, late, small):
    blocks = lax.axis_size("exp")
    part = width // 2
    depth = part // blocks
    if not (
        power_of_two("exp") and lax.axis_size("ctx") == 2 and blocks > 3
        and small.shape[0] <= depth and small.shape[1] <= TILE
    ):
        whole = grads(lambda x, axis: x)
        sums = [
            lax.psum_scatter(x, ("ctx", "exp"), scatter_dimension=0, tiled=True) for x in whole
        ]
        return [*sums, lax.psum(small, ("ctx", "exp"))]
    me = lax.axis_index("ctx")
    rows, columns = small.shape
    small = jnp.pad(small, ((0, depth - rows), (0, TILE - columns)))
    small = jnp.broadcast_to(small[None], (blocks, depth, TILE)).reshape(part, TILE)

    def half_of(side):
        left, right = grads(lambda x, axis: lax.dynamic_slice_in_dim(x, side * part, part, axis))
        return jnp.concatenate([left, small], axis=1), right

    theirs = half_of(1 - me)
    even = [theirs[0].shape[1] - TILE, theirs[1].shape[1]]
    got = [swap(x.astype(bf16), "ctx", 1) for x in theirs]
    mine = half_of(me)
    bits = bits_of("exp")
    held = [after(add_received(m, g, e), late) for m, g, e in zip(mine, got, even)]
    held = [h.reshape((-1, 2, 2, depth, h.shape[1])) for h in held]
    high, low = bits[-2:]
    held = [halve(held[0], "exp", high, 1, even[0]), halve(held[1], "exp", low, 2, even[1])]
    held = [halve(held[0], "exp", low, 1, even[0]), halve(held[1], "exp", high, 1, even[1])]
    for bit in bits[:-2][::-1]:
        held = [
            halve(h.reshape((-1, 2) + h.shape[1:]), "exp", bit, 1, e) for h, e in zip(held, even)
        ]
    left, right = (h.reshape(h.shape[-2:]) for h in held)
    return [left[:, : even[0]], right, left[:rows, even[0] : even[0] + columns]]


def shards(
    inputs,
    cotangent,
    doc_ids,
    routes,
    query_key_value_weight,
    output_projection_weight,
    router,
    attn_gain,
    expert_gain,
    position_bias,
    expert_up,
    expert_down,
):
    batches = inputs.shape[0]
    length = inputs.shape[2]
    width = inputs.shape[3]
    top = routes.shape[3]
    ways = lax.axis_size("ctx")
    experts = lax.axis_size("exp")
    capacity = max(2, top * length * 10 // (7 * experts))
    room = (capacity + 1 + 15) // 16 * 16
    slots = experts * room
    seq_len = doc_ids.shape[2]
    buckets = position_bias.shape[1]
    me = lax.axis_index("ctx")

    expert_ids = jnp.arange(experts, dtype=jnp.int32)
    slot_rows = jnp.arange(slots, dtype=jnp.int32)
    earlier = jnp.tril(jnp.ones((length, length), bf16), -1)
    hots, slot_of, holds, spreads = [], [], [], []
    for b in range(batches):
        route_ids = routes[b, 0]
        hot = route_ids[:, :, None] == expert_ids[None, None, :]
        used = jnp.any(hot, axis=1)
        rank = mm(earlier, used.astype(bf16), ((1,), (0,))).astype(jnp.int32)
        slot = jnp.sum(jnp.where(hot, rank[:, None, :], 0), axis=2) + route_ids * room
        hold = [slot[None, :, k] == slot_rows[:, None] for k in range(top)]
        hots.append(hot)
        slot_of.append(slot)
        holds.append(hold)
        spreads.append(functools.reduce(jnp.logical_or, hold).astype(bf16))

    def dispatch(b, rows):
        sent = mm(spreads[b], rows, ((1,), (0,))).astype(bf16)
        return sent.reshape(experts, room, width)

    def cross(x):
        return lax.all_to_all(x, "exp", split_axis=0, concat_axis=0, tiled=True)

    cots = [cotangent[b, 0] for b in range(batches)]
    pad = -(experts + 2) % 128
    left, right, begun, over_exp = gather_rows(
        jnp.concatenate([query_key_value_weight[:, :width], output_projection_weight], axis=1),
        jnp.concatenate(
            [
                query_key_value_weight[:, width:],
                router,
                attn_gain[:, None],
                expert_gain[:, None],
                jnp.zeros((router.shape[0], pad), bf16),
            ],
            axis=1,
        ),
    )
    query_weight = left[:, :width]
    proj_weight = left[:, width:]
    kv_weight = right[:, : 2 * width]
    router_all = right[:, 2 * width : 2 * width + experts]
    gains = right[:, 2 * width + experts : 2 * width + experts + 2].astype(f32)
    attn_scale = gains[:, 0]
    expert_scale = gains[:, 1]
    expert_weights = [pair_rows(w[0]) for w in (expert_up, expert_down)]

    distance = jnp.arange(2 * TILE, dtype=jnp.int32)
    hot_bucket = (
        bucket_of(distance)[None, :] == jnp.arange(buckets, dtype=jnp.int32)[:, None]
    ).astype(f32)
    by_distance = jnp.sum(
        position_bias.astype(f32)[:, :, None] * hot_bucket[None], axis=1
    ) - position_bias.astype(f32)[:, buckets - 1 :]
    close = jnp.where(distance < TILE, by_distance, MASKED)
    beside = jnp.roll(by_distance, -TILE, axis=1)
    bias_rows = jnp.stack([close, beside], axis=1).reshape(PAIRS, 4, 2 * TILE)

    def norm_stats(values):
        return lax.rsqrt(jnp.mean(values * values, axis=-1, keepdims=True) + epsilon)

    state = []
    for b in range(batches):
        rows = inputs[b, 0].astype(f32)
        inv_one = norm_stats(rows)
        normed = (rows * inv_one * attn_scale).astype(bf16)
        kv = mm(normed, kv_weight, ((1,), (0,))).astype(bf16)
        queries = mm(normed, query_weight, ((1,), (0,))).astype(bf16)
        docs = doc_ids[b, 0].astype(f32)
        padded = jnp.concatenate([jnp.full((BACK,), -1.0, f32), docs])
        key_docs = lax.dynamic_slice_in_dim(padded, me * length, BACK + length)
        query_docs = key_docs[BACK:]
        if ways == 2:
            kv_back = lax.ppermute(kv, "ctx", [(0, 1)])
        else:
            every = lax.all_gather(kv, "ctx", axis=0, tiled=True)
            every = jnp.concatenate([jnp.zeros((BACK, 2 * width), bf16), every], axis=0)
            kv_back = lax.dynamic_slice_in_dim(every, me * length, BACK, 0)
        firsts = query_docs[::TILE]
        start = jnp.sum((key_docs[None, :] < firsts[:, None]).astype(jnp.int32), axis=1)
        tiles = jnp.arange(length // TILE, dtype=jnp.int32) + SPAN - start // TILE
        tiles = jnp.clip(tiles, 1, SPAN)
        view = (tiles, queries, kv, kv_back, query_docs[None], key_docs[None], bias_rows)
        state.append(dict(rows=rows, inv_one=inv_one, normed=normed, view=view))

    cot_sent = jnp.concatenate([dispatch(b, cots[b]) for b in range(batches)], axis=1)
    cot_here = cross(after(cot_sent, *begun))
    sent = ()
    for b, s in enumerate(state):
        s["view"] = (after(s["view"][0], *sent),) + s["view"][1:]
        attended, lse = attend(*s["view"])
        hidden = s["rows"] + mm(attended, proj_weight, ((1,), (0,)))
        inv_two = norm_stats(hidden)
        shared = (hidden * inv_two * expert_scale).astype(bf16)
        logits = mm(shared, router_all, ((1,), (0,)))
        hot = hots[b]
        chosen = jnp.sum(jnp.where(hot, logits[:, None, :], 0.0), axis=2)
        gate_exp = jnp.exp(chosen - jnp.max(chosen, axis=1, keepdims=True))
        gates = gate_exp / jnp.sum(gate_exp, axis=1, keepdims=True)
        gate_slots = sum(
            jnp.sum(jnp.where(holds[b][k], gates[None, :, k], 0.0), axis=1) for k in range(top)
        ).reshape(experts, 1, room)
        gate_slots = jnp.pad(gate_slots, ((0, 0), (0, 0), (0, TILE - room)))
        gate_high = gate_slots.astype(bf16)
        gate_low = (gate_slots - gate_high.astype(f32)).astype(bf16)
        gate_row = jnp.concatenate(
            [gate_high, gate_low, jnp.zeros((experts, 1, width - 2 * TILE), bf16)], axis=2
        )
        at_gate = lax.broadcasted_iota(jnp.int32, (1, room, 1), 1) == capacity
        sent = (jnp.where(at_gate, gate_row, dispatch(b, shared)),)
        s.update(attended=attended, lse=lse, hidden=hidden, inv_two=inv_two, shared=shared,
                 gates=gates, sent=sent[0])

    made = ()
    last = (cot_here, *(s["sent"] for s in state))
    for s in state:
        s["here"] = cross(after(s["sent"], *last))
        last = (s["here"],)
    for b, s in enumerate(state):
        y, back, *sums = run_experts(
            me[None].astype(jnp.int32), s["here"], cot_here, b, *expert_weights, made, capacity,
            ways == 2, ways == 2 and b == batches - 1,
        )
        made = (y, *sums)
        s["back"] = cross(after(back, *last))
        last = (s["back"],)
    results = cross(after(y, *last))
    if ways == 2:
        up_share, down_share = (
            (mine + swap(theirs, "ctx", 1).astype(f32))[None]
            for mine, theirs in zip(sums[::2], sums[1::2])
        )
    else:
        up_share, down_share = (
            lax.psum_scatter(g.astype(bf16), "ctx", scatter_dimension=0, tiled=True).astype(f32)[None]
            for g in sums
        )

    input_grads = []
    parts = []
    picks = []
    before = ()
    for b, s in enumerate(state):
        upstream = cots[b].astype(f32)
        packet = after(s["back"], *before)
        dots = packet[:, capacity, : 2 * TILE].astype(f32)
        dots = (dots[:, :room] + dots[:, TILE : TILE + room]).reshape(1, slots)
        slot = slot_of[b]
        pick = [slot[:, k : k + 1] == slot_rows[None, :] for k in range(top)]
        picks.append(functools.reduce(jnp.logical_or, pick).astype(bf16))
        scaled = jnp.stack([jnp.sum(jnp.where(p, dots, 0.0), axis=1) for p in pick], axis=1)
        chosen_grad = scaled - s["gates"] * jnp.sum(scaled, axis=1, keepdims=True)
        logit_grad = jnp.sum(jnp.where(hots[b], chosen_grad[:, :, None], 0.0), axis=1).astype(bf16)
        shared_grad = mm(picks[b], packet.reshape(slots, width), ((1,), (0,)))
        shared_grad = shared_grad + mm(logit_grad, router_all, ((1,), (1,)))
        unit = s["hidden"] * s["inv_two"]
        grad_expert = jnp.sum(shared_grad * unit, axis=0)
        inner = shared_grad * expert_scale
        hidden_grad = upstream + s["inv_two"] * (
            inner - unit * jnp.mean(inner * unit, axis=1, keepdims=True)
        )
        branch_grad = hidden_grad.astype(bf16)
        attended_grad = mm(branch_grad, proj_weight, ((1,), (1,))).astype(bf16)
        dq, own, back, near = attend_back(*s["view"], s["attended"], attended_grad, s["lse"])
        before = (dq,)
        if ways == 2:
            got = lax.ppermute(back, "ctx", [(1, 0)])
        else:
            every = jnp.zeros((2, BACK + seq_len, width), bf16)
            every = lax.dynamic_update_slice_in_dim(every, back, me * length, 1)
            got = lax.psum_scatter(every[:, BACK:], "ctx", scatter_dimension=1, tiled=True)
        both = (own.astype(f32) + got.astype(f32)).astype(bf16)
        dkv = jnp.concatenate([both[0], both[1]], axis=1)
        normed = s["normed"]
        normed_grad = mm(dq, query_weight, ((1,), (1,))) + mm(dkv, kv_weight, ((1,), (1,)))
        unit = s["rows"] * s["inv_one"]
        grad_attn = jnp.sum(normed_grad * unit, axis=0)
        inner = normed_grad * attn_scale
        input_part = s["inv_one"] * (inner - unit * jnp.mean(inner * unit, axis=1, keepdims=True))
        input_grads.append((hidden_grad + input_part).astype(bf16))
        parts.append((near, grad_attn, grad_expert))
        s.update(dq=dq, dkv=dkv, branch_grad=branch_grad, logit_grad=logit_grad)

    outputs = []
    for b, s in enumerate(state):
        mine = results[:, b * room : (b + 1) * room].reshape(slots, width)
        outputs.append((s["hidden"] + mm(picks[b], mine, ((1,), (0,)))).astype(bf16))

    near, grad_attn, grad_expert = (functools.reduce(jnp.add, p) for p in zip(*parts))

    def weight_grads(rows):
        def total(left, right):
            return functools.reduce(
                jnp.add, [mm(rows(s[left], 1), s[right], ((0,), (0,))) for s in state]
            )

        small = total("shared", "logit_grad")
        return (
            jnp.concatenate([total("normed", "dq"), total("attended", "branch_grad")], axis=1),
            jnp.concatenate(
                [
                    total("normed", "dkv"),
                    small,
                    rows(grad_attn, 0)[:, None],
                    rows(grad_expert, 0)[:, None],
                    jnp.zeros((small.shape[0], pad), f32),
                ],
                axis=1,
            ),
        )

    hot_near = jnp.where(
        jnp.arange(buckets)[:, None] < buckets - 1, hot_bucket[:, :TILE], 0.0
    )
    grad_bias = jnp.sum(near.reshape(HEADS, 1, TILE) * hot_near[None], axis=2)
    far = jnp.where(jnp.arange(buckets) == buckets - 1, 1.0, 0.0)
    grad_bias = grad_bias - jnp.sum(grad_bias, axis=1, keepdims=True) * far
    left, right, bias_total = scatter_sum(weight_grads, width, results, grad_bias)
    return (
        jnp.stack(outputs)[:, None],
        jnp.stack(input_grads)[:, None],
        jnp.concatenate([left[:, :width], right[:, : 2 * width]], axis=1),
        left[:, width:],
        right[:, 2 * width : 2 * width + experts],
        right[:, 2 * width + experts],
        right[:, 2 * width + experts + 1],
        bias_total,
        up_share,
        down_share,
    )


def solution(mesh):
    placed = (
        P(None, "exp", "ctx", None),
        P(None, "exp", "ctx", None),
        P(None, "exp", None),
        P(None, "exp", "ctx", None),
        P(("ctx", "exp"), None),
        P(("ctx", "exp"), None),
        P(("ctx", "exp"), None),
        P(("ctx", "exp")),
        P(("ctx", "exp")),
        P(),
        P("exp", "ctx", None),
        P("exp", "ctx", None),
    )
    return jax.shard_map(
        shards,
        mesh=mesh,
        in_specs=placed,
        out_specs=(
            P(None, "exp", "ctx", None),
            P(None, "exp", "ctx", None),
            P(("ctx", "exp"), None),
            P(("ctx", "exp"), None),
            P(("ctx", "exp"), None),
            P(("ctx", "exp")),
            P(("ctx", "exp")),
            P(),
            P("exp", "ctx", None),
            P("exp", "ctx", None),
        ),
        check_vma=False,
    )
```

```python
import functools
import math

import jax
import jax.numpy as jnp
from jax import lax
from jax.experimental import pallas as pl
from jax.experimental.pallas import tpu as pltpu
from jax.sharding import PartitionSpec as P

HEADS = 12
HEAD = 64
PAIRS = HEADS // 2
GROUP = 3
TILE = 128
BACK = 512
SPAN = BACK // TILE + 1
MASKED = -1000000000.0

epsilon = 1e-06
thresholds = (19, 21, 24, 27, 31, 35, 40, 46, 52, 59, 67, 77, 87, 99, 113)
bf16 = jnp.bfloat16
f32 = jnp.float32


def bucket_of(distance):
    distance = jnp.maximum(distance, 0)
    beyond = jnp.zeros_like(distance)
    for threshold in thresholds:
        beyond = beyond + (distance >= threshold).astype(jnp.int32)
    return jnp.where(distance < 16, distance, 16 + beyond)


def mm(a, b, dims):
    return lax.dot_general(a, b, (dims, ((), ())), preferred_element_type=f32)


def stack_heads(rows):
    lane = lax.broadcasted_iota(jnp.int32, rows.shape, 1)
    zero = jnp.zeros_like(rows)
    return jnp.concatenate(
        [jnp.where(lane < HEAD, rows, zero), jnp.where(lane >= HEAD, rows, zero)], axis=0
    )


def fold_heads(wide):
    return jnp.concatenate([wide[:HEAD, :TILE], wide[HEAD:, TILE:]], axis=0)


def fill_mask(mask, qd_ref, kd_ref):
    for qi in range(qd_ref.shape[1] // TILE):
        docs_row = qd_ref[:, qi * TILE : (qi + 1) * TILE]
        for j in range(SPAN):
            kt = (qi + j) * TILE
            column = jnp.broadcast_to(kd_ref[:, kt : kt + TILE], (TILE, TILE)).T
            mask[qi, j * TILE : (j + 1) * TILE, :] = jnp.where(
                column == docs_row, 0.0, MASKED
            ).astype(f32)


def fill_bias(bias, bv_ref):
    for g in range(GROUP):
        for head in range(2):
            for d in range(2):
                row = bv_ref[g, 2 * head + d : 2 * head + d + 1, :]
                rolled = pltpu.roll(
                    jnp.broadcast_to(row, (TILE, 2 * TILE)), 0, 1, stride=1, stride_axis=0
                )
                bias[g, d, :, head * TILE : (head + 1) * TILE] = rolled[:, :TILE]


def lanes_of(g):
    return slice(g * TILE, (g + 1) * TILE)


def masked_scores(scores, mask, bias, g, qi, tiles):
    parts = []
    for j in range(tiles):
        d = tiles - 1 - j
        off = (SPAN - tiles + j) * TILE
        m = mask[qi, off : off + TILE, :]
        x = scores[j * TILE : (j + 1) * TILE] + jnp.concatenate([m, m], axis=1)
        if d < 2:
            x = x + bias[g, d]
        parts.append(x)
    return parts


def transpose_tiles(out, at, rows_ref):
    for g in range(GROUP):
        for t in range(0, rows_ref.shape[0], TILE):
            out[g, :, at + t : at + t + TILE] = rows_ref[t : t + TILE, lanes_of(g)].T


def fwd_kernel(tiles, q_ref, k_ref, v_ref, kp_ref, vp_ref, qd_ref, kd_ref, bv_ref, o_ref, lse_ref,
               kwin, vwin_t, bias, mask):
    @pl.when(pl.program_id(0) == 0)
    def _():
        fill_mask(mask, qd_ref, kd_ref)

    fill_bias(bias, bv_ref)
    kwin[:BACK] = kp_ref[...]
    kwin[BACK:] = k_ref[...]
    transpose_tiles(vwin_t, 0, vp_ref)
    transpose_tiles(vwin_t, BACK, v_ref)
    groups = range(GROUP)

    def step(qi, carry):
        q0 = pl.multiple_of(qi * TILE, TILE)
        q2 = [stack_heads(q_ref[pl.ds(q0, TILE), lanes_of(g)] * 0.125) for g in groups]

        def branch(count):
            def go():
                lo = pl.multiple_of((qi + SPAN - count) * TILE, TILE)
                rows = pl.ds(lo, count * TILE)
                raw = [mm(kwin[rows, lanes_of(g)], q2[g], ((1,), (1,))) for g in groups]
                lows, tops, totals = [], [], []
                for g in groups:
                    parts = masked_scores(raw[g], mask, bias, g, qi, count)
                    top = functools.reduce(jnp.maximum, parts)
                    top = jnp.max(top, axis=0, keepdims=True)
                    probs = [jnp.exp(x - top) for x in parts]
                    totals.append(
                        jnp.sum(functools.reduce(jnp.add, probs), axis=0, keepdims=True)
                    )
                    tops.append(top)
                    lows.append(jnp.concatenate([p.astype(bf16) for p in probs], axis=0))
                outs = [mm(vwin_t[g, :, rows], lows[g], ((1,), (0,))) for g in groups]
                row = lax.broadcasted_iota(jnp.int32, (TILE, TILE), 0)
                for g in groups:
                    inv = 1.0 / totals[g]
                    out = fold_heads(outs[g]) * jnp.where(
                        row < HEAD, inv[:, :TILE], inv[:, TILE:]
                    )
                    o_ref[pl.ds(q0, TILE), lanes_of(g)] = out.T.astype(bf16)
                    lse_ref[g, pl.ds(qi, 1), :] = tops[g] + jnp.log(totals[g])
                return 0

            return go

        lax.switch(tiles[qi] - 1, [branch(c) for c in range(1, SPAN + 1)])
        return carry

    lax.fori_loop(0, q_ref.shape[0] // TILE, step, 0)


def bwd_kernel(tiles, q_ref, k_ref, v_ref, kp_ref, vp_ref, qd_ref, kd_ref, bv_ref, o_ref, do_ref,
               lse_ref, dq_ref, own_ref, back_ref, near_ref,
               kwin, kwin_t, vwin, dk, dv, near, bias, mask):
    @pl.when(pl.program_id(0) == 0)
    def _():
        fill_mask(mask, qd_ref, kd_ref)

    fill_bias(bias, bv_ref)
    kwin[:BACK] = kp_ref[...]
    kwin[BACK:] = k_ref[...]
    vwin[:BACK] = vp_ref[...]
    vwin[BACK:] = v_ref[...]
    transpose_tiles(kwin_t, 0, kp_ref)
    transpose_tiles(kwin_t, BACK, k_ref)
    dk[...] = jnp.zeros_like(dk)
    dv[...] = jnp.zeros_like(dv)
    near[...] = jnp.zeros_like(near)
    groups = range(GROUP)

    def step(qi, carry):
        q0 = pl.multiple_of(qi * TILE, TILE)
        q2, do2, lse, delta = [], [], [], []
        for g in groups:
            q2.append(stack_heads(q_ref[pl.ds(q0, TILE), lanes_of(g)] * 0.125))
            do = do_ref[pl.ds(q0, TILE), lanes_of(g)]
            do2.append(stack_heads(do))
            lse.append(lse_ref[g, pl.ds(qi, 1), :])
            prod = (do.astype(f32) * o_ref[pl.ds(q0, TILE), lanes_of(g)].astype(f32)).T
            delta.append(
                jnp.concatenate(
                    [jnp.sum(prod[:HEAD], axis=0, keepdims=True),
                     jnp.sum(prod[HEAD:], axis=0, keepdims=True)],
                    axis=1,
                )
            )

        def branch(count):
            def go():
                lo = pl.multiple_of((qi + SPAN - count) * TILE, TILE)
                rows = pl.ds(lo, count * TILE)
                raw = [mm(kwin[rows, lanes_of(g)], q2[g], ((1,), (1,))) for g in groups]
                prob_grad = [mm(vwin[rows, lanes_of(g)], do2[g], ((1,), (1,))) for g in groups]
                low, score_grad = [], []
                for g in groups:
                    parts = masked_scores(raw[g], mask, bias, g, qi, count)
                    lows, grads = [], []
                    for j in range(count):
                        prob = jnp.exp(parts[j] - lse[g])
                        grad = prob * (prob_grad[g][j * TILE : (j + 1) * TILE] - delta[g])
                        if j == count - 1:
                            near[g] += grad
                        elif j == count - 2:
                            r = lax.broadcasted_iota(jnp.int32, grad.shape, 0)
                            c = lax.broadcasted_iota(jnp.int32, grad.shape, 1)
                            c = jnp.where(c >= TILE, c - TILE, c)
                            near[g] += jnp.where(c < r, grad, 0.0)
                        lows.append(prob.astype(bf16))
                        grads.append(grad.astype(bf16))
                    low.append(jnp.concatenate(lows, axis=0))
                    score_grad.append(jnp.concatenate(grads, axis=0))
                for g in groups:
                    dv[rows, lanes_of(g)] += mm(low[g], do2[g], ((1,), (0,)))
                    dk[rows, lanes_of(g)] += mm(score_grad[g], q2[g], ((1,), (0,)))
                for g in groups:
                    dq = fold_heads(mm(kwin_t[g, :, rows], score_grad[g], ((1,), (0,))))
                    dq_ref[pl.ds(q0, TILE), lanes_of(g)] = (dq.T * 0.125).astype(bf16)
                return 0

            return go

        lax.switch(tiles[qi] - 1, [branch(c) for c in range(1, SPAN + 1)])
        return carry

    lax.fori_loop(0, q_ref.shape[0] // TILE, step, 0)
    for i, total in enumerate((dk, dv)):
        back_ref[i] = total[:BACK].astype(bf16)
        own_ref[i] = total[BACK:].astype(bf16)
    for g in groups:
        for head in range(2):
            turned = near[g, :, lanes_of(head)]
            r = lax.broadcasted_iota(jnp.int32, turned.shape, 0)
            bit = 1
            while bit < TILE:
                turned = jnp.where((r & bit) > 0, pltpu.roll(turned, TILE - bit, 1), turned)
                bit *= 2
            near_ref[g, :, lanes_of(head)] = jnp.sum(turned, axis=0, keepdims=True)


def attention_specs(length):
    full = lambda p, *_: (0, 0)
    lanes = lambda off: (lambda p, *_: (0, p + off))
    return [
        pl.BlockSpec((length, GROUP * TILE), lanes(0)),
        pl.BlockSpec((length, GROUP * TILE), lanes(0)),
        pl.BlockSpec((length, GROUP * TILE), lanes(PAIRS // GROUP)),
        pl.BlockSpec((BACK, GROUP * TILE), lanes(0)),
        pl.BlockSpec((BACK, GROUP * TILE), lanes(PAIRS // GROUP)),
        pl.BlockSpec((1, length), full),
        pl.BlockSpec((1, BACK + length), full),
        pl.BlockSpec((GROUP, 4, 2 * TILE), lambda p, *_: (p, 0, 0)),
    ]


def attend(tiles, queries, kv, kv_back, query_docs, key_docs, bias_rows):
    length = queries.shape[0]
    width = HEADS * HEAD
    blocks = length // TILE
    return pl.pallas_call(
        fwd_kernel,
        grid_spec=pltpu.PrefetchScalarGridSpec(
            num_scalar_prefetch=1,
            grid=(PAIRS // GROUP,),
            in_specs=attention_specs(length),
            out_specs=[
                pl.BlockSpec((length, GROUP * TILE), lambda p, *_: (0, p)),
                pl.BlockSpec((GROUP, blocks, 2 * TILE), lambda p, *_: (p, 0, 0)),
            ],
            scratch_shapes=[
                pltpu.VMEM((BACK + length, GROUP * TILE), bf16),
                pltpu.VMEM((GROUP, TILE, BACK + length), bf16),
                pltpu.VMEM((GROUP, 2, TILE, 2 * TILE), f32),
                pltpu.VMEM((blocks, SPAN * TILE, TILE), f32),
            ],
        ),
        out_shape=[
            jax.ShapeDtypeStruct((length, width), bf16),
            jax.ShapeDtypeStruct((PAIRS, blocks, 2 * TILE), f32),
        ],
        compiler_params=pltpu.CompilerParams(vmem_limit_bytes=32 * 2**20),
        cost_estimate=pl.CostEstimate(
            flops=4 * 2 * HEADS * length * BACK * 128, bytes_accessed=6 * 2**20,
            transcendentals=HEADS * length * BACK,
        ),
        name="attend",
    )(tiles, queries, kv, kv, kv_back, kv_back, query_docs, key_docs, bias_rows)


def attend_back(tiles, queries, kv, kv_back, query_docs, key_docs, bias_rows, out, out_grad, lse):
    length = queries.shape[0]
    width = HEADS * HEAD
    blocks = length // TILE
    own = pl.BlockSpec((length, GROUP * TILE), lambda p, *_: (0, p))
    both = lambda n: pl.BlockSpec((2, n, GROUP * TILE), lambda p, *_: (0, 0, p))
    return pl.pallas_call(
        bwd_kernel,
        grid_spec=pltpu.PrefetchScalarGridSpec(
            num_scalar_prefetch=1,
            grid=(PAIRS // GROUP,),
            in_specs=attention_specs(length)
            + [own, own, pl.BlockSpec((GROUP, blocks, 2 * TILE), lambda p, *_: (p, 0, 0))],
            out_specs=[own, both(length), both(BACK),
                       pl.BlockSpec((GROUP, 1, 2 * TILE), lambda p, *_: (p, 0, 0))],
            scratch_shapes=[
                pltpu.VMEM((BACK + length, GROUP * TILE), bf16),
                pltpu.VMEM((GROUP, TILE, BACK + length), bf16),
                pltpu.VMEM((BACK + length, GROUP * TILE), bf16),
                pltpu.VMEM((BACK + length, GROUP * TILE), f32),
                pltpu.VMEM((BACK + length, GROUP * TILE), f32),
                pltpu.VMEM((GROUP, TILE, 2 * TILE), f32),
                pltpu.VMEM((GROUP, 2, TILE, 2 * TILE), f32),
                pltpu.VMEM((blocks, SPAN * TILE, TILE), f32),
            ],
        ),
        out_shape=[
            jax.ShapeDtypeStruct((length, width), bf16),
            jax.ShapeDtypeStruct((2, length, width), bf16),
            jax.ShapeDtypeStruct((2, BACK, width), bf16),
            jax.ShapeDtypeStruct((PAIRS, 1, 2 * TILE), f32),
        ],
        compiler_params=pltpu.CompilerParams(vmem_limit_bytes=32 * 2**20),
        cost_estimate=pl.CostEstimate(
            flops=2**20, bytes_accessed=2**20, transcendentals=0,
        ),
        name="attend_back",
    )(tiles, queries, kv, kv, kv_back, kv_back, query_docs, key_docs, bias_rows, out, out_grad, lse)


GELU_A = 0.7978845608028654
GELU_B = 0.044715


def expert_kernel(more, halves, split, capacity, room, chunk, ctx, x_ref, cot_ref, up_ref, down_ref, *refs):
    refs = list(refs)
    take = lambda n: [refs.pop(0) for _ in range(n)]
    if more:
        _, up_before, down_before = take(3)
    y_ref, back_ref = take(2)
    sums = take(4 if split else 2)
    y_sum, back_sum, x, result_grad, gate, act_all, pre_grad_all = take(7)
    rows, width = x.shape
    step = pl.program_id(0)
    pieces = 2 if halves else 1
    piece = width // pieces

    def columns(i):
        return pl.ds(pl.multiple_of((ctx[0] + i) % pieces * piece, TILE), piece)

    @pl.when(step == 0)
    def _():
        lane = lax.broadcasted_iota(jnp.int32, (1, TILE), 1)
        for e in range(rows // room):
            at = e * room
            for i in range(pieces):
                x[at : at + room, i * piece : (i + 1) * piece] = x_ref[e, :, columns(i)]
            line = x_ref[e, capacity : capacity + 1, : 2 * TILE].astype(f32)
            line = jnp.where(lane < capacity, line[:, :TILE] + line[:, TILE:], 0.0)
            column = jnp.broadcast_to(line, (TILE, TILE)).T[:room]
            gate[at : at + room, :] = column
            for c in range(0, width, TILE):
                result_grad[at : at + room, c : c + TILE] = (
                    cot_ref[e, :, c : c + TILE].astype(f32) * column
                ).astype(bf16)
        y_sum[...] = jnp.zeros_like(y_sum)
        back_sum[...] = jnp.zeros_like(back_sum)

    def part(i, carry):
        r = pl.ds(pl.multiple_of(i * chunk, chunk), chunk)
        pre = mm(x[r, :], up_ref[...], ((1,), (0,)))
        act_grad = mm(result_grad[r, :], down_ref[...], ((1,), (1,)))
        square = pre * pre
        half = 0.5 + 0.5 * jnp.tanh(pre * (GELU_A + (GELU_A * GELU_B) * square))
        act = (pre * half).astype(bf16)
        slope = 2.0 * GELU_A + (6.0 * GELU_A * GELU_B) * square
        pre_grad = (act_grad * (half * (1.0 + pre * (1.0 - half) * slope))).astype(bf16)
        act_all[r, :] = act
        pre_grad_all[r, :] = pre_grad
        y_sum[r, :] += mm(act, down_ref[...], ((1,), (0,)))
        back_sum[r, :] += mm(pre_grad, up_ref[...], ((1,), (1,)))
        return carry

    lax.fori_loop(0, rows // chunk, part, 0)

    def up_grad():
        grad = mm(x[...], pre_grad_all[...], ((0,), (0,)))
        return grad + up_before[...] if more else grad

    def down_grad():
        grad = mm(act_all[...], result_grad[...], ((0,), (0,)))
        return grad + down_before[...] if more else grad

    if split:
        mine, theirs, down_mine, down_theirs = sums
        early = step < pl.num_programs(0) // 2

        @pl.when(early)
        def _():
            down_mine[...] = down_grad()

        @pl.when(jnp.logical_not(early))
        def _():
            down_theirs[...] = down_grad().astype(bf16)

        grad = up_grad()
        mine[...] = grad[:piece]
        theirs[...] = grad[piece:].astype(bf16)
    else:
        sums[1][...] = down_grad()
        sums[0][...] = up_grad()

    @pl.when(step == pl.num_programs(0) - 1)
    def _():
        row = lax.broadcasted_iota(jnp.int32, (room, 1), 0)
        for e in range(rows // room):
            at = e * room
            dots = jnp.zeros((room, TILE), f32)
            for c in range(0, width, TILE):
                scaled = y_sum[at : at + room, c : c + TILE] * gate[at : at + room, :]
                y_ref[e, :, c : c + TILE] = scaled.astype(bf16)
                dots = dots + scaled * cot_ref[e, :, c : c + TILE].astype(f32)
            if room < TILE:
                dots = jnp.concatenate([dots, jnp.zeros((TILE - room, TILE), f32)], axis=0)
            line = jnp.sum(dots.T, axis=0, keepdims=True)
            high = line.astype(bf16).astype(f32)
            line = jnp.concatenate(
                [high, line - high, jnp.zeros((1, width - 2 * TILE), f32)], axis=1
            )
            for i in range(pieces):
                back_ref[e, :, columns(i)] = back_sum[
                    at : at + room, i * piece : (i + 1) * piece
                ].astype(bf16)
            back_ref[e] = jnp.where(row == capacity, line.astype(bf16), back_ref[e])


def run_experts(ctx, x, cot, batch, up, down, made, capacity, halves, split):
    sources, room, width = x.shape
    rows = sources * room
    hidden = up.shape[1]
    part = math.gcd(hidden // 2, 512)
    steps = hidden // part
    ahead = steps // 2 if halves else 0
    chunk = rows // 2 if rows % 32 == 0 else rows
    more = len(made) > 0
    once = pl.Buffered(1)
    columns = pl.BlockSpec((width, part), lambda t, c: (0, (t + c[0] * ahead) % steps))
    lines = pl.BlockSpec((part, width), lambda t, c: (t, 0))
    cot_rows = pl.BlockSpec((sources, room, width), lambda t, c: (0, batch, 0), pipeline_mode=once)
    whole = pl.BlockSpec((sources, room, width), lambda t, c: (0, 0, 0), pipeline_mode=once)
    if split:
        half = pl.BlockSpec((width // 2, part), lambda t, c: (0, (t + c[0] * ahead) % steps))
        sums = [
            (half, (width // 2, hidden), f32),
            (half, (width // 2, hidden), bf16),
            (pl.BlockSpec((part, width), lambda t, c: (jnp.minimum(t, ahead - 1), 0)),
             (hidden // 2, width), f32),
            (pl.BlockSpec((part, width), lambda t, c: (jnp.maximum(t - ahead, 0), 0)),
             (hidden // 2, width), bf16),
        ]
    else:
        sums = [(columns, up.shape, f32), (lines, down.shape, f32)]
    aliases = {5: 0} if split else {5: 0, 6: 2, 7: 3}
    return pl.pallas_call(
        functools.partial(expert_kernel, more, halves, split, capacity, room, chunk),
        grid_spec=pltpu.PrefetchScalarGridSpec(
            num_scalar_prefetch=1,
            grid=(steps,),
            in_specs=[whole, cot_rows, columns, lines]
            + ([pl.BlockSpec(memory_space=pl.ANY), columns, lines] if more else []),
            out_specs=[cot_rows, whole]
            + [spec for spec, _, _ in sums],
            scratch_shapes=[
                pltpu.VMEM((rows, width), f32),
                pltpu.VMEM((rows, width), f32),
                pltpu.VMEM((rows, width), bf16),
                pltpu.VMEM((rows, width), bf16),
                pltpu.VMEM((rows, TILE), f32),
                pltpu.VMEM((rows, part), bf16),
                pltpu.VMEM((rows, part), bf16),
            ]
        ),
        out_shape=[
            jax.ShapeDtypeStruct(cot.shape, bf16),
            jax.ShapeDtypeStruct((sources, room, width), bf16),
        ]
        + [jax.ShapeDtypeStruct(shape, kind) for _, shape, kind in sums],
        input_output_aliases=aliases if more else {},
        compiler_params=pltpu.CompilerParams(vmem_limit_bytes=60 * 2**20),
        cost_estimate=pl.CostEstimate(
            flops=18 * rows * width * hidden, bytes_accessed=40 * 2**20,
            transcendentals=rows * hidden,
        ),
        name="experts",
    )(ctx, x, cot, up, down, *made)


def bits_of(axis):
    return [1 << b for b in range(lax.axis_size(axis).bit_length() - 1)][::-1]


def power_of_two(axis):
    size = lax.axis_size(axis)
    return size & (size - 1) == 0


def swap(x, axis, bit):
    size = lax.axis_size(axis)
    return lax.ppermute(x, axis, [(i, i ^ bit) for i in range(size)])


def ordered(x, other, axis, bit):
    high = (lax.axis_index(axis) & bit) > 0
    return jnp.where(high, other, x), jnp.where(high, x, other)


def after(x, *others):
    return lax.optimization_barrier((x, *others))[0]


def gather_rows(left, right, beside):
    if not (power_of_two("ctx") and power_of_two("exp")):
        every = [lax.all_gather(x, ("ctx", "exp"), axis=0, tiled=True) for x in (left, right)]
        return [*every, beside(every), every]
    bits = bits_of("exp")
    last = bits[-2:]
    parts = [left, right]
    held = [x[None] for x in parts]
    for bit in bits[:-2]:
        got = [swap(h, "exp", bit) for h in held]
        held = [
            jnp.stack(ordered(h, g, "exp", bit), axis=1).reshape((-1,) + h.shape[1:])
            for h, g in zip(held, got)
        ]
    got = [swap(h, "exp", bit) for h, bit in zip(held, last)]
    held = [jnp.stack(ordered(h, g, "exp", bit), axis=1) for h, g, bit in zip(held, got, last)]
    made = beside(held)
    got = [after(swap(h, "exp", bit), made) for h, bit in zip(held, last[::-1])]
    held = [
        jnp.stack(ordered(h, g, "exp", bit), axis=at)
        for h, g, bit, at in zip(held, got, last[::-1], (2, 1))
    ]
    held = [h.reshape(-1, h.shape[-1]) for h in held]
    over_exp = held
    for bit in bits_of("ctx"):
        got = [swap(h, "ctx", bit) for h in held]
        held = [
            jnp.stack(ordered(h, g, "ctx", bit), axis=0).reshape(-1, h.shape[-1])
            for h, g in zip(held, got)
        ]
    return [*held, made, over_exp]


def pair_rows(x):
    if lax.axis_size("ctx") != 2:
        return lax.all_gather(x, "ctx", axis=0, tiled=True)
    return jnp.concatenate([x, swap(x, "ctx", 1)], axis=0)


def add_received(mine, got, even):
    column = lax.broadcasted_iota(jnp.int32, mine.shape, mine.ndim - 1)
    rounded = lax.reduce_precision(mine, 8, 7)
    return jnp.where(column < even, mine, rounded) + got.astype(f32)


def halve(x, axis, bit, dim, even):
    side = ((lax.axis_index(axis) & bit) > 0).astype(jnp.int32)
    mine = lax.dynamic_index_in_dim(x, side, dim, keepdims=False)
    theirs = lax.dynamic_index_in_dim(x, 1 - side, dim, keepdims=False)
    return add_received(mine, swap(theirs.astype(bf16), axis, bit), even)


def scatter_sum(grads, width, late, small):
    blocks = lax.axis_size("exp")
    part = width // 2
    depth = part // blocks
    if not (
        power_of_two("exp") and lax.axis_size("ctx") == 2 and blocks > 3
        and small.shape[0] <= depth and small.shape[1] <= TILE
    ):
        whole = grads(lambda x, axis: x)
        sums = [
            lax.psum_scatter(x, ("ctx", "exp"), scatter_dimension=0, tiled=True) for x in whole
        ]
        return [*sums, lax.psum(small, ("ctx", "exp"))]
    me = lax.axis_index("ctx")
    rows, columns = small.shape
    small = jnp.pad(small, ((0, depth - rows), (0, TILE - columns)))
    small = jnp.broadcast_to(small[None], (blocks, depth, TILE)).reshape(part, TILE)

    def half_of(side):
        left, right = grads(lambda x, axis: lax.dynamic_slice_in_dim(x, side * part, part, axis))
        return jnp.concatenate([left, small], axis=1), right

    theirs = half_of(1 - me)
    even = [theirs[0].shape[1] - TILE, theirs[1].shape[1]]
    got = [swap(x.astype(bf16), "ctx", 1) for x in theirs]
    mine = half_of(me)
    bits = bits_of("exp")
    held = [after(add_received(m, g, e), late) for m, g, e in zip(mine, got, even)]
    held = [h.reshape((-1, 2, 2, depth, h.shape[1])) for h in held]
    high, low = bits[-2:]
    held = [halve(held[0], "exp", high, 1, even[0]), halve(held[1], "exp", low, 2, even[1])]
    held = [halve(held[0], "exp", low, 1, even[0]), halve(held[1], "exp", high, 1, even[1])]
    for bit in bits[:-2][::-1]:
        held = [
            halve(h.reshape((-1, 2) + h.shape[1:]), "exp", bit, 1, e) for h, e in zip(held, even)
        ]
    left, right = (h.reshape(h.shape[-2:]) for h in held)
    return [left[:, : even[0]], right, left[:rows, even[0] : even[0] + columns]]


def shards(
    inputs,
    cotangent,
    doc_ids,
    routes,
    query_key_value_weight,
    output_projection_weight,
    router,
    attn_gain,
    expert_gain,
    position_bias,
    expert_up,
    expert_down,
):
    batches = inputs.shape[0]
    length = inputs.shape[2]
    width = inputs.shape[3]
    top = routes.shape[3]
    ways = lax.axis_size("ctx")
    experts = lax.axis_size("exp")
    capacity = max(2, top * length * 10 // (7 * experts))
    room = (capacity + 1 + 15) // 16 * 16
    slots = experts * room
    seq_len = doc_ids.shape[2]
    buckets = position_bias.shape[1]
    me = lax.axis_index("ctx")

    expert_ids = jnp.arange(experts, dtype=jnp.int32)
    slot_rows = jnp.arange(slots, dtype=jnp.int32)
    earlier = jnp.tril(jnp.ones((length, length), bf16), -1)
    hots, slot_of, holds, spreads = [], [], [], []
    cots = [cotangent[b, 0] for b in range(batches)]

    def dispatch(b, rows):
        sent = mm(spreads[b], rows, ((1,), (0,))).astype(bf16)
        return sent.reshape(experts, room, width)

    def cross(x):
        return lax.all_to_all(x, "exp", split_axis=0, concat_axis=0, tiled=True)

    def send_cotangents(held):
        ids = after(routes, *held)
        for b in range(batches):
            route_ids = ids[b, 0]
            hot = route_ids[:, :, None] == expert_ids[None, None, :]
            used = jnp.any(hot, axis=1)
            rank = mm(earlier, used.astype(bf16), ((1,), (0,))).astype(jnp.int32)
            slot = jnp.sum(jnp.where(hot, rank[:, None, :], 0), axis=2) + route_ids * room
            hold = [slot[None, :, k] == slot_rows[:, None] for k in range(top)]
            hots.append(hot)
            slot_of.append(slot)
            holds.append(hold)
            spreads.append(functools.reduce(jnp.logical_or, hold).astype(bf16))
        return jnp.concatenate([dispatch(b, cots[b]) for b in range(batches)], axis=1)

    pad = -(experts + 2) % 128
    left, right, cot_sent, over_exp = gather_rows(
        jnp.concatenate([query_key_value_weight[:, :width], output_projection_weight], axis=1),
        jnp.concatenate(
            [
                query_key_value_weight[:, width:],
                router,
                attn_gain[:, None],
                expert_gain[:, None],
                jnp.zeros((router.shape[0], pad), bf16),
            ],
            axis=1,
        ),
        send_cotangents,
    )
    query_weight = left[:, :width]
    proj_weight = left[:, width:]
    kv_weight = right[:, : 2 * width]
    router_all = right[:, 2 * width : 2 * width + experts]
    gains = right[:, 2 * width + experts : 2 * width + experts + 2].astype(f32)
    attn_scale = gains[:, 0]
    expert_scale = gains[:, 1]
    expert_weights = [pair_rows(w[0]) for w in (expert_up, expert_down)]

    distance = jnp.arange(2 * TILE, dtype=jnp.int32)
    hot_bucket = (
        bucket_of(distance)[None, :] == jnp.arange(buckets, dtype=jnp.int32)[:, None]
    ).astype(f32)
    by_distance = jnp.sum(
        position_bias.astype(f32)[:, :, None] * hot_bucket[None], axis=1
    ) - position_bias.astype(f32)[:, buckets - 1 :]
    close = jnp.where(distance < TILE, by_distance, MASKED)
    beside = jnp.roll(by_distance, -TILE, axis=1)
    bias_rows = jnp.stack([close, beside], axis=1).reshape(PAIRS, 4, 2 * TILE)

    def norm_stats(values):
        return lax.rsqrt(jnp.mean(values * values, axis=-1, keepdims=True) + epsilon)

    state = []
    for b in range(batches):
        rows = inputs[b, 0].astype(f32)
        inv_one = norm_stats(rows)
        normed = (rows * inv_one * attn_scale).astype(bf16)
        kv = mm(normed, kv_weight, ((1,), (0,))).astype(bf16)
        queries = mm(normed, query_weight, ((1,), (0,))).astype(bf16)
        docs = doc_ids[b, 0].astype(f32)
        padded = jnp.concatenate([jnp.full((BACK,), -1.0, f32), docs])
        key_docs = lax.dynamic_slice_in_dim(padded, me * length, BACK + length)
        query_docs = key_docs[BACK:]
        if ways == 2:
            kv_back = lax.ppermute(kv, "ctx", [(0, 1)])
        else:
            every = lax.all_gather(kv, "ctx", axis=0, tiled=True)
            every = jnp.concatenate([jnp.zeros((BACK, 2 * width), bf16), every], axis=0)
            kv_back = lax.dynamic_slice_in_dim(every, me * length, BACK, 0)
        firsts = query_docs[::TILE]
        start = jnp.sum((key_docs[None, :] < firsts[:, None]).astype(jnp.int32), axis=1)
        tiles = jnp.arange(length // TILE, dtype=jnp.int32) + SPAN - start // TILE
        tiles = jnp.clip(tiles, 1, SPAN)
        view = (tiles, queries, kv, kv_back, query_docs[None], key_docs[None], bias_rows)
        state.append(dict(rows=rows, inv_one=inv_one, normed=normed, view=view))

    cot_here = cross(after(cot_sent, *over_exp))
    sent = ()
    for b, s in enumerate(state):
        s["view"] = (after(s["view"][0], *sent),) + s["view"][1:]
        attended, lse = attend(*s["view"])
        hidden = s["rows"] + mm(attended, proj_weight, ((1,), (0,)))
        inv_two = norm_stats(hidden)
        shared = (hidden * inv_two * expert_scale).astype(bf16)
        logits = mm(shared, router_all, ((1,), (0,)))
        hot = hots[b]
        chosen = jnp.sum(jnp.where(hot, logits[:, None, :], 0.0), axis=2)
        gate_exp = jnp.exp(chosen - jnp.max(chosen, axis=1, keepdims=True))
        gates = gate_exp / jnp.sum(gate_exp, axis=1, keepdims=True)
        gate_slots = sum(
            jnp.sum(jnp.where(holds[b][k], gates[None, :, k], 0.0), axis=1) for k in range(top)
        ).reshape(experts, 1, room)
        gate_slots = jnp.pad(gate_slots, ((0, 0), (0, 0), (0, TILE - room)))
        gate_high = gate_slots.astype(bf16)
        gate_low = (gate_slots - gate_high.astype(f32)).astype(bf16)
        gate_row = jnp.concatenate(
            [gate_high, gate_low, jnp.zeros((experts, 1, width - 2 * TILE), bf16)], axis=2
        )
        at_gate = lax.broadcasted_iota(jnp.int32, (1, room, 1), 1) == capacity
        sent = (jnp.where(at_gate, gate_row, dispatch(b, shared)),)
        s.update(attended=attended, lse=lse, hidden=hidden, inv_two=inv_two, shared=shared,
                 gates=gates, sent=sent[0])

    made = ()
    last = (cot_here, *(s["sent"] for s in state))
    for s in state:
        s["here"] = cross(after(s["sent"], *last))
        last = (s["here"],)
    for b, s in enumerate(state):
        y, back, *sums = run_experts(
            me[None].astype(jnp.int32), s["here"], cot_here, b, *expert_weights, made, capacity,
            ways == 2, ways == 2 and b == batches - 1,
        )
        made = (y, *sums)
        s["back"] = cross(after(back, *last))
        last = (s["back"],)
    results = cross(after(y, *last))
    if ways == 2:
        up_share, down_share = (
            (mine + swap(theirs, "ctx", 1).astype(f32))[None]
            for mine, theirs in zip(sums[::2], sums[1::2])
        )
    else:
        up_share, down_share = (
            lax.psum_scatter(g.astype(bf16), "ctx", scatter_dimension=0, tiled=True).astype(f32)[None]
            for g in sums
        )

    input_grads = []
    parts = []
    picks = []
    before = ()
    for b, s in enumerate(state):
        upstream = cots[b].astype(f32)
        packet = after(s["back"], *before)
        dots = packet[:, capacity, : 2 * TILE].astype(f32)
        dots = (dots[:, :room] + dots[:, TILE : TILE + room]).reshape(1, slots)
        slot = slot_of[b]
        pick = [slot[:, k : k + 1] == slot_rows[None, :] for k in range(top)]
        picks.append(functools.reduce(jnp.logical_or, pick).astype(bf16))
        scaled = jnp.stack([jnp.sum(jnp.where(p, dots, 0.0), axis=1) for p in pick], axis=1)
        chosen_grad = scaled - s["gates"] * jnp.sum(scaled, axis=1, keepdims=True)
        logit_grad = jnp.sum(jnp.where(hots[b], chosen_grad[:, :, None], 0.0), axis=1).astype(bf16)
        shared_grad = mm(picks[b], packet.reshape(slots, width), ((1,), (0,)))
        shared_grad = shared_grad + mm(logit_grad, router_all, ((1,), (1,)))
        unit = s["hidden"] * s["inv_two"]
        grad_expert = jnp.sum(shared_grad * unit, axis=0)
        inner = shared_grad * expert_scale
        hidden_grad = upstream + s["inv_two"] * (
            inner - unit * jnp.mean(inner * unit, axis=1, keepdims=True)
        )
        branch_grad = hidden_grad.astype(bf16)
        attended_grad = mm(branch_grad, proj_weight, ((1,), (1,))).astype(bf16)
        dq, own, back, near = attend_back(*s["view"], s["attended"], attended_grad, s["lse"])
        before = (dq,)
        if ways == 2:
            got = lax.ppermute(back, "ctx", [(1, 0)])
        else:
            every = jnp.zeros((2, BACK + seq_len, width), bf16)
            every = lax.dynamic_update_slice_in_dim(every, back, me * length, 1)
            got = lax.psum_scatter(every[:, BACK:], "ctx", scatter_dimension=1, tiled=True)
        both = (own.astype(f32) + got.astype(f32)).astype(bf16)
        dkv = jnp.concatenate([both[0], both[1]], axis=1)
        normed = s["normed"]
        normed_grad = mm(dq, query_weight, ((1,), (1,))) + mm(dkv, kv_weight, ((1,), (1,)))
        unit = s["rows"] * s["inv_one"]
        grad_attn = jnp.sum(normed_grad * unit, axis=0)
        inner = normed_grad * attn_scale
        input_part = s["inv_one"] * (inner - unit * jnp.mean(inner * unit, axis=1, keepdims=True))
        input_grads.append((hidden_grad + input_part).astype(bf16))
        parts.append((near, grad_attn, grad_expert))
        s.update(dq=dq, dkv=dkv, branch_grad=branch_grad, logit_grad=logit_grad)

    outputs = []
    for b, s in enumerate(state):
        mine = results[:, b * room : (b + 1) * room].reshape(slots, width)
        outputs.append((s["hidden"] + mm(picks[b], mine, ((1,), (0,)))).astype(bf16))

    near, grad_attn, grad_expert = (functools.reduce(jnp.add, p) for p in zip(*parts))

    def weight_grads(rows):
        def total(left, right):
            return functools.reduce(
                jnp.add, [mm(rows(s[left], 1), s[right], ((0,), (0,))) for s in state]
            )

        small = total("shared", "logit_grad")
        return (
            jnp.concatenate([total("normed", "dq"), total("attended", "branch_grad")], axis=1),
            jnp.concatenate(
                [
                    total("normed", "dkv"),
                    small,
                    rows(grad_attn, 0)[:, None],
                    rows(grad_expert, 0)[:, None],
                    jnp.zeros((small.shape[0], pad), f32),
                ],
                axis=1,
            ),
        )

    hot_near = jnp.where(
        jnp.arange(buckets)[:, None] < buckets - 1, hot_bucket[:, :TILE], 0.0
    )
    grad_bias = jnp.sum(near.reshape(HEADS, 1, TILE) * hot_near[None], axis=2)
    far = jnp.where(jnp.arange(buckets) == buckets - 1, 1.0, 0.0)
    grad_bias = grad_bias - jnp.sum(grad_bias, axis=1, keepdims=True) * far
    left, right, bias_total = scatter_sum(weight_grads, width, results, grad_bias)
    return (
        jnp.stack(outputs)[:, None],
        jnp.stack(input_grads)[:, None],
        jnp.concatenate([left[:, :width], right[:, : 2 * width]], axis=1),
        left[:, width:],
        right[:, 2 * width : 2 * width + experts],
        right[:, 2 * width + experts],
        right[:, 2 * width + experts + 1],
        bias_total,
        up_share,
        down_share,
    )


def solution(mesh):
    placed = (
        P(None, "exp", "ctx", None),
        P(None, "exp", "ctx", None),
        P(None, "exp", None),
        P(None, "exp", "ctx", None),
        P(("ctx", "exp"), None),
        P(("ctx", "exp"), None),
        P(("ctx", "exp"), None),
        P(("ctx", "exp")),
        P(("ctx", "exp")),
        P(),
        P("exp", "ctx", None),
        P("exp", "ctx", None),
    )
    return jax.shard_map(
        shards,
        mesh=mesh,
        in_specs=placed,
        out_specs=(
            P(None, "exp", "ctx", None),
            P(None, "exp", "ctx", None),
            P(("ctx", "exp"), None),
            P(("ctx", "exp"), None),
            P(("ctx", "exp"), None),
            P(("ctx", "exp")),
            P(("ctx", "exp")),
            P(),
            P("exp", "ctx", None),
            P("exp", "ctx", None),
        ),
        check_vma=False,
    )
```

```python
import functools
import math

import jax
import jax.numpy as jnp
from jax import lax
from jax.experimental import pallas as pl
from jax.experimental.pallas import tpu as pltpu
from jax.sharding import PartitionSpec as P

HEADS = 12
HEAD = 64
PAIRS = HEADS // 2
GROUP = 3
TILE = 128
BACK = 512
SPAN = BACK // TILE + 1
MASKED = -1000000000.0

epsilon = 1e-06
thresholds = (19, 21, 24, 27, 31, 35, 40, 46, 52, 59, 67, 77, 87, 99, 113)
bf16 = jnp.bfloat16
f32 = jnp.float32


def bucket_of(distance):
    distance = jnp.maximum(distance, 0)
    beyond = jnp.zeros_like(distance)
    for threshold in thresholds:
        beyond = beyond + (distance >= threshold).astype(jnp.int32)
    return jnp.where(distance < 16, distance, 16 + beyond)


def mm(a, b, dims):
    return lax.dot_general(a, b, (dims, ((), ())), preferred_element_type=f32)


def stack_heads(rows):
    lane = lax.broadcasted_iota(jnp.int32, rows.shape, 1)
    zero = jnp.zeros_like(rows)
    return jnp.concatenate(
        [jnp.where(lane < HEAD, rows, zero), jnp.where(lane >= HEAD, rows, zero)], axis=0
    )


def fold_heads(wide):
    return jnp.concatenate([wide[:HEAD, :TILE], wide[HEAD:, TILE:]], axis=0)


def fill_mask(mask, qd_ref, kd_ref):
    for qi in range(qd_ref.shape[1] // TILE):
        docs_row = qd_ref[:, qi * TILE : (qi + 1) * TILE]
        for j in range(SPAN):
            kt = (qi + j) * TILE
            column = jnp.broadcast_to(kd_ref[:, kt : kt + TILE], (TILE, TILE)).T
            mask[qi, j * TILE : (j + 1) * TILE, :] = jnp.where(
                column == docs_row, 0.0, MASKED
            ).astype(f32)


def fill_bias(bias, bv_ref):
    for g in range(GROUP):
        for head in range(2):
            for d in range(2):
                row = bv_ref[g, 2 * head + d : 2 * head + d + 1, :]
                rolled = pltpu.roll(
                    jnp.broadcast_to(row, (TILE, 2 * TILE)), 0, 1, stride=1, stride_axis=0
                )
                bias[g, d, :, head * TILE : (head + 1) * TILE] = rolled[:, :TILE]


def lanes_of(g):
    return slice(g * TILE, (g + 1) * TILE)


def masked_scores(scores, mask, bias, g, qi, tiles):
    parts = []
    for j in range(tiles):
        d = tiles - 1 - j
        off = (SPAN - tiles + j) * TILE
        m = mask[qi, off : off + TILE, :]
        x = scores[j * TILE : (j + 1) * TILE] + jnp.concatenate([m, m], axis=1)
        if d < 2:
            x = x + bias[g, d]
        parts.append(x)
    return parts


def transpose_tiles(out, at, rows_ref):
    for g in range(GROUP):
        for t in range(0, rows_ref.shape[0], TILE):
            out[g, :, at + t : at + t + TILE] = rows_ref[t : t + TILE, lanes_of(g)].T


def fwd_kernel(tiles, q_ref, k_ref, v_ref, kp_ref, vp_ref, qd_ref, kd_ref, bv_ref, o_ref, lse_ref,
               kwin, vwin_t, bias, mask):
    @pl.when(pl.program_id(0) == 0)
    def _():
        fill_mask(mask, qd_ref, kd_ref)

    fill_bias(bias, bv_ref)
    kwin[:BACK] = kp_ref[...]
    kwin[BACK:] = k_ref[...]
    transpose_tiles(vwin_t, 0, vp_ref)
    transpose_tiles(vwin_t, BACK, v_ref)
    groups = range(GROUP)

    def step(qi, carry):
        q0 = pl.multiple_of(qi * TILE, TILE)
        q2 = [stack_heads(q_ref[pl.ds(q0, TILE), lanes_of(g)] * 0.125) for g in groups]

        def branch(count):
            def go():
                lo = pl.multiple_of((qi + SPAN - count) * TILE, TILE)
                rows = pl.ds(lo, count * TILE)
                raw = [mm(kwin[rows, lanes_of(g)], q2[g], ((1,), (1,))) for g in groups]
                lows, tops, totals = [], [], []
                for g in groups:
                    parts = masked_scores(raw[g], mask, bias, g, qi, count)
                    top = functools.reduce(jnp.maximum, parts)
                    top = jnp.max(top, axis=0, keepdims=True)
                    probs = [jnp.exp(x - top) for x in parts]
                    totals.append(
                        jnp.sum(functools.reduce(jnp.add, probs), axis=0, keepdims=True)
                    )
                    tops.append(top)
                    lows.append(jnp.concatenate([p.astype(bf16) for p in probs], axis=0))
                outs = [mm(vwin_t[g, :, rows], lows[g], ((1,), (0,))) for g in groups]
                row = lax.broadcasted_iota(jnp.int32, (TILE, TILE), 0)
                for g in groups:
                    inv = 1.0 / totals[g]
                    out = fold_heads(outs[g]) * jnp.where(
                        row < HEAD, inv[:, :TILE], inv[:, TILE:]
                    )
                    o_ref[pl.ds(q0, TILE), lanes_of(g)] = out.T.astype(bf16)
                    lse_ref[g, pl.ds(qi, 1), :] = tops[g] + jnp.log(totals[g])
                return 0

            return go

        lax.switch(tiles[qi] - 1, [branch(c) for c in range(1, SPAN + 1)])
        return carry

    lax.fori_loop(0, q_ref.shape[0] // TILE, step, 0)


def bwd_kernel(tiles, q_ref, k_ref, v_ref, kp_ref, vp_ref, qd_ref, kd_ref, bv_ref, o_ref, do_ref,
               lse_ref, dq_ref, own_ref, back_ref, near_ref,
               kwin, kwin_t, vwin, dk, dv, near, bias, mask):
    @pl.when(pl.program_id(0) == 0)
    def _():
        fill_mask(mask, qd_ref, kd_ref)

    fill_bias(bias, bv_ref)
    kwin[:BACK] = kp_ref[...]
    kwin[BACK:] = k_ref[...]
    vwin[:BACK] = vp_ref[...]
    vwin[BACK:] = v_ref[...]
    transpose_tiles(kwin_t, 0, kp_ref)
    transpose_tiles(kwin_t, BACK, k_ref)
    dk[...] = jnp.zeros_like(dk)
    dv[...] = jnp.zeros_like(dv)
    near[...] = jnp.zeros_like(near)
    groups = range(GROUP)

    def step(qi, carry):
        q0 = pl.multiple_of(qi * TILE, TILE)
        q2, do2, lse, delta = [], [], [], []
        for g in groups:
            q2.append(stack_heads(q_ref[pl.ds(q0, TILE), lanes_of(g)] * 0.125))
            do = do_ref[pl.ds(q0, TILE), lanes_of(g)]
            do2.append(stack_heads(do))
            lse.append(lse_ref[g, pl.ds(qi, 1), :])
            prod = (do.astype(f32) * o_ref[pl.ds(q0, TILE), lanes_of(g)].astype(f32)).T
            delta.append(
                jnp.concatenate(
                    [jnp.sum(prod[:HEAD], axis=0, keepdims=True),
                     jnp.sum(prod[HEAD:], axis=0, keepdims=True)],
                    axis=1,
                )
            )

        def branch(count):
            def go():
                lo = pl.multiple_of((qi + SPAN - count) * TILE, TILE)
                rows = pl.ds(lo, count * TILE)
                raw = [mm(kwin[rows, lanes_of(g)], q2[g], ((1,), (1,))) for g in groups]
                prob_grad = [mm(vwin[rows, lanes_of(g)], do2[g], ((1,), (1,))) for g in groups]
                low, score_grad = [], []
                for g in groups:
                    parts = masked_scores(raw[g], mask, bias, g, qi, count)
                    lows, grads = [], []
                    for j in range(count):
                        prob = jnp.exp(parts[j] - lse[g])
                        grad = prob * (prob_grad[g][j * TILE : (j + 1) * TILE] - delta[g])
                        if j == count - 1:
                            near[g] += grad
                        elif j == count - 2:
                            r = lax.broadcasted_iota(jnp.int32, grad.shape, 0)
                            c = lax.broadcasted_iota(jnp.int32, grad.shape, 1)
                            c = jnp.where(c >= TILE, c - TILE, c)
                            near[g] += jnp.where(c < r, grad, 0.0)
                        lows.append(prob.astype(bf16))
                        grads.append(grad.astype(bf16))
                    low.append(jnp.concatenate(lows, axis=0))
                    score_grad.append(jnp.concatenate(grads, axis=0))
                for g in groups:
                    dv[rows, lanes_of(g)] += mm(low[g], do2[g], ((1,), (0,)))
                    dk[rows, lanes_of(g)] += mm(score_grad[g], q2[g], ((1,), (0,)))
                for g in groups:
                    dq = fold_heads(mm(kwin_t[g, :, rows], score_grad[g], ((1,), (0,))))
                    dq_ref[pl.ds(q0, TILE), lanes_of(g)] = (dq.T * 0.125).astype(bf16)
                return 0

            return go

        lax.switch(tiles[qi] - 1, [branch(c) for c in range(1, SPAN + 1)])
        return carry

    lax.fori_loop(0, q_ref.shape[0] // TILE, step, 0)
    for i, total in enumerate((dk, dv)):
        back_ref[i] = total[:BACK].astype(bf16)
        own_ref[i] = total[BACK:].astype(bf16)
    for g in groups:
        for head in range(2):
            turned = near[g, :, lanes_of(head)]
            r = lax.broadcasted_iota(jnp.int32, turned.shape, 0)
            bit = 1
            while bit < TILE:
                turned = jnp.where((r & bit) > 0, pltpu.roll(turned, TILE - bit, 1), turned)
                bit *= 2
            near_ref[g, :, lanes_of(head)] = jnp.sum(turned, axis=0, keepdims=True)


def attention_specs(length):
    full = lambda p, *_: (0, 0)
    lanes = lambda off: (lambda p, *_: (0, p + off))
    return [
        pl.BlockSpec((length, GROUP * TILE), lanes(0)),
        pl.BlockSpec((length, GROUP * TILE), lanes(0)),
        pl.BlockSpec((length, GROUP * TILE), lanes(PAIRS // GROUP)),
        pl.BlockSpec((BACK, GROUP * TILE), lanes(0)),
        pl.BlockSpec((BACK, GROUP * TILE), lanes(PAIRS // GROUP)),
        pl.BlockSpec((1, length), full),
        pl.BlockSpec((1, BACK + length), full),
        pl.BlockSpec((GROUP, 4, 2 * TILE), lambda p, *_: (p, 0, 0)),
    ]


def attend(tiles, queries, kv, kv_back, query_docs, key_docs, bias_rows):
    length = queries.shape[0]
    width = HEADS * HEAD
    blocks = length // TILE
    return pl.pallas_call(
        fwd_kernel,
        grid_spec=pltpu.PrefetchScalarGridSpec(
            num_scalar_prefetch=1,
            grid=(PAIRS // GROUP,),
            in_specs=attention_specs(length),
            out_specs=[
                pl.BlockSpec((length, GROUP * TILE), lambda p, *_: (0, p)),
                pl.BlockSpec((GROUP, blocks, 2 * TILE), lambda p, *_: (p, 0, 0)),
            ],
            scratch_shapes=[
                pltpu.VMEM((BACK + length, GROUP * TILE), bf16),
                pltpu.VMEM((GROUP, TILE, BACK + length), bf16),
                pltpu.VMEM((GROUP, 2, TILE, 2 * TILE), f32),
                pltpu.VMEM((blocks, SPAN * TILE, TILE), f32),
            ],
        ),
        out_shape=[
            jax.ShapeDtypeStruct((length, width), bf16),
            jax.ShapeDtypeStruct((PAIRS, blocks, 2 * TILE), f32),
        ],
        compiler_params=pltpu.CompilerParams(vmem_limit_bytes=32 * 2**20),
        cost_estimate=pl.CostEstimate(
            flops=4 * 2 * HEADS * length * BACK * 128, bytes_accessed=6 * 2**20,
            transcendentals=HEADS * length * BACK,
        ),
        name="attend",
    )(tiles, queries, kv, kv, kv_back, kv_back, query_docs, key_docs, bias_rows)


def attend_back(tiles, queries, kv, kv_back, query_docs, key_docs, bias_rows, out, out_grad, lse):
    length = queries.shape[0]
    width = HEADS * HEAD
    blocks = length // TILE
    own = pl.BlockSpec((length, GROUP * TILE), lambda p, *_: (0, p))
    both = lambda n: pl.BlockSpec((2, n, GROUP * TILE), lambda p, *_: (0, 0, p))
    return pl.pallas_call(
        bwd_kernel,
        grid_spec=pltpu.PrefetchScalarGridSpec(
            num_scalar_prefetch=1,
            grid=(PAIRS // GROUP,),
            in_specs=attention_specs(length)
            + [own, own, pl.BlockSpec((GROUP, blocks, 2 * TILE), lambda p, *_: (p, 0, 0))],
            out_specs=[own, both(length), both(BACK),
                       pl.BlockSpec((GROUP, 1, 2 * TILE), lambda p, *_: (p, 0, 0))],
            scratch_shapes=[
                pltpu.VMEM((BACK + length, GROUP * TILE), bf16),
                pltpu.VMEM((GROUP, TILE, BACK + length), bf16),
                pltpu.VMEM((BACK + length, GROUP * TILE), bf16),
                pltpu.VMEM((BACK + length, GROUP * TILE), f32),
                pltpu.VMEM((BACK + length, GROUP * TILE), f32),
                pltpu.VMEM((GROUP, TILE, 2 * TILE), f32),
                pltpu.VMEM((GROUP, 2, TILE, 2 * TILE), f32),
                pltpu.VMEM((blocks, SPAN * TILE, TILE), f32),
            ],
        ),
        out_shape=[
            jax.ShapeDtypeStruct((length, width), bf16),
            jax.ShapeDtypeStruct((2, length, width), bf16),
            jax.ShapeDtypeStruct((2, BACK, width), bf16),
            jax.ShapeDtypeStruct((PAIRS, 1, 2 * TILE), f32),
        ],
        compiler_params=pltpu.CompilerParams(vmem_limit_bytes=32 * 2**20),
        cost_estimate=pl.CostEstimate(
            flops=2**20, bytes_accessed=2**20, transcendentals=0,
        ),
        name="attend_back",
    )(tiles, queries, kv, kv, kv_back, kv_back, query_docs, key_docs, bias_rows, out, out_grad, lse)


GELU_A = 0.7978845608028654
GELU_B = 0.044715


def expert_kernel(more, halves, split, capacity, room, chunk, ctx, x_ref, cot_ref, up_ref, down_ref, *refs):
    refs = list(refs)
    take = lambda n: [refs.pop(0) for _ in range(n)]
    if more:
        _, up_before, down_before = take(3)
    y_ref, back_ref = take(2)
    sums = take(4 if split else 2)
    y_sum, back_sum, x, result_grad, gate, act_all, pre_grad_all = take(7)
    rows, width = x.shape
    step = pl.program_id(0)
    pieces = 2 if halves else 1
    piece = width // pieces

    def columns(i):
        return pl.ds(pl.multiple_of((ctx[0] + i) % pieces * piece, TILE), piece)

    @pl.when(step == 0)
    def _():
        lane = lax.broadcasted_iota(jnp.int32, (1, TILE), 1)
        for e in range(rows // room):
            at = e * room
            for i in range(pieces):
                x[at : at + room, i * piece : (i + 1) * piece] = x_ref[e, :, columns(i)]
            line = x_ref[e, capacity : capacity + 1, : 2 * TILE].astype(f32)
            line = jnp.where(lane < capacity, line[:, :TILE] + line[:, TILE:], 0.0)
            column = jnp.broadcast_to(line, (TILE, TILE)).T[:room]
            gate[at : at + room, :] = column
            for c in range(0, width, TILE):
                result_grad[at : at + room, c : c + TILE] = (
                    cot_ref[e, :, c : c + TILE].astype(f32) * column
                ).astype(bf16)
        y_sum[...] = jnp.zeros_like(y_sum)
        back_sum[...] = jnp.zeros_like(back_sum)

    def part(i, carry):
        r = pl.ds(pl.multiple_of(i * chunk, chunk), chunk)
        pre = mm(x[r, :], up_ref[...], ((1,), (0,)))
        act_grad = mm(result_grad[r, :], down_ref[...], ((1,), (1,)))
        square = pre * pre
        half = 0.5 + 0.5 * jnp.tanh(pre * (GELU_A + (GELU_A * GELU_B) * square))
        act = (pre * half).astype(bf16)
        slope = 2.0 * GELU_A + (6.0 * GELU_A * GELU_B) * square
        pre_grad = (act_grad * (half * (1.0 + pre * (1.0 - half) * slope))).astype(bf16)
        act_all[r, :] = act
        pre_grad_all[r, :] = pre_grad
        y_sum[r, :] += mm(act, down_ref[...], ((1,), (0,)))
        back_sum[r, :] += mm(pre_grad, up_ref[...], ((1,), (1,)))
        return carry

    lax.fori_loop(0, rows // chunk, part, 0)

    def up_grad():
        grad = mm(x[...], pre_grad_all[...], ((0,), (0,)))
        return grad + up_before[...] if more else grad

    def down_grad():
        grad = mm(act_all[...], result_grad[...], ((0,), (0,)))
        return grad + down_before[...] if more else grad

    if split:
        mine, theirs, down_mine, down_theirs = sums
        early = step < pl.num_programs(0) // 2

        @pl.when(early)
        def _():
            down_mine[...] = down_grad()

        @pl.when(jnp.logical_not(early))
        def _():
            down_theirs[...] = down_grad().astype(bf16)

        grad = up_grad()
        mine[...] = grad[:piece]
        theirs[...] = grad[piece:].astype(bf16)
    else:
        sums[1][...] = down_grad()
        sums[0][...] = up_grad()

    @pl.when(step == pl.num_programs(0) - 1)
    def _():
        row = lax.broadcasted_iota(jnp.int32, (room, 1), 0)
        for e in range(rows // room):
            at = e * room
            dots = jnp.zeros((room, TILE), f32)
            for c in range(0, width, TILE):
                scaled = y_sum[at : at + room, c : c + TILE] * gate[at : at + room, :]
                y_ref[e, :, c : c + TILE] = scaled.astype(bf16)
                dots = dots + scaled * cot_ref[e, :, c : c + TILE].astype(f32)
            if room < TILE:
                dots = jnp.concatenate([dots, jnp.zeros((TILE - room, TILE), f32)], axis=0)
            line = jnp.sum(dots.T, axis=0, keepdims=True)
            high = line.astype(bf16).astype(f32)
            line = jnp.concatenate(
                [high, line - high, jnp.zeros((1, width - 2 * TILE), f32)], axis=1
            )
            for i in range(pieces):
                back_ref[e, :, columns(i)] = back_sum[
                    at : at + room, i * piece : (i + 1) * piece
                ].astype(bf16)
            back_ref[e] = jnp.where(row == capacity, line.astype(bf16), back_ref[e])


def run_experts(ctx, x, cot, batch, up, down, made, capacity, halves, split):
    sources, room, width = x.shape
    rows = sources * room
    hidden = up.shape[1]
    part = math.gcd(hidden // 2, 512)
    steps = hidden // part
    ahead = steps // 2 if halves else 0
    chunk = rows // 2 if rows % 32 == 0 else rows
    more = len(made) > 0
    once = pl.Buffered(1)
    columns = pl.BlockSpec((width, part), lambda t, c: (0, (t + c[0] * ahead) % steps))
    lines = pl.BlockSpec((part, width), lambda t, c: (t, 0))
    cot_rows = pl.BlockSpec((sources, room, width), lambda t, c: (0, batch, 0), pipeline_mode=once)
    whole = pl.BlockSpec((sources, room, width), lambda t, c: (0, 0, 0), pipeline_mode=once)
    if split:
        half = pl.BlockSpec((width // 2, part), lambda t, c: (0, (t + c[0] * ahead) % steps))
        sums = [
            (half, (width // 2, hidden), f32),
            (half, (width // 2, hidden), bf16),
            (pl.BlockSpec((part, width), lambda t, c: (jnp.minimum(t, ahead - 1), 0)),
             (hidden // 2, width), f32),
            (pl.BlockSpec((part, width), lambda t, c: (jnp.maximum(t - ahead, 0), 0)),
             (hidden // 2, width), bf16),
        ]
    else:
        sums = [(columns, up.shape, f32), (lines, down.shape, f32)]
    aliases = {5: 0} if split else {5: 0, 6: 2, 7: 3}
    return pl.pallas_call(
        functools.partial(expert_kernel, more, halves, split, capacity, room, chunk),
        grid_spec=pltpu.PrefetchScalarGridSpec(
            num_scalar_prefetch=1,
            grid=(steps,),
            in_specs=[whole, cot_rows, columns, lines]
            + ([pl.BlockSpec(memory_space=pl.ANY), columns, lines] if more else []),
            out_specs=[cot_rows, whole]
            + [spec for spec, _, _ in sums],
            scratch_shapes=[
                pltpu.VMEM((rows, width), f32),
                pltpu.VMEM((rows, width), f32),
                pltpu.VMEM((rows, width), bf16),
                pltpu.VMEM((rows, width), bf16),
                pltpu.VMEM((rows, TILE), f32),
                pltpu.VMEM((rows, part), bf16),
                pltpu.VMEM((rows, part), bf16),
            ]
        ),
        out_shape=[
            jax.ShapeDtypeStruct(cot.shape, bf16),
            jax.ShapeDtypeStruct((sources, room, width), bf16),
        ]
        + [jax.ShapeDtypeStruct(shape, kind) for _, shape, kind in sums],
        input_output_aliases=aliases if more else {},
        compiler_params=pltpu.CompilerParams(vmem_limit_bytes=60 * 2**20),
        cost_estimate=pl.CostEstimate(
            flops=18 * rows * width * hidden, bytes_accessed=40 * 2**20,
            transcendentals=rows * hidden,
        ),
        name="experts",
    )(ctx, x, cot, up, down, *made)


def bits_of(axis):
    return [1 << b for b in range(lax.axis_size(axis).bit_length() - 1)][::-1]


def power_of_two(axis):
    size = lax.axis_size(axis)
    return size & (size - 1) == 0


def swap(x, axis, bit):
    size = lax.axis_size(axis)
    return lax.ppermute(x, axis, [(i, i ^ bit) for i in range(size)])


def ordered(x, other, axis, bit):
    high = (lax.axis_index(axis) & bit) > 0
    return jnp.where(high, other, x), jnp.where(high, x, other)


def after(x, *others):
    return lax.optimization_barrier((x, *others))[0]


def gather_rows(left, right, beside):
    if not (power_of_two("ctx") and power_of_two("exp")):
        every = [lax.all_gather(x, ("ctx", "exp"), axis=0, tiled=True) for x in (left, right)]
        return [*every, beside(every), every]
    bits = bits_of("exp")
    last = bits[-2:]
    parts = [left, right]
    held = [x[None] for x in parts]
    for bit in bits[:-2]:
        got = [swap(h, "exp", bit) for h in held]
        held = [
            jnp.stack(ordered(h, g, "exp", bit), axis=1).reshape((-1,) + h.shape[1:])
            for h, g in zip(held, got)
        ]
    got = [swap(h, "exp", bit) for h, bit in zip(held, last)]
    held = [jnp.stack(ordered(h, g, "exp", bit), axis=1) for h, g, bit in zip(held, got, last)]
    made = beside(held)
    got = [after(swap(h, "exp", bit), made) for h, bit in zip(held, last[::-1])]
    held = [
        jnp.stack(ordered(h, g, "exp", bit), axis=at)
        for h, g, bit, at in zip(held, got, last[::-1], (2, 1))
    ]
    held = [h.reshape(-1, h.shape[-1]) for h in held]
    over_exp = held
    for bit in bits_of("ctx"):
        got = [swap(h, "ctx", bit) for h in held]
        held = [
            jnp.stack(ordered(h, g, "ctx", bit), axis=0).reshape(-1, h.shape[-1])
            for h, g in zip(held, got)
        ]
    return [*held, made, over_exp]


def pair_rows(x):
    if lax.axis_size("ctx") != 2:
        return lax.all_gather(x, "ctx", axis=0, tiled=True)
    return jnp.concatenate([x, swap(x, "ctx", 1)], axis=0)


def add_received(mine, got, even):
    column = lax.broadcasted_iota(jnp.int32, mine.shape, mine.ndim - 1)
    rounded = lax.reduce_precision(mine, 8, 7)
    return jnp.where(column < even, mine, rounded) + got.astype(f32)


def halve(x, axis, bit, dim, even):
    side = ((lax.axis_index(axis) & bit) > 0).astype(jnp.int32)
    mine = lax.dynamic_index_in_dim(x, side, dim, keepdims=False)
    theirs = lax.dynamic_index_in_dim(x, 1 - side, dim, keepdims=False)
    return add_received(mine, swap(theirs.astype(bf16), axis, bit), even)


def scatter_sum(grads, width, late, small):
    blocks = lax.axis_size("exp")
    part = width // 2
    depth = part // blocks
    if not (
        power_of_two("exp") and lax.axis_size("ctx") == 2 and blocks > 3
        and small.shape[0] <= depth and small.shape[1] <= TILE
    ):
        whole = grads(lambda x, axis: x)
        sums = [
            lax.psum_scatter(x, ("ctx", "exp"), scatter_dimension=0, tiled=True) for x in whole
        ]
        return [*sums, lax.psum(small, ("ctx", "exp"))]
    me = lax.axis_index("ctx")
    rows, columns = small.shape
    small = jnp.pad(small, ((0, depth - rows), (0, TILE - columns)))
    small = jnp.broadcast_to(small[None], (blocks, depth, TILE)).reshape(part, TILE)

    def half_of(side):
        left, right = grads(lambda x, axis: lax.dynamic_slice_in_dim(x, side * part, part, axis))
        return jnp.concatenate([left, small], axis=1), right

    theirs = half_of(1 - me)
    even = [theirs[0].shape[1] - TILE, theirs[1].shape[1]]
    got = [swap(x.astype(bf16), "ctx", 1) for x in theirs]
    mine = half_of(me)
    bits = bits_of("exp")
    held = [add_received(m, after(g, late), e) for m, g, e in zip(mine, got, even)]
    held = [h.reshape((-1, 2, 2, depth, h.shape[1])) for h in held]
    high, low = bits[-2:]
    held = [halve(held[0], "exp", high, 1, even[0]), halve(held[1], "exp", low, 2, even[1])]
    held = [halve(held[0], "exp", low, 1, even[0]), halve(held[1], "exp", high, 1, even[1])]
    for bit in bits[:-2][::-1]:
        held = [
            halve(h.reshape((-1, 2) + h.shape[1:]), "exp", bit, 1, e) for h, e in zip(held, even)
        ]
    left, right = (h.reshape(h.shape[-2:]) for h in held)
    return [left[:, : even[0]], right, left[:rows, even[0] : even[0] + columns]]


def shards(
    inputs,
    cotangent,
    doc_ids,
    routes,
    query_key_value_weight,
    output_projection_weight,
    router,
    attn_gain,
    expert_gain,
    position_bias,
    expert_up,
    expert_down,
):
    batches = inputs.shape[0]
    length = inputs.shape[2]
    width = inputs.shape[3]
    top = routes.shape[3]
    ways = lax.axis_size("ctx")
    experts = lax.axis_size("exp")
    capacity = max(2, top * length * 10 // (7 * experts))
    room = (capacity + 1 + 15) // 16 * 16
    slots = experts * room
    seq_len = doc_ids.shape[2]
    buckets = position_bias.shape[1]
    me = lax.axis_index("ctx")

    expert_ids = jnp.arange(experts, dtype=jnp.int32)
    slot_rows = jnp.arange(slots, dtype=jnp.int32)
    earlier = jnp.tril(jnp.ones((length, length), bf16), -1)
    hots, slot_of, holds, spreads = [], [], [], []
    cots = [cotangent[b, 0] for b in range(batches)]

    def dispatch(b, rows):
        sent = mm(spreads[b], rows, ((1,), (0,))).astype(bf16)
        return sent.reshape(experts, room, width)

    def cross(x):
        return lax.all_to_all(x, "exp", split_axis=0, concat_axis=0, tiled=True)

    def send_cotangents(held):
        ids = after(routes, *held)
        for b in range(batches):
            route_ids = ids[b, 0]
            hot = route_ids[:, :, None] == expert_ids[None, None, :]
            used = jnp.any(hot, axis=1)
            rank = mm(earlier, used.astype(bf16), ((1,), (0,))).astype(jnp.int32)
            slot = jnp.sum(jnp.where(hot, rank[:, None, :], 0), axis=2) + route_ids * room
            hold = [slot[None, :, k] == slot_rows[:, None] for k in range(top)]
            hots.append(hot)
            slot_of.append(slot)
            holds.append(hold)
            spreads.append(functools.reduce(jnp.logical_or, hold).astype(bf16))
        return jnp.concatenate([dispatch(b, cots[b]) for b in range(batches)], axis=1)

    pad = -(experts + 2) % 128
    left, right, cot_sent, over_exp = gather_rows(
        jnp.concatenate([query_key_value_weight[:, :width], output_projection_weight], axis=1),
        jnp.concatenate(
            [
                query_key_value_weight[:, width:],
                router,
                attn_gain[:, None],
                expert_gain[:, None],
                jnp.zeros((router.shape[0], pad), bf16),
            ],
            axis=1,
        ),
        send_cotangents,
    )
    query_weight = left[:, :width]
    proj_weight = left[:, width:]
    kv_weight = right[:, : 2 * width]
    router_all = right[:, 2 * width : 2 * width + experts]
    gains = right[:, 2 * width + experts : 2 * width + experts + 2].astype(f32)
    attn_scale = gains[:, 0]
    expert_scale = gains[:, 1]
    expert_weights = [pair_rows(w[0]) for w in (expert_up, expert_down)]

    distance = jnp.arange(2 * TILE, dtype=jnp.int32)
    hot_bucket = (
        bucket_of(distance)[None, :] == jnp.arange(buckets, dtype=jnp.int32)[:, None]
    ).astype(f32)
    by_distance = jnp.sum(
        position_bias.astype(f32)[:, :, None] * hot_bucket[None], axis=1
    ) - position_bias.astype(f32)[:, buckets - 1 :]
    close = jnp.where(distance < TILE, by_distance, MASKED)
    beside = jnp.roll(by_distance, -TILE, axis=1)
    bias_rows = jnp.stack([close, beside], axis=1).reshape(PAIRS, 4, 2 * TILE)

    def norm_stats(values):
        return lax.rsqrt(jnp.mean(values * values, axis=-1, keepdims=True) + epsilon)

    state = []
    for b in range(batches):
        rows = inputs[b, 0].astype(f32)
        inv_one = norm_stats(rows)
        normed = (rows * inv_one * attn_scale).astype(bf16)
        kv = mm(normed, kv_weight, ((1,), (0,))).astype(bf16)
        queries = mm(normed, query_weight, ((1,), (0,))).astype(bf16)
        docs = doc_ids[b, 0].astype(f32)
        padded = jnp.concatenate([jnp.full((BACK,), -1.0, f32), docs])
        key_docs = lax.dynamic_slice_in_dim(padded, me * length, BACK + length)
        query_docs = key_docs[BACK:]
        if ways == 2:
            kv_back = lax.ppermute(kv, "ctx", [(0, 1)])
        else:
            every = lax.all_gather(kv, "ctx", axis=0, tiled=True)
            every = jnp.concatenate([jnp.zeros((BACK, 2 * width), bf16), every], axis=0)
            kv_back = lax.dynamic_slice_in_dim(every, me * length, BACK, 0)
        firsts = query_docs[::TILE]
        start = jnp.sum((key_docs[None, :] < firsts[:, None]).astype(jnp.int32), axis=1)
        tiles = jnp.arange(length // TILE, dtype=jnp.int32) + SPAN - start // TILE
        tiles = jnp.clip(tiles, 1, SPAN)
        view = (tiles, queries, kv, kv_back, query_docs[None], key_docs[None], bias_rows)
        state.append(dict(rows=rows, inv_one=inv_one, normed=normed, view=view))

    cot_here = cross(after(cot_sent, *over_exp))
    sent = ()
    for b, s in enumerate(state):
        s["view"] = (after(s["view"][0], *sent),) + s["view"][1:]
        attended, lse = attend(*s["view"])
        hidden = s["rows"] + mm(attended, proj_weight, ((1,), (0,)))
        inv_two = norm_stats(hidden)
        shared = (hidden * inv_two * expert_scale).astype(bf16)
        logits = mm(shared, router_all, ((1,), (0,)))
        hot = hots[b]
        chosen = jnp.sum(jnp.where(hot, logits[:, None, :], 0.0), axis=2)
        gate_exp = jnp.exp(chosen - jnp.max(chosen, axis=1, keepdims=True))
        gates = gate_exp / jnp.sum(gate_exp, axis=1, keepdims=True)
        gate_slots = sum(
            jnp.sum(jnp.where(holds[b][k], gates[None, :, k], 0.0), axis=1) for k in range(top)
        ).reshape(experts, 1, room)
        gate_slots = jnp.pad(gate_slots, ((0, 0), (0, 0), (0, TILE - room)))
        gate_high = gate_slots.astype(bf16)
        gate_low = (gate_slots - gate_high.astype(f32)).astype(bf16)
        gate_row = jnp.concatenate(
            [gate_high, gate_low, jnp.zeros((experts, 1, width - 2 * TILE), bf16)], axis=2
        )
        at_gate = lax.broadcasted_iota(jnp.int32, (1, room, 1), 1) == capacity
        sent = (jnp.where(at_gate, gate_row, dispatch(b, shared)),)
        s.update(attended=attended, lse=lse, hidden=hidden, inv_two=inv_two, shared=shared,
                 gates=gates, sent=sent[0])

    made = ()
    last = (cot_here, *(s["sent"] for s in state))
    for s in state:
        s["here"] = cross(after(s["sent"], *last))
        last = (s["here"],)
    for b, s in enumerate(state):
        y, back, *sums = run_experts(
            me[None].astype(jnp.int32), s["here"], cot_here, b, *expert_weights, made, capacity,
            ways == 2, ways == 2 and b == batches - 1,
        )
        made = (y, *sums)
        s["back"] = cross(after(back, *last))
        last = (s["back"],)
    results = cross(after(y, *last))
    if ways == 2:
        up_share, down_share = (
            (mine + swap(theirs, "ctx", 1).astype(f32))[None]
            for mine, theirs in zip(sums[::2], sums[1::2])
        )
    else:
        up_share, down_share = (
            lax.psum_scatter(g.astype(bf16), "ctx", scatter_dimension=0, tiled=True).astype(f32)[None]
            for g in sums
        )

    input_grads = []
    parts = []
    picks = []
    before = ()
    for b, s in enumerate(state):
        upstream = cots[b].astype(f32)
        packet = after(s["back"], *before)
        dots = packet[:, capacity, : 2 * TILE].astype(f32)
        dots = (dots[:, :room] + dots[:, TILE : TILE + room]).reshape(1, slots)
        slot = slot_of[b]
        pick = [slot[:, k : k + 1] == slot_rows[None, :] for k in range(top)]
        picks.append(functools.reduce(jnp.logical_or, pick).astype(bf16))
        scaled = jnp.stack([jnp.sum(jnp.where(p, dots, 0.0), axis=1) for p in pick], axis=1)
        chosen_grad = scaled - s["gates"] * jnp.sum(scaled, axis=1, keepdims=True)
        logit_grad = jnp.sum(jnp.where(hots[b], chosen_grad[:, :, None], 0.0), axis=1).astype(bf16)
        shared_grad = mm(picks[b], packet.reshape(slots, width), ((1,), (0,)))
        shared_grad = shared_grad + mm(logit_grad, router_all, ((1,), (1,)))
        unit = s["hidden"] * s["inv_two"]
        grad_expert = jnp.sum(shared_grad * unit, axis=0)
        inner = shared_grad * expert_scale
        hidden_grad = upstream + s["inv_two"] * (
            inner - unit * jnp.mean(inner * unit, axis=1, keepdims=True)
        )
        branch_grad = hidden_grad.astype(bf16)
        attended_grad = mm(branch_grad, proj_weight, ((1,), (1,))).astype(bf16)
        dq, own, back, near = attend_back(*s["view"], s["attended"], attended_grad, s["lse"])
        before = (dq,)
        if ways == 2:
            got = lax.ppermute(back, "ctx", [(1, 0)])
        else:
            every = jnp.zeros((2, BACK + seq_len, width), bf16)
            every = lax.dynamic_update_slice_in_dim(every, back, me * length, 1)
            got = lax.psum_scatter(every[:, BACK:], "ctx", scatter_dimension=1, tiled=True)
        both = (own.astype(f32) + got.astype(f32)).astype(bf16)
        dkv = jnp.concatenate([both[0], both[1]], axis=1)
        normed = s["normed"]
        normed_grad = mm(dq, query_weight, ((1,), (1,))) + mm(dkv, kv_weight, ((1,), (1,)))
        unit = s["rows"] * s["inv_one"]
        grad_attn = jnp.sum(normed_grad * unit, axis=0)
        inner = normed_grad * attn_scale
        input_part = s["inv_one"] * (inner - unit * jnp.mean(inner * unit, axis=1, keepdims=True))
        input_grads.append((hidden_grad + input_part).astype(bf16))
        parts.append((near, grad_attn, grad_expert))
        s.update(dq=dq, dkv=dkv, branch_grad=branch_grad, logit_grad=logit_grad)

    outputs = []
    for b, s in enumerate(state):
        mine = results[:, b * room : (b + 1) * room].reshape(slots, width)
        outputs.append((s["hidden"] + mm(picks[b], mine, ((1,), (0,)))).astype(bf16))

    near, grad_attn, grad_expert = (functools.reduce(jnp.add, p) for p in zip(*parts))

    def weight_grads(rows):
        def total(left, right):
            return functools.reduce(
                jnp.add, [mm(rows(s[left], 1), s[right], ((0,), (0,))) for s in state]
            )

        small = total("shared", "logit_grad")
        return (
            jnp.concatenate([total("normed", "dq"), total("attended", "branch_grad")], axis=1),
            jnp.concatenate(
                [
                    total("normed", "dkv"),
                    small,
                    rows(grad_attn, 0)[:, None],
                    rows(grad_expert, 0)[:, None],
                    jnp.zeros((small.shape[0], pad), f32),
                ],
                axis=1,
            ),
        )

    hot_near = jnp.where(
        jnp.arange(buckets)[:, None] < buckets - 1, hot_bucket[:, :TILE], 0.0
    )
    grad_bias = jnp.sum(near.reshape(HEADS, 1, TILE) * hot_near[None], axis=2)
    far = jnp.where(jnp.arange(buckets) == buckets - 1, 1.0, 0.0)
    grad_bias = grad_bias - jnp.sum(grad_bias, axis=1, keepdims=True) * far
    left, right, bias_total = scatter_sum(weight_grads, width, results, grad_bias)
    return (
        jnp.stack(outputs)[:, None],
        jnp.stack(input_grads)[:, None],
        jnp.concatenate([left[:, :width], right[:, : 2 * width]], axis=1),
        left[:, width:],
        right[:, 2 * width : 2 * width + experts],
        right[:, 2 * width + experts],
        right[:, 2 * width + experts + 1],
        bias_total,
        up_share,
        down_share,
    )


def solution(mesh):
    placed = (
        P(None, "exp", "ctx", None),
        P(None, "exp", "ctx", None),
        P(None, "exp", None),
        P(None, "exp", "ctx", None),
        P(("ctx", "exp"), None),
        P(("ctx", "exp"), None),
        P(("ctx", "exp"), None),
        P(("ctx", "exp")),
        P(("ctx", "exp")),
        P(),
        P("exp", "ctx", None),
        P("exp", "ctx", None),
    )
    return jax.shard_map(
        shards,
        mesh=mesh,
        in_specs=placed,
        out_specs=(
            P(None, "exp", "ctx", None),
            P(None, "exp", "ctx", None),
            P(("ctx", "exp"), None),
            P(("ctx", "exp"), None),
            P(("ctx", "exp"), None),
            P(("ctx", "exp")),
            P(("ctx", "exp")),
            P(),
            P("exp", "ctx", None),
            P("exp", "ctx", None),
        ),
        check_vma=False,
    )
```
